32 devices in a mesh: dp: 8 (over z, x), tensor: 4 (over y, core).
Axes of the slice: x: 2, y: 2, z: 4, core: 2. Of those that a mesh axis runs over, the one named last changes fastest.
Arguments:
- tokens: bfloat16 [16384, 1024], P('dp', 'tensor'), may hold values from -6 to 6
- out_grad: bfloat16 [16384, 1024], P('dp', 'tensor'), may hold values from -6 to 6
- segments: int32 [8, 2048], P('dp'), may hold values from 0 to 3, never falling along the last dimension, each value on 1 to 1792 neighbouring positions
- padding: int32 [8, 2048], P('dp'), may hold values 0 or 1
- norm1_gain: bfloat16 [1024], P('tensor'), may hold values from 0.5 to 1.5
- norm1_bias: bfloat16 [1024], P('tensor'), may hold values from -3 to 3
- w_query: bfloat16 [1024, 1024], P(None, 'tensor'), may hold values from -1 to 1
- b_query: bfloat16 [1024], P('tensor'), may hold values from -4 to 4
- w_key: bfloat16 [1024, 1024], P(None, 'tensor'), may hold values from -0.1875 to 0.1875
- w_value: bfloat16 [1024, 1024], P(None, 'tensor'), may hold values from -0.1875 to 0.1875
- b_value: bfloat16 [1024], P('tensor'), may hold values from -4 to 4
- w_dense: bfloat16 [1024, 1024], P('tensor'), may hold values from -0.5 to 0.5
- dense_bias: bfloat16 [1024], P('tensor'), may hold values from -4 to 4
- norm2_gain: bfloat16 [1024], P('tensor'), may hold values from 0.5 to 1.5
- norm2_bias: bfloat16 [1024], P('tensor'), may hold values from -3 to 3
- w_up: bfloat16 [1024, 4096], P(None, 'tensor'), may hold values from -0.1875 to 0.1875
- b_up: bfloat16 [4096], P('tensor'), may hold values from -4 to 4
- w_down: bfloat16 [4096, 1024], P('tensor'), may hold values from -0.09375 to 0.09375
- down_bias: bfloat16 [1024], P('tensor'), may hold values from -4 to 4
Outputs:
- output: bfloat16 [16384, 1024], P('dp', 'tensor')
- tokens_grad: float32 [16384, 1024], P('dp', 'tensor')
- norm1_gain_grad: float32 [1024], P('tensor')
- norm1_bias_grad: float32 [1024], P('tensor')
- w_query_grad: float32 [1024, 1024], P('dp', 'tensor')
- b_query_grad: float32 [1024], P('tensor')
- w_key_grad: float32 [1024, 1024], P('dp', 'tensor')
- w_value_grad: float32 [1024, 1024], P('dp', 'tensor')
- b_value_grad: float32 [1024], P('tensor')
- w_dense_grad: float32 [1024, 1024], P('tensor', 'dp')
- dense_bias_grad: float32 [1024], P('tensor')
- norm2_gain_grad: float32 [1024], P('tensor')
- norm2_bias_grad: float32 [1024], P('tensor')
- w_up_grad: float32 [1024, 4096], P('dp', 'tensor')
- b_up_grad: float32 [4096], P('tensor')
- w_down_grad: float32 [4096, 1024], P('tensor', 'dp')
- down_bias_grad: float32 [1024], P('tensor')
- head_max: float32 [16], P('tensor')
- clipped_query: float32 [1024, 1024], P(None, 'tensor')
- clipped_query_bias: float32 [1024], P('tensor')
- clipped_key: float32 [1024, 1024], P(None, 'tensor')
The draws below stay inside these ranges and needn't reach their ends.
Inputs may be any that keep to these rules, and one draw needn't show every extreme that they name: `segments`: document numbers never fall along a sequence and each of the 4 numbers occurs; a document spans 1 to 1792 tokens, and one spans exactly that many.
All inputs are finite; a program needn't handle non-finite values. No bound on the sum of `padding` on one device may be relied on, other than what follows from the above.
Results may differ from the reference program's by a relative error of at most 0.018.
Values may be sent and summed in bfloat16 or wider, within the bound.
A program may use at most 192 MiB of HBM per device.

```python
import math
import jax
import jax.numpy as jnp
import numpy as np
from jax import lax

D = 1024
HEADS = 16
HD = 64
FF = 4096
SEQ_LEN = 2048
WIN = 1024
DOCS = 4
SEQS = 8
TOKENS = 16384
N_TENSOR = 4


def draw_w_query(key, part):
    key = jax.random.fold_in(key, 11)
    key_base, key_order, key_jitter = jax.random.split(key, 3)
    spread = math.sqrt(3.0 / D)
    base = jax.random.uniform(key_base, (D, D), jnp.float32, -spread, spread)
    order = jax.random.permutation(key_order, HEADS).astype(jnp.float32)
    jitter = jax.random.uniform(key_jitter, (HEADS,), jnp.float32)
    head_scale = jnp.exp(math.log(0.5) + (order + jitter) / HEADS * math.log(5.0))
    return (base * jnp.repeat(head_scale, HD)[None, :]).astype(jnp.bfloat16)


def plant(drawn, key, least, largest):
    longest = drawn.shape.index(max(drawn.shape))
    spots = []
    for shift in (0, 1):
        where = [jax.random.randint(jax.random.fold_in(key, axis), (), 0, length) for axis, length in enumerate(drawn.shape)]
        where[longest] = (where[longest] + shift) % drawn.shape[longest]
        spots.append(tuple(where))
    return drawn.at[spots[0]].set(least).at[spots[1]].set(largest)


def shard_levels(key, shape, cuts, low, high):
    level, own = 1.0, jax.random.fold_in(key, 6)
    for position, shards_of in cuts:
        steps = jnp.exp(jax.random.uniform(jax.random.fold_in(own, position), (shards_of,), jnp.float32, low / len(cuts), high / len(cuts)))
        level = level * jnp.repeat(steps, shape[position] // shards_of).reshape([-1 if axis == position else 1 for axis in range(len(shape))])
    return level


def length_profile(count, total, limit, slope):
    portions = [(1 << 20) // math.isqrt(grade ** slope) + 1 for grade in range(2, count + 1)]
    spare, given = total - limit - (count - 1), [1] * (count - 1)
    while spare > 0:
        free = [i for i in range(count - 1) if given[i] < limit]
        pool, budget = sum([portions[i] for i in free]), spare
        for i in free:
            addition = min(limit - given[i], max(1, budget * portions[i] // pool), spare)
            given[i] = given[i] + addition
            spare = spare - addition
    return np.array([limit] + given)


def uneven_parts(key, count, total, bound, lean):
    if count == 2:
        one = jax.random.randint(key, (), max(1, total - bound), min(bound, total - 1) + 1)
        return jnp.stack([one, total - one])
    sizes = jnp.asarray(length_profile(count, total, bound, lean), jnp.int32)
    couples = (count - 1) // 2
    source_of, sink = sizes[1:1 + 2 * couples:2], sizes[2:2 + 2 * couples:2]
    room = jnp.minimum(source_of - 1, bound - sink)
    passed = jax.random.randint(jax.random.fold_in(key, 1), (couples,), 0, 1 << 20) % (room + 1)
    sizes = sizes.at[1:1 + 2 * couples:2].set(source_of - passed).at[2:2 + 2 * couples:2].set(sink + passed)
    return sizes[jax.random.permutation(jax.random.fold_in(key, 2), count)]


def scatter_about(stream_key, dims, deviation, bound, cuts=(), held_as=jnp.bfloat16):
    values = deviation * jax.random.normal(stream_key, dims, jnp.float32)
    if cuts:
        values = values * shard_levels(stream_key, dims, cuts, -0.22, 0.18)
    return jnp.clip(values, -bound, bound).astype(held_as)


def setup_inputs(seed: int = 0) -> dict:
    streams_of = jax.random.split(jax.random.key(seed), 20)
    tokens = scatter_about(streams_of[0], (TOKENS, D), 1.0, 6.0, ((0, 8), (1, 4)))
    out_grad = scatter_about(streams_of[1], (TOKENS, D), 1.0, 6.0, ((0, 8), (1, 4)))
    segments = jax.vmap(lambda own: jnp.searchsorted(jnp.cumsum(uneven_parts(own, DOCS, SEQ_LEN, 7 * SEQ_LEN // 8, 1)), jnp.arange(SEQ_LEN), side="right"))(jax.random.split(streams_of[2], SEQS)).reshape((SEQS, SEQ_LEN)).astype(jnp.int32)
    padding = plant((jax.random.randint(streams_of[3], (SEQS, SEQ_LEN), 0, 8) < 7).astype(jnp.int32), jax.random.fold_in(streams_of[3], 1), 0, 1)
    norm1_gain = jnp.clip(1.0 + 0.1 * jax.random.normal(streams_of[4], (D,), jnp.float32), 0.5, 1.5).astype(jnp.bfloat16)
    norm1_bias = scatter_about(streams_of[5], (D,), 0.3, 3.0, ((0, 4),))
    w_query = draw_w_query(jax.random.fold_in(streams_of[19], 71), 0)
    b_query = scatter_about(streams_of[7], (D,), 0.5, 4.0, ((0, 4),))
    w_key = scatter_about(streams_of[8], (D, D), D ** -0.5, 0.1875, ((1, 4),))
    w_value = scatter_about(streams_of[9], (D, D), D ** -0.5, 0.1875, ((1, 4),))
    b_value = scatter_about(streams_of[10], (D,), 0.5, 4.0, ((0, 4),))
    w_dense = scatter_about(streams_of[11], (D, D), (D // 8) ** -0.5, 0.5, ((0, 4),))
    dense_bias = scatter_about(streams_of[12], (D,), 0.5, 4.0, ((0, 4),))
    norm2_gain = jnp.clip(1.0 + 0.1 * jax.random.normal(streams_of[13], (D,), jnp.float32), 0.5, 1.5).astype(jnp.bfloat16)
    norm2_bias = scatter_about(streams_of[14], (D,), 0.3, 3.0, ((0, 4),))
    w_up = scatter_about(streams_of[15], (D, FF), D ** -0.5, 0.1875, ((1, 4),))
    b_up = scatter_about(streams_of[16], (FF,), 0.5, 4.0, ((0, 4),))
    w_down = scatter_about(streams_of[17], (FF, D), FF ** -0.5, 0.09375, ((0, 4),))
    down_bias = scatter_about(streams_of[18], (D,), 0.5, 4.0, ((0, 4),))
    return dict(tokens=tokens, out_grad=out_grad, segments=segments, padding=padding, norm1_gain=norm1_gain, norm1_bias=norm1_bias, w_query=w_query, b_query=b_query, w_key=w_key, w_value=w_value, b_value=b_value, w_dense=w_dense, dense_bias=dense_bias, norm2_gain=norm2_gain, norm2_bias=norm2_bias, w_up=w_up, b_up=b_up, w_down=w_down, down_bias=down_bias)


EPS = 1e-05
TAU = 2.0
NEG = -1e+30

@jax.custom_vjp
def low(v):
    return lax.optimization_barrier(v.astype(jnp.bfloat16)).astype(jnp.float32)

@jax.custom_vjp
def low_back(v):
    return v

def low_keep(v):
    return (low(v), None)

def low_pass(kept, grad):
    return (grad,)

def back_keep(v):
    return (v, None)

def back_low(kept, grad):
    return (low(grad),)
low.defvjp(low_keep, low_pass)
low_back.defvjp(back_keep, back_low)

def product(left_side, right_side):
    return jnp.dot(left_side, right_side, precision=lax.Precision.HIGHEST, preferred_element_type=jnp.float32)

def layer_norm(values, gain_row, bias_row):
    mean_row = lax.optimization_barrier(jnp.mean(values, axis=-1, keepdims=True))
    square_row = lax.optimization_barrier(jnp.mean(values * values, axis=-1, keepdims=True))
    return (values - mean_row) * lax.rsqrt(square_row - mean_row * mean_row + EPS) * gain_row + bias_row

def attend_head(input_rows):
    head_query, head_key, head_value, seg_row, pad_row, head_slope = input_rows
    positions = jnp.arange(SEQ_LEN)
    offsets = positions[:, None] - positions[None, :]
    allowed = (seg_row[:, None] == seg_row[None, :]) & (offsets >= 0) & (offsets < WIN) & ((pad_row[None, :] == 1) | (offsets == 0))
    raw_scores = product(head_query, head_key.T) * (1.0 / math.sqrt(HD))
    scores = low_back(raw_scores - head_slope * offsets.astype(jnp.float32))
    masked = jnp.where(allowed, scores, NEG)
    top_score = lax.optimization_barrier(jnp.max(masked, axis=-1, keepdims=True))
    weights = jnp.where(allowed, jnp.exp(masked - top_score), 0.0)
    probabilities = weights / lax.optimization_barrier(jnp.sum(weights, axis=-1, keepdims=True))
    context = product(low(probabilities), head_value)
    return (context, jnp.max(jnp.where(allowed, raw_scores, NEG)))

def forward(tokens, norm1_gain, norm1_bias, w_query, b_query, w_key, w_value, b_value, w_dense, dense_bias, norm2_gain, norm2_bias, w_up, b_up, w_down, down_bias, segments, padding):
    group_width = D // N_TENSOR
    unit_width = FF // N_TENSOR
    seq_total = segments.shape[0]
    first_norm_output = low(layer_norm(tokens, norm1_gain, norm1_bias))
    query_parts, key_parts, value_parts = ([], [], [])
    for tensor_group in range(N_TENSOR):
        columns = slice(tensor_group * group_width, (tensor_group + 1) * group_width)
        shared = low_back(first_norm_output)
        query_parts.append(product(shared, w_query[:, columns]) + b_query[columns])
        key_parts.append(product(shared, w_key[:, columns]))
        value_parts.append(product(shared, w_value[:, columns]) + b_value[columns])
    queries = low(low_back(jnp.concatenate(query_parts, axis=1)))
    keys_all = low(low_back(jnp.concatenate(key_parts, axis=1)))
    values_all = low(low_back(jnp.concatenate(value_parts, axis=1)))

    def split_heads(matrix):
        return matrix.reshape(seq_total, SEQ_LEN, HEADS, HD).transpose(0, 2, 1, 3).reshape(seq_total * HEADS, SEQ_LEN, HD)
    slopes = jnp.exp2(-8.0 * (jnp.arange(HEADS).astype(jnp.float32) + 1.0) / HEADS)
    contexts, biggest = lax.map(jax.checkpoint(attend_head), (split_heads(queries), split_heads(keys_all), split_heads(values_all), jnp.repeat(segments, HEADS, axis=0), jnp.repeat(padding, HEADS, axis=0), jnp.tile(slopes, seq_total)))
    context = contexts.reshape(seq_total, HEADS, SEQ_LEN, HD).transpose(0, 2, 1, 3).reshape(seq_total * SEQ_LEN, D)
    context = low(low_back(context))
    head_max = lax.optimization_barrier(jnp.max(biggest.reshape(seq_total, HEADS), axis=0))
    attention = jnp.zeros_like(tokens)
    for tensor_group in range(N_TENSOR):
        columns = slice(tensor_group * group_width, (tensor_group + 1) * group_width)
        attention = attention + low(low_back(product(context[:, columns], w_dense[columns, :])))
    hidden_single = tokens + attention + dense_bias
    second_norm_output = low(layer_norm(hidden_single, norm2_gain, norm2_bias))
    feed_sum = jnp.zeros_like(tokens)
    for tensor_group in range(N_TENSOR):
        units = slice(tensor_group * unit_width, (tensor_group + 1) * unit_width)
        shared = low_back(second_norm_output)
        pre_act = low_back(product(shared, w_up[:, units]) + b_up[units])
        activation = low(jax.nn.gelu(pre_act, approximate=True))
        feed_sum = feed_sum + low(low_back(product(activation, w_down[units, :])))
    return (hidden_single + feed_sum + down_bias, head_max)

def reference(tokens, out_grad, segments, padding, norm1_gain, norm1_bias, w_query, b_query, w_key, w_value, b_value, w_dense, dense_bias, norm2_gain, norm2_bias, w_up, b_up, w_down, down_bias):
    params = [array.astype(jnp.float32) for array in (tokens, norm1_gain, norm1_bias, w_query, b_query, w_key, w_value, b_value, w_dense, dense_bias, norm2_gain, norm2_bias, w_up, b_up, w_down, down_bias)]

    def wrapped(*input_rows):
        return forward(*input_rows, segments, padding)
    output, pullback, head_max = jax.vjp(wrapped, *params, has_aux=True)
    grads = pullback(out_grad.astype(jnp.float32))
    clip_scale = jnp.repeat(jnp.sqrt(TAU / jnp.maximum(head_max, TAU)), HD)
    return (output.astype(jnp.bfloat16), grads[0], grads[1], grads[2], grads[3], grads[4], grads[5], grads[6], grads[7], grads[8], grads[9], grads[10], grads[11], grads[12], grads[13], grads[14], grads[15], head_max, params[3] * clip_scale, params[4] * clip_scale, params[5] * clip_scale)
```

```python
import functools
import math

import jax
import jax.numpy as jnp
from jax import lax
from jax.experimental import pallas as pl
from jax.experimental.pallas import tpu as pltpu
from jax.sharding import PartitionSpec as P

HEADS = 16
HD = 64
WIN = 1024
D = 1024
FF = 4096
SEQ = 2048
B = 256
NB = SEQ // B
SLOTS = WIN // B + 1
STRIP = SLOTS * B
LH = 4
SHARE = LH * HD
UNITS = FF // 4
TILE = 512
OWN = SEQ // 2

EPS = 1e-05
TAU = 2.0
NEG = -1e30
F32 = jnp.float32
BF = jnp.bfloat16
VMEM_LIMIT = 56 * 2**20


def dot(a, b):
    return jnp.dot(a, b, preferred_element_type=F32)


def dot_nt(a, b):
    return lax.dot_general(a, b, (((1,), (1,)), ((), ())), preferred_element_type=F32)


def params():
    return pltpu.CompilerParams(
        dimension_semantics=("arbitrary",), vmem_limit_bytes=VMEM_LIMIT
    )


def feature_block(rank):
    return pl.ds(pl.multiple_of(rank * SHARE, SHARE), SHARE)


def head_of_lane(shape):
    return lax.broadcasted_iota(jnp.int32, shape, 1) // HD


def row_stats(rows):
    mean = jnp.sum(rows, axis=1, keepdims=True) / D
    square = jnp.sum(rows * rows, axis=1, keepdims=True) / D
    return mean, lax.rsqrt(square - mean * mean + EPS)


def split_store(keep_ref, send_ref, value_ref, core):
    for half in range(2):
        cols = slice(half * SHARE, (half + 1) * SHARE)
        keep_ref[:, cols] = value_ref[:, feature_block(2 * half + core)].astype(keep_ref.dtype)
        send_ref[:, cols] = value_ref[:, feature_block(2 * half + 1 - core)].astype(
            send_ref.dtype
        )


def fwd_kernel(
    ids, x0, x1, x2, x3, vec, wq, wk, wv, bqv, wd, lo, pad, alibi,
    p_ref, q_ref, k_ref, v_ref, linv_ref, ctx_ref, keep_ref, send_ref, hm_ref,
    xs, qm_s, k_s, va_s, u_s, res_s, lo_s,
):
    b = pl.program_id(0)
    t = ids[0]
    core = lax.rem(t, 2)
    for r, x in enumerate((x0, x1, x2, x3)):
        xs[:, feature_block(t ^ r)] = x[...].astype(F32)
    rows = xs[...]
    mean, rstd = row_stats(rows)
    n1 = ((rows - mean) * rstd * vec[0:1, :] + vec[1:2, :]).astype(BF)
    q = (dot(n1, wq[...]) + bqv[0:1, :]).astype(BF)
    k = dot(n1, wk[...]).astype(BF)
    v = (dot(n1, wv[...]) + bqv[1:2, :]).astype(BF)
    qs = q * jnp.asarray(1.0 / math.sqrt(HD), BF)
    q_ref[...] = qs
    k_ref[...] = k
    v_ref[...] = v
    here = pl.ds(pl.multiple_of(b * B, B), B)
    k_s[here, :] = k
    lanes = head_of_lane((B, SHARE))
    for h in range(LH):
        qm_s[h] = jnp.where(lanes == h, qs, jnp.zeros_like(qs))
        va_s[h, here, :] = jnp.where(lanes == h, v, jnp.ones_like(v))
    lo_s[...] = jnp.broadcast_to(lo[...], (B, B))

    @pl.when(b == 0)
    def _():
        hm_ref[...] = jnp.full(hm_ref.shape, NEG, F32)

    row_i = lax.broadcasted_iota(jnp.int32, (B, B), 0)
    col_i = lax.broadcasted_iota(jnp.int32, (B, B), 1)

    def attend(nb):
        start = pl.multiple_of((b + 1 - nb) * B, B)

        def head(h, carry):
            qm = qm_s[h]
            top = jnp.full((B, 128), NEG, F32)
            biggest = hm_ref[h]
            for r in range(nb):
                slot = SLOTS - nb + r
                base = pl.multiple_of(start + r * B, B)
                s = dot_nt(qm, k_s[pl.ds(base, B), :])
                inside = col_i + base >= lo_s[...]
                shut = pad[0:1, pl.ds(base, B)]
                if r == nb - 1:
                    s = jnp.where(row_i == col_i, s, s + shut)
                    s = jnp.where(inside & (col_i <= row_i), s, NEG)
                else:
                    s = jnp.where(inside, s + shut, NEG)
                biggest = jnp.maximum(biggest, jnp.max(s.reshape(B // 8, 8, B), axis=0))
                s = s + alibi[pl.ds(h, 1), slot * B : (slot + 1) * B]
                u_s[:, slot * B : (slot + 1) * B] = s
                top = jnp.maximum(top, jnp.maximum(s[:, :128], s[:, 128:]))
            hm_ref[h] = biggest
            top = jnp.max(top, axis=1, keepdims=True)
            for r in range(nb):
                slot = SLOTS - nb + r
                cols = slice(slot * B, (slot + 1) * B)
                p_ref[h, :, cols] = jnp.exp(u_s[:, cols] - top).astype(BF)
            res_s[h] = dot(p_ref[h, :, (SLOTS - nb) * B :], va_s[h, pl.ds(start, nb * B), :])
            return carry

        lax.fori_loop(0, LH, head, 0)

    count = b - ids[1 + b] + 1
    for nb in range(1, SLOTS + 1):
        pl.when(count == nb)(functools.partial(attend, nb))

    ctx = res_s[0]
    total = res_s[LH - 1]
    for h in range(1, LH):
        ctx = jnp.where(lanes == h, res_s[h], ctx)
        total = jnp.where(lanes == h, res_s[h - 1], total)
    inv = 1.0 / pltpu.roll(total, SHARE - HD, 1)
    linv_ref[...] = inv
    ctx = (ctx * inv).astype(BF)
    ctx_ref[...] = ctx
    xs[...] = dot(ctx, wd[...])
    split_store(keep_ref, send_ref, xs, core)


def attention_forward(ids, xs, vec, wq, wk, wv, bqv, wd, lo, pad, alibi):
    row = lambda width: pl.BlockSpec((B, width), lambda b, ids: (b, 0))
    whole = lambda shape: pl.BlockSpec(shape, lambda b, ids: (0,) * len(shape))
    return pl.pallas_call(
        fwd_kernel,
        grid_spec=pltpu.PrefetchScalarGridSpec(
            num_scalar_prefetch=1,
            grid=(NB,),
            in_specs=[row(SHARE)] * 4
            + [whole((8, D))]
            + [whole((D, SHARE))] * 3
            + [whole((8, SHARE)), whole((SHARE, D)), row(1), whole((8, SEQ)), whole((8, STRIP))],
            out_specs=[
                pl.BlockSpec((LH, B, STRIP), lambda b, ids: (0, b, 0)),
                row(SHARE), row(SHARE), row(SHARE), row(SHARE), row(SHARE), row(D // 2), row(D // 2),
                whole((LH, 8, B)),
            ],
            scratch_shapes=[
                pltpu.VMEM((B, D), F32),
                pltpu.VMEM((LH, B, SHARE), BF),
                pltpu.VMEM((SEQ, SHARE), BF),
                pltpu.VMEM((LH, SEQ, SHARE), BF),
                pltpu.VMEM((B, STRIP), F32),
                pltpu.VMEM((LH, B, SHARE), F32),
                pltpu.VMEM((B, B), jnp.int32),
            ],
        ),
        out_shape=[
            jax.ShapeDtypeStruct((LH, SEQ, STRIP), BF),
            jax.ShapeDtypeStruct((SEQ, SHARE), BF),
            jax.ShapeDtypeStruct((SEQ, SHARE), BF),
            jax.ShapeDtypeStruct((SEQ, SHARE), BF),
            jax.ShapeDtypeStruct((SEQ, SHARE), F32),
            jax.ShapeDtypeStruct((SEQ, SHARE), BF),
            jax.ShapeDtypeStruct((SEQ, D // 2), BF),
            jax.ShapeDtypeStruct((SEQ, D // 2), BF),
            jax.ShapeDtypeStruct((LH, 8, B), F32),
        ],
        compiler_params=params(),
        cost_estimate=pl.CostEstimate(
            flops=16 * 10**9, bytes_accessed=40 * 2**20, transcendentals=8 * 10**6
        ),
        name="attention_forward",
    )(ids, *xs, vec, wq, wk, wv, bqv, wd, lo, pad, alibi)


def mlp_kernel(
    ids, a_own, a_par, x0, x1, x2, x3, d0, d1, d2, d3, vec, bup, wu0, wu1, wd0, wd1,
    mk_ref, ms_ref, gn_ref, h1_ref, gu_ref, gd_ref, bs_ref,
    n2_s, n2t_s, dy_s, dyt_s, am_s, ag_s, act_s, gp_s,
):
    i = pl.program_id(0)
    t = ids[0]
    core = lax.rem(t, 2)

    @pl.when(i == 0)
    def _():
        def assemble(rb, carry):
            rows = pl.ds(pl.multiple_of(rb * B, B), B)
            for r, (x, d) in enumerate(((x0, d0), (x1, d1), (x2, d2), (x3, d3))):
                h1_ref[rows, feature_block(t ^ r)] = x[rb, 0].astype(F32)
                dy_s[rows, feature_block(t ^ r)] = d[rows, :]
            for part, a in ((core, a_own), (1 - core, a_par)):
                for half in range(2):
                    cols = feature_block(2 * half + part)
                    h1_ref[rows, cols] += a[rows, half * SHARE : (half + 1) * SHARE].astype(F32)
            value = h1_ref[rows, :] + vec[2:3, :]
            h1_ref[rows, :] = value
            mean, rstd = row_stats(value)
            n2 = ((value - mean) * rstd * vec[3:4, :] + vec[4:5, :]).astype(BF)
            n2_s[rows, :] = n2
            n2t_s[:, rows] = n2.T
            dyt_s[:, rows] = dy_s[rows, :].T
            am_s[rows, :] = jnp.zeros((B, D), F32)
            ag_s[rows, :] = jnp.zeros((B, D), F32)
            return carry

        lax.fori_loop(0, OWN // B, assemble, 0)

    def tile(wu, wd, which):
        bias = bup[which : which + 1, pl.ds(pl.multiple_of(lax.rem(i, 2) * TILE, TILE), TILE)]
        scale = math.sqrt(2.0 / math.pi)

        def rows_of(rb, sums):
            rows = pl.ds(pl.multiple_of(rb * B, B), B)
            pre = dot(n2_s[rows, :], wu[...]) + bias
            back = dot_nt(dy_s[rows, :], wd[...])
            square = pre * pre
            th = jnp.tanh(scale * pre * (1.0 + 0.044715 * square))
            half = 0.5 * (1.0 + th)
            act = (pre * half).astype(BF)
            slope = half + 0.5 * pre * (1.0 - th * th) * (scale + (3 * 0.044715 * scale) * square)
            gp = (slope * back).astype(BF)
            act_s[rows, :] = act
            gp_s[rows, :] = gp
            am_s[rows, :] += dot(act, wd[...])
            ag_s[rows, :] += dot_nt(gp, wu[...])
            return sums + jnp.sum(gp.astype(F32), axis=0, keepdims=True)

        sums = lax.fori_loop(0, OWN // B, rows_of, jnp.zeros((1, TILE), F32))
        bs_ref[...] = jnp.broadcast_to(sums, bs_ref.shape)

        def grads(fb, carry):
            rows = pl.ds(pl.multiple_of(fb * B, B), B)
            gu_ref[rows, :] = dot(n2t_s[rows, :], gp_s[...]).astype(gu_ref.dtype)
            gd_ref[rows, :] = dot(dyt_s[rows, :], act_s[...]).astype(gd_ref.dtype)
            return carry

        lax.fori_loop(0, D // B, grads, 0)

    pl.when(i < 2)(lambda: tile(wu0, wd0, 0))
    pl.when(i >= 2)(lambda: tile(wu1, wd1, 1))

    @pl.when(i == 3)
    def _():
        split_store(mk_ref, ms_ref, am_s, core)
        gn_ref[...] = ag_s[...].astype(BF)


def feed_forward(ids, a_own, a_par, xs, ds, vec, bup, wu0, wu1, wd0, wd1):
    whole = lambda shape: pl.BlockSpec(shape, lambda i, ids: (0,) * len(shape))
    low = lambda i: jnp.minimum(i, 1)
    high = lambda i: jnp.maximum(i - 2, 0)
    xs = [x.reshape(NB // 2, 2, B, SHARE) for x in xs]
    return pl.pallas_call(
        mlp_kernel,
        grid_spec=pltpu.PrefetchScalarGridSpec(
            num_scalar_prefetch=1,
            grid=(4,),
            in_specs=[whole((OWN, D // 2))] * 2
            + [pl.BlockSpec((NB // 2, 1, B, SHARE), lambda i, ids: (0, ids[0] // 2, 0, 0))] * 4
            + [whole((OWN, SHARE))] * 4
            + [
                whole((8, D)),
                whole((8, UNITS)),
                pl.BlockSpec((D, TILE), lambda i, ids: (0, low(i))),
                pl.BlockSpec((D, TILE), lambda i, ids: (0, high(i))),
                pl.BlockSpec((TILE, D), lambda i, ids: (low(i), 0)),
                pl.BlockSpec((TILE, D), lambda i, ids: (high(i), 0)),
            ],
            out_specs=[
                whole((OWN, D // 2)),
                whole((OWN, D // 2)),
                whole((OWN, D)),
                whole((OWN, D)),
                pl.BlockSpec((D, TILE), lambda i, ids: (0, i)),
                pl.BlockSpec((D, TILE), lambda i, ids: (0, i)),
                pl.BlockSpec((8, TILE), lambda i, ids: (0, i)),
            ],
            scratch_shapes=[
                pltpu.VMEM((OWN, D), BF),
                pltpu.VMEM((D, OWN), BF),
                pltpu.VMEM((OWN, D), BF),
                pltpu.VMEM((D, OWN), BF),
                pltpu.VMEM((OWN, D), F32),
                pltpu.VMEM((OWN, D), F32),
                pltpu.VMEM((OWN, TILE), BF),
                pltpu.VMEM((OWN, TILE), BF),
            ],
        ),
        out_shape=[
            jax.ShapeDtypeStruct((OWN, D // 2), BF),
            jax.ShapeDtypeStruct((OWN, D // 2), BF),
            jax.ShapeDtypeStruct((OWN, D), BF),
            jax.ShapeDtypeStruct((OWN, D), F32),
            jax.ShapeDtypeStruct((D, 2 * UNITS), BF),
            jax.ShapeDtypeStruct((D, 2 * UNITS), BF),
            jax.ShapeDtypeStruct((8, 2 * UNITS), F32),
        ],
        compiler_params=params(),
        cost_estimate=pl.CostEstimate(
            flops=26 * 10**9, bytes_accessed=40 * 2**20, transcendentals=2 * 10**6
        ),
        name="feed_forward",
    )(ids, a_own, a_par, *xs, *ds, vec, bup, wu0, wu1, wd0, wd1)


def mid_kernel(
    ids, h1, gn, gr, d0, d1, d2, d3, mk, mr, vec,
    gh_ref, gs_ref, oo_ref, os_ref, cs_ref,
    w_s,
):
    i = pl.program_id(0)
    t = ids[0]
    core = lax.rem(t, 2)
    y = t // 2
    for r, d in enumerate((d0, d1, d2, d3)):
        w_s[:, feature_block(t ^ r)] = d[...].astype(F32)
    dy = w_s[...]
    rows = h1[...]
    for half, ref in ((y, oo_ref), (1 - y, os_ref)):
        cols = feature_block(2 * half + core)
        part = pl.ds(pl.multiple_of(half * SHARE, SHARE), SHARE)
        total = mk[:, part].astype(F32) + mr[:, part].astype(F32)
        ref[...] = (h1[:, cols] + total + vec[5:6, cols]).astype(BF)
    mean, rstd = row_stats(rows)
    xhat = (rows - mean) * rstd
    grad = gn[...].astype(F32) + gr[...].astype(F32)
    scaled = grad * vec[3:4, :]
    first = jnp.sum(scaled, axis=1, keepdims=True) / D
    second = jnp.sum(scaled * xhat, axis=1, keepdims=True) / D
    gh = dy + rstd * (scaled - first - xhat * second)
    low = gh.astype(BF)
    gh_ref[...] = low
    w_s[...] = gh
    for half in range(2):
        gs_ref[:, half * SHARE : (half + 1) * SHARE] = w_s[:, feature_block(2 * half + core)].astype(BF)

    @pl.when(i == 0)
    def _():
        cs_ref[...] = jnp.zeros(cs_ref.shape, F32)

    for n, value in enumerate((grad * xhat, grad, gh, dy)):
        cs_ref[n : n + 1, :] += jnp.sum(value, axis=0, keepdims=True)


def middle(ids, h1, gn, gr, ds, mk, mr, vec):
    row = lambda width: pl.BlockSpec((B, width), lambda i, ids: (i, 0))
    whole = lambda shape: pl.BlockSpec(shape, lambda i, ids: (0,) * len(shape))
    return pl.pallas_call(
        mid_kernel,
        grid_spec=pltpu.PrefetchScalarGridSpec(
            num_scalar_prefetch=1,
            grid=(OWN // B,),
            in_specs=[row(D)] * 3 + [row(SHARE)] * 4 + [row(D // 2)] * 2 + [whole((8, D))],
            out_specs=[row(D), row(D // 2), row(SHARE), row(SHARE), whole((8, D))],
            scratch_shapes=[pltpu.VMEM((B, D), F32)],
        ),
        out_shape=[
            jax.ShapeDtypeStruct((OWN, D), BF),
            jax.ShapeDtypeStruct((OWN, D // 2), BF),
            jax.ShapeDtypeStruct((OWN, SHARE), BF),
            jax.ShapeDtypeStruct((OWN, SHARE), BF),
            jax.ShapeDtypeStruct((8, D), F32),
        ],
        compiler_params=params(),
        cost_estimate=pl.CostEstimate(flops=20 * 2**20, bytes_accessed=16 * 2**20, transcendentals=0),
        name="second_norm_backward",
    )(ids, h1, gn, gr, *ds, mk, mr, vec)


def bwd_kernel(
    ids, x0, x1, x2, x3, gh, ga, gb, p_ref, q_ref, linv_ref, ctx_ref, k_ref, v_ref, vec, wq, wk, wv, wd,
    keep_ref, send_ref, st_ref, ghx_ref, gw_ref, bs_ref,
    xs, gh_s, gm_s, gt_s, qt_s, dl_s, ds_s, res_s, dkt_s, dvt_s, acc_s,
):
    i = pl.program_id(0)
    b = NB - 1 - i
    t = ids[0]
    core = lax.rem(t, 2)
    y = t // 2

    @pl.when(i == 0)
    def _():
        dkt_s[...] = jnp.zeros(dkt_s.shape, F32)
        dvt_s[...] = jnp.zeros(dvt_s.shape, F32)
        acc_s[...] = jnp.zeros(acc_s.shape, F32)
        bs_ref[...] = jnp.zeros(bs_ref.shape, F32)

    @pl.when(lax.rem(b, 2) == y)
    def _():
        gh_s[...] = gh[...]

    @pl.when(lax.rem(b, 2) != y)
    def _():
        for part, ref in ((core, ga), (1 - core, gb)):
            for half in range(2):
                gh_s[:, feature_block(2 * half + part)] = ref[:, half * SHARE : (half + 1) * SHARE]

    ghl = gh_s[...]
    ghx_ref[...] = gh_s[:, feature_block(t)]
    gc = dot_nt(ghl, wd[...]).astype(BF).astype(F32)
    ctx = ctx_ref[...]
    scaled = gc * linv_ref[...]
    gcs = scaled.astype(BF)
    product = scaled * ctx.astype(F32)
    lanes = head_of_lane((B, SHARE))
    q = q_ref[...]
    qt_s[...] = q.T.reshape(LH, HD, B)
    gt_s[...] = gcs.T.reshape(LH, HD, B)
    for h in range(LH):
        gm_s[h] = jnp.where(lanes == h, gcs, jnp.zeros_like(gcs))
        delta = jnp.sum(jnp.where(lanes == h, product, 0.0), axis=1, keepdims=True)
        dl_s[h] = jnp.broadcast_to(delta, (B, B))

    def attend(nb):
        start = pl.multiple_of((b + 1 - nb) * B, B)

        def head(h, carry):
            gm = gm_s[h]
            for r in range(nb):
                slot = SLOTS - nb + r
                cols = slice(slot * B, (slot + 1) * B)
                dp = dot_nt(gm, v_ref[pl.ds(pl.multiple_of(start + r * B, B), B), :])
                ds_s[:, cols] = (p_ref[h, :, cols].astype(F32) * (dp - dl_s[h])).astype(BF)
            live = slice((SLOTS - nb) * B, STRIP)
            keys = pl.ds(start, nb * B)
            res_s[h] = dot(ds_s[:, live], k_ref[keys, :])
            dkt_s[h, :, keys] += dot(qt_s[h], ds_s[:, live])
            dvt_s[h, :, keys] += dot(gt_s[h], p_ref[h, :, live])
            return carry

        lax.fori_loop(0, LH, head, 0)

    count = b - ids[1 + b] + 1
    for nb in range(1, SLOTS + 1):
        pl.when(count == nb)(functools.partial(attend, nb))

    dq = res_s[0]
    for h in range(1, LH):
        dq = jnp.where(lanes == h, res_s[h], dq)
    dq = (dq * (1.0 / math.sqrt(HD))).astype(BF)
    here = pl.ds(pl.multiple_of(b * B, B), B)
    dkt = dkt_s[:, :, here].reshape(SHARE, B).astype(BF)
    dvt = dvt_s[:, :, here].reshape(SHARE, B).astype(BF)
    dk = dkt.T
    dv = dvt.T
    bs_ref[0:1, :] += jnp.sum(dq.astype(F32), axis=0, keepdims=True)
    bs_ref[1:2, :] += jnp.sum(dv.astype(F32), axis=0, keepdims=True)

    for r, x in enumerate((x0, x1, x2, x3)):
        xs[:, feature_block(t ^ r)] = x[...].astype(F32)
    rows = xs[...]
    mean, rstd = row_stats(rows)
    xhat = (rows - mean) * rstd
    n1 = (xhat * vec[0:1, :] + vec[1:2, :]).astype(BF)
    acc_s[0:SHARE, :] += dot(dq.T, n1)
    acc_s[SHARE : 2 * SHARE, :] += dot(dkt, n1)
    acc_s[2 * SHARE : 3 * SHARE, :] += dot(dvt, n1)
    acc_s[3 * SHARE :, :] += dot(ctx.T, ghl)

    grad = dot_nt(dq, wq[...]) + dot_nt(dk, wk[...]) + dot_nt(dv, wv[...])
    xs[...] = grad
    split_store(keep_ref, send_ref, xs, core)
    scaled = grad * vec[0:1, :]
    first = jnp.sum(scaled, axis=1, keepdims=True)
    second = jnp.sum(scaled * xhat, axis=1, keepdims=True)
    column = lax.broadcasted_iota(jnp.int32, (B, 128), 1)
    packed = jnp.where(
        column == 0, first, jnp.where(column == 1, second, jnp.where(column == 2, mean, rstd))
    )
    st_ref[...] = packed.T[0:8, :]

    @pl.when(i == NB - 1)
    def _():
        gw_ref[...] = acc_s[...].astype(BF)


def attention_backward(ids, xs, gh, ga, gb, p, q, linv, ctx, k, v, vec, wq, wk, wv, wd):
    row = lambda width: pl.BlockSpec((B, width), lambda i, ids: (NB - 1 - i, 0))
    own = lambda width: pl.BlockSpec((B, width), lambda i, ids: ((NB - 1 - i) // 2, 0))
    whole = lambda shape: pl.BlockSpec(shape, lambda i, ids: (0,) * len(shape))
    return pl.pallas_call(
        bwd_kernel,
        grid_spec=pltpu.PrefetchScalarGridSpec(
            num_scalar_prefetch=1,
            grid=(NB,),
            in_specs=[row(SHARE)] * 4
            + [own(D), own(D // 2), own(D // 2)]
            + [pl.BlockSpec((LH, B, STRIP), lambda i, ids: (0, NB - 1 - i, 0))]
            + [row(SHARE)] * 3
            + [whole((SEQ, SHARE))] * 2
            + [whole((8, D))]
            + [whole((D, SHARE))] * 3
            + [whole((SHARE, D))],
            out_specs=[
                row(D // 2),
                row(D // 2),
                pl.BlockSpec((8, B), lambda i, ids: (0, NB - 1 - i)),
                row(SHARE),
                whole((D, D)),
                whole((8, SHARE)),
            ],
            scratch_shapes=[
                pltpu.VMEM((B, D), F32),
                pltpu.VMEM((B, D), BF),
                pltpu.VMEM((LH, B, SHARE), BF),
                pltpu.VMEM((LH, HD, B), BF),
                pltpu.VMEM((LH, HD, B), BF),
                pltpu.VMEM((LH, B, B), F32),
                pltpu.VMEM((B, STRIP), BF),
                pltpu.VMEM((LH, B, SHARE), F32),
                pltpu.VMEM((LH, HD, SEQ), F32),
                pltpu.VMEM((LH, HD, SEQ), F32),
                pltpu.VMEM((4 * SHARE, D), F32),
            ],
        ),
        out_shape=[
            jax.ShapeDtypeStruct((SEQ, D // 2), BF),
            jax.ShapeDtypeStruct((SEQ, D // 2), BF),
            jax.ShapeDtypeStruct((8, SEQ), F32),
            jax.ShapeDtypeStruct((SEQ, SHARE), BF),
            jax.ShapeDtypeStruct((4 * SHARE, D), BF),
            jax.ShapeDtypeStruct((8, SHARE), F32),
        ],
        compiler_params=params(),
        cost_estimate=pl.CostEstimate(
            flops=30 * 10**9, bytes_accessed=50 * 2**20, transcendentals=0
        ),
        name="attention_backward",
    )(ids, *xs, gh, ga, gb, p, q, linv, ctx, k, v, vec, wq, wk, wv, wd)


def swap(value, axis, bit):
    size = lax.axis_size(axis)
    return lax.ppermute(value, axis, [(i, i ^ bit) for i in range(size)])


def dp_bits():
    bits, bit = [], 1
    while bit < lax.axis_size("dp"):
        bits.append(bit)
        bit *= 2
    return bits


def dp_total(value):
    for bit in dp_bits():
        value = value + swap(value, "dp", bit)
    return value


def pick(value, axis, index):
    return lax.dynamic_index_in_dim(value, index, axis, keepdims=False)


def dp_scatter(value, order):
    rank = lax.axis_index("dp")
    size = lax.axis_size("dp")
    levels = len(dp_bits())
    rest = value.shape[1:]
    value = value.reshape((2,) * levels + rest)
    left = list(reversed(dp_bits()))
    for bit in order:
        axis = left.index(bit)
        left.pop(axis)
        mine = (rank // bit) % 2
        other = swap(pick(value, axis, 1 - mine), "dp", bit)
        value = (pick(value, axis, mine).astype(F32) + other.astype(F32)).astype(BF)
    return value.reshape(rest)


def shards(
    tokens,
    out_grad,
    segments,
    padding,
    norm1_gain,
    norm1_bias,
    w_query,
    b_query,
    w_key,
    w_value,
    b_value,
    w_dense,
    dense_bias,
    norm2_gain,
    norm2_bias,
    w_up,
    b_up,
    w_down,
    down_bias,
):
    t = lax.axis_index("tensor")
    rank = lax.axis_index("dp")
    size = lax.axis_size("dp")
    core, y = t % 2, t // 2
    core_swap = lambda value: swap(value, "tensor", 1)
    y_swap = lambda value: swap(value, "tensor", 2)
    rows8 = lambda value: jnp.pad(value, ((0, 8 - value.shape[0]), (0, 0)))

    x_own = tokens
    x_y = y_swap(x_own)
    x_core = core_swap(x_own)
    x_far = core_swap(x_y)
    xs = [x_own, x_core, x_y, x_far]
    vectors = jnp.stack([norm1_gain, norm1_bias, dense_bias, norm2_gain, norm2_bias, down_bias])
    vec = lax.dynamic_update_slice(jnp.zeros((6, D), BF), vectors, (0, t * SHARE))
    vec = vec + core_swap(vec)
    vec = rows8((vec + y_swap(vec)).astype(F32))

    part = D // size
    cut = lambda w: lax.dynamic_slice_in_dim(w, rank * part, part, 0)
    w_part = y_swap(jnp.concatenate([cut(w_up), cut(w_down)], axis=1))
    w_other = lax.all_gather(w_part, "dp", axis=0, tiled=True)
    up_other, down_other = w_other[:, :UNITS], w_other[:, UNITS:]
    b_up_pair = jnp.stack([b_up, y_swap(b_up)]).astype(F32)

    seg = segments.reshape(SEQ)
    index = jnp.arange(SEQ, dtype=jnp.int32)
    first = jnp.zeros((SEQ,), jnp.int32)
    for value in range(1, 4):
        first = jnp.where(seg == value, jnp.sum((seg < value).astype(jnp.int32)), first)
    lowest = jnp.maximum(first, index - (WIN - 1))
    ids = jnp.concatenate([t[None].astype(jnp.int32), lowest[::B] // B])
    pad_row = rows8(jnp.where(padding.reshape(1, SEQ) == 1, 0.0, NEG).astype(F32))
    heads = t * LH + jnp.arange(LH)
    slopes = jnp.exp2(-8.0 * (heads.astype(F32) + 1.0) / HEADS)
    alibi = rows8(slopes[:, None] * (jnp.arange(STRIP) - (STRIP - 1)).astype(F32)[None, :])

    p, q, k, v, linv, ctx, keep, send, hm = attention_forward(
        ids, xs, vec, w_query, w_key, w_value,
        rows8(jnp.stack([b_query, b_value]).astype(F32)), w_dense,
        lowest.reshape(SEQ, 1), pad_row, alibi,
    )

    by_y = lambda value, which: pick(value.reshape(NB // 2, 2, B, value.shape[-1]), 1, which).reshape(
        OWN, value.shape[-1]
    )
    d_own = by_y(out_grad, y)
    d_y = y_swap(by_y(out_grad, 1 - y))
    ds = [d_own, core_swap(d_own), d_y, core_swap(d_y)]

    both = (keep.astype(F32) + core_swap(send).astype(F32)).astype(BF)
    mine = by_y(both, y).astype(F32) + y_swap(by_y(both, 1 - y)).astype(F32)
    a_own = mine.astype(BF)
    a_par = core_swap(a_own)

    mk, ms, gn, h1, gu, gd, bs = feed_forward(
        ids, a_own, a_par, xs, ds, vec, rows8(b_up_pair), w_up, up_other, w_down, down_other
    )
    gr = core_swap(gn)
    mr = core_swap(ms)
    gh, gs, out_own, out_send, cs = middle(ids, h1, gn, gr, ds, mk, mr, vec)
    ga = y_swap(gs)
    gb = core_swap(ga)

    out_y = y_swap(out_send)
    pair = jnp.stack([out_own, out_y]).reshape(2, NB // 2, B, SHARE)
    output = jnp.where(y == 0, pair, pair[::-1]).transpose(1, 0, 2, 3).reshape(SEQ, SHARE)

    grads = jnp.concatenate([gu, gd], axis=1).reshape(size, D // size, 4 * UNITS)
    bits = dp_bits()
    grads = dp_scatter(grads, bits).reshape(D // size, 2, 2, UNITS)
    grads = grads[:, :, 0].astype(F32) + y_swap(grads[:, :, 1]).astype(F32)
    w_up_grad = grads[:, 0]
    w_down_grad = grads[:, 1].T

    keep, send, stats, ghx, gw, qv = attention_backward(
        ids, xs, gh, ga, gb, p, q, linv, ctx, k, v, vec, w_query, w_key, w_value, w_dense
    )
    both = (keep.astype(F32) + core_swap(send).astype(F32)).astype(BF).reshape(SEQ, 2, SHARE)
    g_first = pick(both, 1, y).astype(F32) + y_swap(pick(both, 1, 1 - y)).astype(F32)
    sums = stats[0:2]
    sums = sums + core_swap(sums)
    sums = sums + y_swap(sums)
    first, second = sums[0][:, None] / D, sums[1][:, None] / D
    mean, rstd = stats[2][:, None], stats[3][:, None]
    xhat = (tokens.astype(F32) - mean) * rstd
    scaled = g_first * norm1_gain.astype(F32)[None, :]
    tokens_grad = ghx.astype(F32) + rstd * (scaled - first - xhat * second)

    gw = gw.reshape(4 * SHARE, size, D // size).transpose(1, 0, 2)
    gw = dp_scatter(gw, bits).astype(F32).reshape(4, SHARE, D // size)

    local = jnp.max(hm, axis=(1, 2))
    for bit in bits:
        local = jnp.maximum(local, swap(local, "dp", bit))
    head_max = local
    cs4 = cs[0:4].reshape(4, 2, 2, SHARE)
    cs4 = pick(cs4, 2, core)
    early = jnp.concatenate([pick(cs4, 1, y).reshape(-1), bs[0, :UNITS]])
    away = jnp.concatenate([pick(cs4, 1, 1 - y).reshape(-1), bs[0, UNITS:]])
    early = dp_total(early + y_swap(away))
    late = dp_total(
        jnp.concatenate([jnp.sum(g_first * xhat, axis=0), jnp.sum(g_first, axis=0), qv[0], qv[1]])
    )
    of = lambda value, n: value[n * SHARE : (n + 1) * SHARE]

    column_scale = jnp.repeat(jnp.sqrt(TAU / jnp.maximum(head_max, TAU)), HD)
    return (
        output,
        tokens_grad,
        of(late, 0),
        of(late, 1),
        gw[0].T,
        of(late, 2),
        gw[1].T,
        gw[2].T,
        of(late, 3),
        gw[3],
        of(early, 2),
        of(early, 0),
        of(early, 1),
        w_up_grad,
        early[4 * SHARE :],
        w_down_grad,
        of(early, 3),
        head_max,
        w_query.astype(F32) * column_scale,
        b_query.astype(F32) * column_scale,
        w_key.astype(F32) * column_scale,
    )


def solution(mesh):
    in_specs = (
        P("dp", "tensor"),
        P("dp", "tensor"),
        P("dp", None),
        P("dp", None),
        P("tensor"),
        P("tensor"),
        P(None, "tensor"),
        P("tensor"),
        P(None, "tensor"),
        P(None, "tensor"),
        P("tensor"),
        P("tensor", None),
        P("tensor"),
        P("tensor"),
        P("tensor"),
        P(None, "tensor"),
        P("tensor"),
        P("tensor", None),
        P("tensor"),
    )
    out_specs = (
        P("dp", "tensor"),
        P("dp", "tensor"),
        P("tensor"),
        P("tensor"),
        P("dp", "tensor"),
        P("tensor"),
        P("dp", "tensor"),
        P("dp", "tensor"),
        P("tensor"),
        P("tensor", "dp"),
        P("tensor"),
        P("tensor"),
        P("tensor"),
        P("dp", "tensor"),
        P("tensor"),
        P("tensor", "dp"),
        P("tensor"),
        P("tensor"),
        P(None, "tensor"),
        P("tensor"),
        P(None, "tensor"),
    )
    return jax.shard_map(shards, mesh=mesh, in_specs=in_specs, out_specs=out_specs, check_vma=False)
```

```python
import functools
import math

import jax
import jax.numpy as jnp
from jax import lax
from jax.experimental import pallas as pl
from jax.experimental.pallas import tpu as pltpu
from jax.sharding import PartitionSpec as P

HEADS = 16
HD = 64
WIN = 1024
D = 1024
FF = 4096
SEQ = 2048
B = 256
NB = SEQ // B
SLOTS = WIN // B + 1
STRIP = SLOTS * B
LH = 4
SHARE = LH * HD
UNITS = FF // 4
TILE = 512
OWN = SEQ // 2

EPS = 1e-05
TAU = 2.0
NEG = -1e30
F32 = jnp.float32
BF = jnp.bfloat16
VMEM_LIMIT = 56 * 2**20


def dot(a, b):
    return jnp.dot(a, b, preferred_element_type=F32)


def dot_nt(a, b):
    return lax.dot_general(a, b, (((1,), (1,)), ((), ())), preferred_element_type=F32)


def params():
    return pltpu.CompilerParams(
        dimension_semantics=("arbitrary",), vmem_limit_bytes=VMEM_LIMIT
    )


def feature_block(rank):
    return pl.ds(pl.multiple_of(rank * SHARE, SHARE), SHARE)


def head_of_lane(shape):
    return lax.broadcasted_iota(jnp.int32, shape, 1) // HD


def ordered(kernel, count):
    return lambda ids, *refs: kernel(ids, *refs[count:])


def waits(after):
    return [pl.BlockSpec(memory_space=pl.ANY)] * len(after)


def row_stats(rows):
    mean = jnp.sum(rows, axis=1, keepdims=True) / D
    square = jnp.sum(rows * rows, axis=1, keepdims=True) / D
    return mean, lax.rsqrt(square - mean * mean + EPS)


def piece(ids, j, bit, chunk):
    inner = bit * chunk
    mine = lax.rem(ids[1 + NB] // bit, 2)
    base = (j * 128) // inner * (2 * inner) + (j * 128) % inner
    return [
        pl.ds(pl.multiple_of(base + side * inner, 128), 128) for side in (mine, 1 - mine)
    ]


def split_store(keep_ref, send_ref, value_ref, core):
    for half in range(2):
        cols = slice(half * SHARE, (half + 1) * SHARE)
        keep_ref[:, cols] = value_ref[:, feature_block(2 * half + core)].astype(keep_ref.dtype)
        send_ref[:, cols] = value_ref[:, feature_block(2 * half + 1 - core)].astype(
            send_ref.dtype
        )


TAIL = 3


def place():
    t = lax.axis_index("tensor")
    core, y = lax.rem(t, 2), lax.div(t, 2)
    return core, y, (t, 2 * y + 1 - core, 2 * (1 - y) + core, 2 * (1 - y) + 1 - core)


def fwd_kernel(
    x_any, x_own, vec, wq, wk, wv, bqv, wd, lo, pad, alibi,
    p_ref, q_ref, k_ref, v_ref, linv_ref, ctx_ref, a_ref, b_ref, x1_ref, x2_ref, x3_ref, hm_ref,
    xs, qm_s, k_s, va_s, u_s, res_s, lo_s,
    xc, xy, xf, part_keep, part_send, part_got, sum_keep, sum_send, sum_got, whole_own, whole_got,
    s_xc, r_xc, s_xy, r_xy, s_xf, r_xf, s_pc, r_pc, s_sy, r_sy, s_wc, r_wc,
):
    step = pl.program_id(0)
    core, y, ranks = place()

    def rows(b):
        return pl.ds(pl.multiple_of(b * B, B), B)

    def remote(src, dst, send, got, rank):
        return pltpu.make_async_remote_copy(
            src_ref=src, dst_ref=dst, send_sem=send, recv_sem=got,
            device_id={"tensor": rank}, device_id_type=pl.DeviceIdType.MESH,
        )

    def to_core(b):
        return remote(x_any.at[rows(b)], xc.at[b], s_xc.at[b], r_xc.at[b], ranks[1])

    def to_y(b):
        return remote(x_any.at[rows(b)], xy.at[b], s_xy.at[b], r_xy.at[b], ranks[2])

    def forward(b):
        return remote(xy.at[b], xf.at[b], s_xf.at[b], r_xf.at[b], ranks[1])

    def part_to_core(b):
        return remote(part_send.at[b], part_got.at[b], s_pc.at[b], r_pc.at[b], ranks[1])

    def sum_to_y(j):
        return remote(sum_send.at[j], sum_got.at[j], s_sy.at[j], r_sy.at[j], ranks[2])

    def whole_to_core(j):
        return remote(whole_own.at[j], whole_got.at[j], s_wc.at[j], r_wc.at[j], ranks[1])

    @pl.when(step == 0)
    def _():
        barrier = pltpu.get_barrier_semaphore()
        for rank in (ranks[1], ranks[2]):
            pl.semaphore_signal(
                barrier, inc=1, device_id={"tensor": rank}, device_id_type=pl.DeviceIdType.MESH
            )
        pl.semaphore_wait(barrier, 2)
        for b in range(3):
            to_y(b).start()
            to_core(b).start()
        to_y(0).wait_recv()
        forward(0).start()
        hm_ref[...] = jnp.full(hm_ref.shape, NEG, F32)

    for b in range(3, NB):

        @pl.when(step == b - 2)
        def _():
            to_y(b).start()
            to_core(b).start()

    row_i = lax.broadcasted_iota(jnp.int32, (B, B), 0)
    col_i = lax.broadcasted_iota(jnp.int32, (B, B), 1)
    lanes = head_of_lane((B, SHARE))

    @pl.when(step < NB - 1)
    def _():
        to_y(step + 1).wait_recv()
        forward(step + 1).start()

    @pl.when(step < NB)
    def _():
        to_core(step).wait_recv()
        forward(step).wait_recv()
        blocks = (x_own[...], xc[step], xy[step], xf[step])
        for rank, block, ref in zip(ranks, blocks, (None, x1_ref, x2_ref, x3_ref)):
            xs[:, feature_block(rank)] = block.astype(F32)
            if ref is not None:
                ref[...] = block
        value = xs[...]
        mean, rstd = row_stats(value)
        n1 = ((value - mean) * rstd * vec[0:1, :] + vec[1:2, :]).astype(BF)
        q = (dot(n1, wq[...]) + bqv[0:1, :]).astype(BF)
        k = dot(n1, wk[...]).astype(BF)
        v = (dot(n1, wv[...]) + bqv[1:2, :]).astype(BF)
        qs = q * jnp.asarray(1.0 / math.sqrt(HD), BF)
        q_ref[...] = qs
        k_ref[...] = k
        v_ref[...] = v
        here = rows(step)
        k_s[here, :] = k
        for h in range(LH):
            qm_s[h] = jnp.where(lanes == h, qs, jnp.zeros_like(qs))
            va_s[h, here, :] = jnp.where(lanes == h, v, jnp.ones_like(v))
        lo_s[...] = jnp.broadcast_to(lo[...], (B, B))

    def attend(nb):
        start = pl.multiple_of((step + 1 - nb) * B, B)

        def head(h, carry):
            qm = qm_s[h]
            top = jnp.full((B, 128), NEG, F32)
            biggest = hm_ref[h]
            for r in range(nb):
                slot = SLOTS - nb + r
                base = pl.multiple_of(start + r * B, B)
                s = dot_nt(qm, k_s[pl.ds(base, B), :])
                inside = col_i + base >= lo_s[...]
                shut = pad[0:1, pl.ds(base, B)]
                if r == nb - 1:
                    s = jnp.where(row_i == col_i, s, s + shut)
                    s = jnp.where(inside & (col_i <= row_i), s, NEG)
                else:
                    s = jnp.where(inside, s + shut, NEG)
                biggest = jnp.maximum(biggest, jnp.max(s.reshape(B // 8, 8, B), axis=0))
                s = s + alibi[pl.ds(h, 1), slot * B : (slot + 1) * B]
                u_s[:, slot * B : (slot + 1) * B] = s
                top = jnp.maximum(top, jnp.maximum(s[:, :128], s[:, 128:]))
            hm_ref[h] = biggest
            top = jnp.max(top, axis=1, keepdims=True)
            for r in range(nb):
                slot = SLOTS - nb + r
                cols = slice(slot * B, (slot + 1) * B)
                p_ref[h, :, cols] = jnp.exp(u_s[:, cols] - top).astype(BF)
            res_s[h] = dot(p_ref[h, :, (SLOTS - nb) * B :], va_s[h, pl.ds(start, nb * B), :])
            return carry

        lax.fori_loop(0, LH, head, 0)

    for nb in range(1, SLOTS):
        pl.when(step == nb - 1)(functools.partial(attend, nb))
    pl.when((step >= SLOTS - 1) & (step < NB))(functools.partial(attend, SLOTS))

    @pl.when(step < NB)
    def _():
        ctx = res_s[0]
        total = res_s[LH - 1]
        for h in range(1, LH):
            ctx = jnp.where(lanes == h, res_s[h], ctx)
            total = jnp.where(lanes == h, res_s[h - 1], total)
        inv = 1.0 / pltpu.roll(total, SHARE - HD, 1)
        linv_ref[...] = inv
        ctx = (ctx * inv).astype(BF)
        ctx_ref[...] = ctx
        xs[...] = dot(ctx, wd[...])
        split_store(part_keep.at[step], part_send.at[step], xs, core)
        part_to_core(step).start()

    @pl.when((step >= 1) & (step <= NB))
    def _():
        b = step - 1
        j = b // 2
        part_to_core(b).wait_recv()
        total = part_keep[b].astype(F32) + part_got[b].astype(F32)

        @pl.when(lax.rem(b, 2) == y)
        def _():
            sum_keep[j] = total

        @pl.when(lax.rem(b, 2) != y)
        def _():
            sum_send[j] = total.astype(BF)
            sum_to_y(j).start()

    @pl.when((step >= TAIL) & (lax.rem(step + NB - TAIL, 2) == y))
    def _():
        j = (step - TAIL) // 2
        sum_to_y(j).wait_recv()
        total = (sum_keep[j] + sum_got[j].astype(F32)).astype(BF)
        whole_own[j] = total
        a_ref[rows(j), :] = total
        whole_to_core(j).start()

    @pl.when(step == NB + TAIL - 1)
    def _():
        for j in range(NB // 2):
            whole_to_core(j).wait_recv()
            b_ref[rows(j), :] = whole_got[j]
        for b in range(NB):
            to_core(b).wait_send()
            to_y(b).wait_send()
            forward(b).wait_send()
            part_to_core(b).wait_send()
        for j in range(NB // 2):
            sum_to_y(j).wait_send()
            whole_to_core(j).wait_send()


def attention_forward(x, vec, wq, wk, wv, bqv, wd, lo, pad, alibi):
    last = lambda s: jnp.minimum(s, NB - 1)
    row = lambda width: pl.BlockSpec((B, width), lambda s: (last(s), 0))
    whole = lambda shape: pl.BlockSpec(shape, lambda s: (0,) * len(shape))
    like = jax.ShapeDtypeStruct
    dma = lambda n: pltpu.SemaphoreType.DMA((n,))
    half = NB // 2
    return pl.pallas_call(
        fwd_kernel,
        grid=(NB + TAIL,),
        in_specs=[pl.BlockSpec(memory_space=pl.ANY), row(SHARE), whole((8, D))]
        + [whole((D, SHARE))] * 3
        + [whole((8, SHARE)), whole((SHARE, D)), row(1), whole((8, SEQ)), whole((8, STRIP))],
        out_specs=[pl.BlockSpec((LH, B, STRIP), lambda s: (0, last(s), 0))]
        + [row(SHARE)] * 5
        + [whole((OWN, D // 2))] * 2
        + [row(SHARE)] * 3
        + [whole((LH, 8, B))],
        scratch_shapes=[
            pltpu.VMEM((B, D), F32),
            pltpu.VMEM((LH, B, SHARE), BF),
            pltpu.VMEM((SEQ, SHARE), BF),
            pltpu.VMEM((LH, SEQ, SHARE), BF),
            pltpu.VMEM((B, STRIP), F32),
            pltpu.VMEM((LH, B, SHARE), F32),
            pltpu.VMEM((B, B), jnp.int32),
        ]
        + [pltpu.VMEM((NB, B, SHARE), BF)] * 3
        + [pltpu.VMEM((NB, B, D // 2), BF)] * 3
        + [pltpu.VMEM((half, B, D // 2), F32)]
        + [pltpu.VMEM((half, B, D // 2), BF)] * 4
        + [dma(NB)] * 8
        + [dma(half)] * 4,
        out_shape=[like((LH, SEQ, STRIP), BF)]
        + [like((SEQ, SHARE), BF)] * 3
        + [like((SEQ, SHARE), F32), like((SEQ, SHARE), BF)]
        + [like((OWN, D // 2), BF)] * 2
        + [like((SEQ, SHARE), BF)] * 3
        + [like((LH, 8, B), F32)],
        compiler_params=pltpu.CompilerParams(
            dimension_semantics=("arbitrary",),
            vmem_limit_bytes=VMEM_LIMIT,
            collective_id=0,
            has_side_effects=True,
        ),
        cost_estimate=pl.CostEstimate(
            flops=16 * 10**9, bytes_accessed=40 * 2**20, transcendentals=8 * 10**6
        ),
        name="attention_forward",
    )(x, x, vec, wq, wk, wv, bqv, wd, lo, pad, alibi)


def mlp_kernel(
    ids, a_own, a_par, x0, x1, x2, x3, d0, d1, d2, d3, vec, bup, wu0, wu1, wd0, wd1,
    mk_ref, ms_ref, gn_ref, h1_ref, gu_ref, su_ref, gd_ref, sd_ref, bs_ref,
    n2_s, n2t_s, dy_s, dyt_s, am_s, ag_s, act_s, gp_s,
    *, bits, chunk,
):
    i = pl.program_id(0)
    t = ids[0]
    core = lax.rem(t, 2)

    @pl.when(i == 0)
    def _():
        def assemble(rb, carry):
            rows = pl.ds(pl.multiple_of(rb * B, B), B)
            for r, (x, d) in enumerate(((x0, d0), (x1, d1), (x2, d2), (x3, d3))):
                h1_ref[rows, feature_block(t ^ r)] = x[rb, 0].astype(F32)
                dy_s[rows, feature_block(t ^ r)] = d[rows, :]
            for part, a in ((core, a_own), (1 - core, a_par)):
                for half in range(2):
                    cols = feature_block(2 * half + part)
                    h1_ref[rows, cols] += a[rows, half * SHARE : (half + 1) * SHARE].astype(F32)
            value = h1_ref[rows, :] + vec[2:3, :]
            h1_ref[rows, :] = value
            mean, rstd = row_stats(value)
            n2 = ((value - mean) * rstd * vec[3:4, :] + vec[4:5, :]).astype(BF)
            n2_s[rows, :] = n2
            n2t_s[:, rows] = n2.T
            dyt_s[:, rows] = dy_s[rows, :].T
            am_s[rows, :] = jnp.zeros((B, D), F32)
            ag_s[rows, :] = jnp.zeros((B, D), F32)
            return carry

        lax.fori_loop(0, OWN // B, assemble, 0)

    def tile(wu, wd, which):
        bias = bup[which : which + 1, pl.ds(pl.multiple_of(lax.rem(i, 2) * TILE, TILE), TILE)]
        scale = math.sqrt(2.0 / math.pi)

        def rows_of(rb, sums):
            rows = pl.ds(pl.multiple_of(rb * B, B), B)
            pre = dot(n2_s[rows, :], wu[...]) + bias
            back = dot_nt(dy_s[rows, :], wd[...])
            square = pre * pre
            th = jnp.tanh(scale * pre * (1.0 + 0.044715 * square))
            half = 0.5 * (1.0 + th)
            act = (pre * half).astype(BF)
            slope = half + 0.5 * pre * (1.0 - th * th) * (scale + (3 * 0.044715 * scale) * square)
            gp = (slope * back).astype(BF)
            act_s[rows, :] = act
            gp_s[rows, :] = gp
            am_s[rows, :] += dot(act, wd[...])
            ag_s[rows, :] += dot_nt(gp, wu[...])
            return sums + jnp.sum(gp.astype(F32), axis=0, keepdims=True)

        sums = lax.fori_loop(0, OWN // B, rows_of, jnp.zeros((1, TILE), F32))
        bs_ref[...] = jnp.broadcast_to(sums, bs_ref.shape)

        def grads(j, carry):
            to = pl.ds(pl.multiple_of(j * 128, 128), 128)
            for bit, left, right, keep, send in (
                (bits[0], n2t_s, gp_s, gu_ref, su_ref),
                (bits[1], dyt_s, act_s, gd_ref, sd_ref),
            ):
                for ref, rows in zip((keep, send), piece(ids, j, bit, chunk)):
                    ref[to, :] = dot(left[rows, :], right[...]).astype(ref.dtype)
            return carry

        lax.fori_loop(0, D // 256, grads, 0)

    pl.when(i < 2)(lambda: tile(wu0, wd0, 0))
    pl.when(i >= 2)(lambda: tile(wu1, wd1, 1))

    @pl.when(i == 3)
    def _():
        split_store(mk_ref, ms_ref, am_s, core)
        gn_ref[...] = ag_s[...].astype(BF)


def feed_forward(ids, a_own, a_par, xs, ds, vec, bup, wu0, wd0, w_other, bits, chunk):
    whole = lambda shape: pl.BlockSpec(shape, lambda i, ids: (0,) * len(shape))
    low = lambda i: jnp.minimum(i, 1)
    high = lambda i: jnp.maximum(i - 2, 0)
    xs = [x.reshape(NB // 2, 2, B, SHARE) for x in xs]
    return pl.pallas_call(
        functools.partial(mlp_kernel, bits=bits, chunk=chunk),
        grid_spec=pltpu.PrefetchScalarGridSpec(
            num_scalar_prefetch=1,
            grid=(4,),
            in_specs=[whole((OWN, D // 2))] * 2
            + [pl.BlockSpec((NB // 2, 1, B, SHARE), lambda i, ids: (0, ids[0] // 2, 0, 0))] * 4
            + [whole((OWN, SHARE))] * 4
            + [
                whole((8, D)),
                whole((8, UNITS)),
                pl.BlockSpec((D, TILE), lambda i, ids: (0, low(i))),
                pl.BlockSpec((D, TILE), lambda i, ids: (0, high(i))),
                pl.BlockSpec((TILE, D), lambda i, ids: (low(i), 0)),
                pl.BlockSpec((TILE, D), lambda i, ids: (high(i), 1)),
            ],
            out_specs=[
                whole((OWN, D // 2)),
                whole((OWN, D // 2)),
                whole((OWN, D)),
                whole((OWN, D)),
                pl.BlockSpec((D // 2, TILE), lambda i, ids: (0, i)),
                pl.BlockSpec((D // 2, TILE), lambda i, ids: (0, i)),
                pl.BlockSpec((D // 2, TILE), lambda i, ids: (0, i)),
                pl.BlockSpec((D // 2, TILE), lambda i, ids: (0, i)),
                pl.BlockSpec((8, TILE), lambda i, ids: (0, i)),
            ],
            scratch_shapes=[
                pltpu.VMEM((OWN, D), BF),
                pltpu.VMEM((D, OWN), BF),
                pltpu.VMEM((OWN, D), BF),
                pltpu.VMEM((D, OWN), BF),
                pltpu.VMEM((OWN, D), F32),
                pltpu.VMEM((OWN, D), F32),
                pltpu.VMEM((OWN, TILE), BF),
                pltpu.VMEM((OWN, TILE), BF),
            ],
        ),
        out_shape=[
            jax.ShapeDtypeStruct((OWN, D // 2), BF),
            jax.ShapeDtypeStruct((OWN, D // 2), BF),
            jax.ShapeDtypeStruct((OWN, D), BF),
            jax.ShapeDtypeStruct((OWN, D), F32),
            jax.ShapeDtypeStruct((D // 2, 2 * UNITS), BF),
            jax.ShapeDtypeStruct((D // 2, 2 * UNITS), BF),
            jax.ShapeDtypeStruct((D // 2, 2 * UNITS), BF),
            jax.ShapeDtypeStruct((D // 2, 2 * UNITS), BF),
            jax.ShapeDtypeStruct((8, 2 * UNITS), F32),
        ],
        compiler_params=params(),
        cost_estimate=pl.CostEstimate(
            flops=26 * 10**9, bytes_accessed=40 * 2**20, transcendentals=2 * 10**6
        ),
        name="feed_forward",
    )(ids, a_own, a_par, *xs, *ds, vec, bup, wu0, w_other, wd0, w_other)


def mid_kernel(
    ids, h1, gn, gr, d0, d1, d2, d3, mk, mr, vec,
    gh_ref, gs_ref, oo_ref, os_ref, cs_ref,
    w_s,
):
    i = pl.program_id(0)
    t = ids[0]
    core = lax.rem(t, 2)
    y = t // 2
    for r, d in enumerate((d0, d1, d2, d3)):
        w_s[:, feature_block(t ^ r)] = d[...].astype(F32)
    dy = w_s[...]
    rows = h1[...]
    for half, ref in ((y, oo_ref), (1 - y, os_ref)):
        cols = feature_block(2 * half + core)
        part = pl.ds(pl.multiple_of(half * SHARE, SHARE), SHARE)
        total = mk[:, part].astype(F32) + mr[:, part].astype(F32)
        ref[...] = (h1[:, cols] + total + vec[5:6, cols]).astype(BF)
    mean, rstd = row_stats(rows)
    xhat = (rows - mean) * rstd
    grad = gn[...].astype(F32) + gr[...].astype(F32)
    scaled = grad * vec[3:4, :]
    first = jnp.sum(scaled, axis=1, keepdims=True) / D
    second = jnp.sum(scaled * xhat, axis=1, keepdims=True) / D
    gh = dy + rstd * (scaled - first - xhat * second)
    low = gh.astype(BF)
    gh_ref[...] = low
    w_s[...] = gh
    for half in range(2):
        gs_ref[:, half * SHARE : (half + 1) * SHARE] = w_s[:, feature_block(2 * half + core)].astype(BF)

    @pl.when(i == 0)
    def _():
        cs_ref[...] = jnp.zeros(cs_ref.shape, F32)

    for n, value in enumerate((grad * xhat, grad, gh, dy)):
        cs_ref[n : n + 1, :] += jnp.sum(value, axis=0, keepdims=True)


def middle(ids, h1, gn, gr, ds, mk, mr, vec):
    row = lambda width: pl.BlockSpec((B, width), lambda i, ids: (i, 0))
    whole = lambda shape: pl.BlockSpec(shape, lambda i, ids: (0,) * len(shape))
    return pl.pallas_call(
        mid_kernel,
        grid_spec=pltpu.PrefetchScalarGridSpec(
            num_scalar_prefetch=1,
            grid=(OWN // B,),
            in_specs=[row(D)] * 3 + [row(SHARE)] * 4 + [row(D // 2)] * 2 + [whole((8, D))],
            out_specs=[row(D), row(D // 2), row(SHARE), row(SHARE), whole((8, D))],
            scratch_shapes=[pltpu.VMEM((B, D), F32)],
        ),
        out_shape=[
            jax.ShapeDtypeStruct((OWN, D), BF),
            jax.ShapeDtypeStruct((OWN, D // 2), BF),
            jax.ShapeDtypeStruct((OWN, SHARE), BF),
            jax.ShapeDtypeStruct((OWN, SHARE), BF),
            jax.ShapeDtypeStruct((8, D), F32),
        ],
        compiler_params=params(),
        cost_estimate=pl.CostEstimate(flops=20 * 2**20, bytes_accessed=16 * 2**20, transcendentals=0),
        name="second_norm_backward",
    )(ids, h1, gn, gr, *ds, mk, mr, vec)


def bwd_kernel(
    ids, x0, x1, x2, x3, gh, ga, gb, p_ref, q_ref, linv_ref, ctx_ref, k_ref, v_ref, vec, wq, wk, wv, wd,
    f0, f1, f2, f3, st_ref, ghx_ref, ka_ref, sa_ref, kb_ref, sb_ref, bs_ref,
    xs, gh_s, gm_s, gt_s, qt_s, dl_s, ds_s, res_s, dkt_s, dvt_s, acc_s,
    *, bits, chunk,
):
    i = pl.program_id(0)
    b = NB - 1 - i
    t = ids[0]
    core = lax.rem(t, 2)
    y = t // 2

    @pl.when(i == 0)
    def _():
        dkt_s[...] = jnp.zeros(dkt_s.shape, F32)
        dvt_s[...] = jnp.zeros(dvt_s.shape, F32)
        acc_s[...] = jnp.zeros(acc_s.shape, F32)
        bs_ref[...] = jnp.zeros(bs_ref.shape, F32)

    @pl.when(lax.rem(b, 2) == y)
    def _():
        gh_s[...] = gh[...]

    @pl.when(lax.rem(b, 2) != y)
    def _():
        for part, ref in ((core, ga), (1 - core, gb)):
            for half in range(2):
                gh_s[:, feature_block(2 * half + part)] = ref[:, half * SHARE : (half + 1) * SHARE]

    ghl = gh_s[...]
    ghx_ref[...] = gh_s[:, feature_block(t)]
    gc = dot_nt(ghl, wd[...]).astype(BF).astype(F32)
    ctx = ctx_ref[...]
    scaled = gc * linv_ref[...]
    gcs = scaled.astype(BF)
    product = scaled * ctx.astype(F32)
    lanes = head_of_lane((B, SHARE))
    q = q_ref[...]
    qt_s[...] = q.T.reshape(LH, HD, B)
    gt_s[...] = gcs.T.reshape(LH, HD, B)
    for h in range(LH):
        gm_s[h] = jnp.where(lanes == h, gcs, jnp.zeros_like(gcs))
        delta = jnp.sum(jnp.where(lanes == h, product, 0.0), axis=1, keepdims=True)
        dl_s[h] = jnp.broadcast_to(delta, (B, B))

    def attend(nb):
        start = pl.multiple_of((b + 1 - nb) * B, B)

        def head(h, carry):
            gm = gm_s[h]
            for r in range(nb):
                slot = SLOTS - nb + r
                cols = slice(slot * B, (slot + 1) * B)
                dp = dot_nt(gm, v_ref[pl.ds(pl.multiple_of(start + r * B, B), B), :])
                ds_s[:, cols] = (p_ref[h, :, cols].astype(F32) * (dp - dl_s[h])).astype(BF)
            live = slice((SLOTS - nb) * B, STRIP)
            keys = pl.ds(start, nb * B)
            res_s[h] = dot(ds_s[:, live], k_ref[keys, :])
            dkt_s[h, :, keys] += dot(qt_s[h], ds_s[:, live])
            dvt_s[h, :, keys] += dot(gt_s[h], p_ref[h, :, live])
            return carry

        lax.fori_loop(0, LH, head, 0)

    count = b - ids[1 + b] + 1
    for nb in range(1, SLOTS + 1):
        pl.when(count == nb)(functools.partial(attend, nb))

    dq = res_s[0]
    for h in range(1, LH):
        dq = jnp.where(lanes == h, res_s[h], dq)
    dq = (dq * (1.0 / math.sqrt(HD))).astype(BF)
    here = pl.ds(pl.multiple_of(b * B, B), B)
    dkt = dkt_s[:, :, here].reshape(SHARE, B).astype(BF)
    dvt = dvt_s[:, :, here].reshape(SHARE, B).astype(BF)
    dk = dkt.T
    dv = dvt.T
    bs_ref[0:1, :] += jnp.sum(dq.astype(F32), axis=0, keepdims=True)
    bs_ref[1:2, :] += jnp.sum(dv.astype(F32), axis=0, keepdims=True)

    for r, x in enumerate((x0, x1, x2, x3)):
        xs[:, feature_block(t ^ r)] = x[...].astype(F32)
    rows = xs[...]
    mean, rstd = row_stats(rows)
    xhat = (rows - mean) * rstd
    n1 = (xhat * vec[0:1, :] + vec[1:2, :]).astype(BF)
    n1t = n1.T
    acc_s[:, 0:SHARE] += dot(n1t, dq)
    acc_s[:, SHARE : 2 * SHARE] += dot(n1t, dk)
    acc_s[:, 2 * SHARE : 3 * SHARE] += dot(n1t, dv)
    acc_s[:, 3 * SHARE :] += dot(ghl.T, ctx)

    grad = dot_nt(dq, wq[...]) + dot_nt(dk, wk[...]) + dot_nt(dv, wv[...])
    xs[...] = grad
    for r, ref in enumerate((f0, f1, f2, f3)):
        ref[...] = xs[:, feature_block(t ^ r)].astype(BF)
    scaled = grad * vec[0:1, :]
    first = jnp.sum(scaled, axis=1, keepdims=True)
    second = jnp.sum(scaled * xhat, axis=1, keepdims=True)
    column = lax.broadcasted_iota(jnp.int32, (B, 128), 1)
    packed = jnp.where(
        column == 0, first, jnp.where(column == 1, second, jnp.where(column == 2, mean, rstd))
    )
    st_ref[...] = packed.T[0:8, :]

    @pl.when(i == NB - 1)
    def _():
        for j in range(D // 256):
            to = slice(j * 128, (j + 1) * 128)
            for bit, keep, send, cols in (
                (bits[0], ka_ref, sa_ref, slice(0, 2 * SHARE)),
                (bits[1], kb_ref, sb_ref, slice(2 * SHARE, 4 * SHARE)),
            ):
                for ref, rows in zip((keep, send), piece(ids, j, bit, chunk)):
                    ref[to, :] = acc_s[rows, cols].astype(BF)


def attention_backward(
    ids, xs, gh, ga, gb, p, q, linv, ctx, k, v, vec, wq, wk, wv, wd, bits, chunk, after
):
    row = lambda width: pl.BlockSpec((B, width), lambda i, ids: (NB - 1 - i, 0))
    own = lambda width: pl.BlockSpec((B, width), lambda i, ids: ((NB - 1 - i) // 2, 0))
    whole = lambda shape: pl.BlockSpec(shape, lambda i, ids: (0,) * len(shape))
    return pl.pallas_call(
        ordered(functools.partial(bwd_kernel, bits=bits, chunk=chunk), len(after)),
        grid_spec=pltpu.PrefetchScalarGridSpec(
            num_scalar_prefetch=1,
            grid=(NB,),
            in_specs=waits(after)
            + [row(SHARE)] * 4
            + [own(D), own(D // 2), own(D // 2)]
            + [pl.BlockSpec((LH, B, STRIP), lambda i, ids: (0, NB - 1 - i, 0))]
            + [row(SHARE)] * 3
            + [whole((SEQ, SHARE))] * 2
            + [whole((8, D))]
            + [whole((D, SHARE))] * 3
            + [whole((SHARE, D))],
            out_specs=[
                row(SHARE),
                row(SHARE),
                row(SHARE),
                row(SHARE),
                pl.BlockSpec((8, B), lambda i, ids: (0, NB - 1 - i)),
                row(SHARE),
                whole((D // 2, 2 * SHARE)),
                whole((D // 2, 2 * SHARE)),
                whole((D // 2, 2 * SHARE)),
                whole((D // 2, 2 * SHARE)),
                whole((8, SHARE)),
            ],
            scratch_shapes=[
                pltpu.VMEM((B, D), F32),
                pltpu.VMEM((B, D), BF),
                pltpu.VMEM((LH, B, SHARE), BF),
                pltpu.VMEM((LH, HD, B), BF),
                pltpu.VMEM((LH, HD, B), BF),
                pltpu.VMEM((LH, B, B), F32),
                pltpu.VMEM((B, STRIP), BF),
                pltpu.VMEM((LH, B, SHARE), F32),
                pltpu.VMEM((LH, HD, SEQ), F32),
                pltpu.VMEM((LH, HD, SEQ), F32),
                pltpu.VMEM((D, 4 * SHARE), F32),
            ],
        ),
        out_shape=[
            jax.ShapeDtypeStruct((SEQ, SHARE), BF),
            jax.ShapeDtypeStruct((SEQ, SHARE), BF),
            jax.ShapeDtypeStruct((SEQ, SHARE), BF),
            jax.ShapeDtypeStruct((SEQ, SHARE), BF),
            jax.ShapeDtypeStruct((8, SEQ), F32),
            jax.ShapeDtypeStruct((SEQ, SHARE), BF),
            jax.ShapeDtypeStruct((D // 2, 2 * SHARE), BF),
            jax.ShapeDtypeStruct((D // 2, 2 * SHARE), BF),
            jax.ShapeDtypeStruct((D // 2, 2 * SHARE), BF),
            jax.ShapeDtypeStruct((D // 2, 2 * SHARE), BF),
            jax.ShapeDtypeStruct((8, SHARE), F32),
        ],
        compiler_params=params(),
        cost_estimate=pl.CostEstimate(
            flops=30 * 10**9, bytes_accessed=50 * 2**20, transcendentals=0
        ),
        name="attention_backward",
    )(ids, *after, *xs, gh, ga, gb, p, q, linv, ctx, k, v, vec, wq, wk, wv, wd)


def swap(value, axis, bit):
    size = lax.axis_size(axis)
    return lax.ppermute(value, axis, [(i, i ^ bit) for i in range(size)])


def dp_bits():
    bits, bit = [], 1
    while bit < lax.axis_size("dp"):
        bits.append(bit)
        bit *= 2
    return bits


def dp_total(value):
    for bit in dp_bits():
        value = value + swap(value, "dp", bit)
    return value


def pick(value, axis, index):
    return lax.dynamic_index_in_dim(value, index, axis, keepdims=False)


def sum_kernel(bit, km, rm, ko, ro, keep_ref, send_ref):
    for a, b, ref in ((km, rm, keep_ref), (ko, ro, send_ref)):
        ref[...] = (a[...].astype(F32) + b[...].astype(F32)).astype(ref.dtype)


def sum_and_split(bit, keep, other, inner, after=()):
    rows, cols = keep.shape
    step = min(inner, 128)
    per = inner // step
    block = lambda side: pl.BlockSpec(
        (step, cols),
        lambda i, bit: (i // per * 2 * per + (bit[0] if side else 1 - bit[0]) * per + i % per, 0),
    )
    out = pl.BlockSpec((step, cols), lambda i, bit: (i, 0))
    return pl.pallas_call(
        ordered(sum_kernel, len(after)),
        grid_spec=pltpu.PrefetchScalarGridSpec(
            num_scalar_prefetch=1,
            grid=(rows // 2 // step,),
            in_specs=waits(after) + [block(True), block(True), block(False), block(False)],
            out_specs=[out, out],
        ),
        out_shape=[jax.ShapeDtypeStruct((rows // 2, cols), BF)] * 2,
        compiler_params=params(),
        cost_estimate=pl.CostEstimate(flops=rows * cols, bytes_accessed=6 * rows * cols, transcendentals=0),
        name="sum_and_split",
    )(bit, *after, keep, other, keep, other)


def dp_scatter(keep, send, order, after=()):
    rank = lax.axis_index("dp")
    chunk = D // lax.axis_size("dp")
    for n, bit in enumerate(order):
        other = swap(send, "dp", bit)
        if n == len(order) - 1:
            yield keep.astype(F32) + other.astype(F32)
            return
        following = order[n + 1]
        inner = chunk
        for b in order[n + 2 :]:
            inner *= 2 if b < following else 1
        wait = yield send
        mine = ((rank // following) % 2)[None]
        keep, send = sum_and_split(mine, keep, other, inner, wait or ())


def finish(steps, after=()):
    try:
        while True:
            value = steps.send(after)
    except StopIteration:
        return value


def shards(
    tokens,
    out_grad,
    segments,
    padding,
    norm1_gain,
    norm1_bias,
    w_query,
    b_query,
    w_key,
    w_value,
    b_value,
    w_dense,
    dense_bias,
    norm2_gain,
    norm2_bias,
    w_up,
    b_up,
    w_down,
    down_bias,
):
    t = lax.axis_index("tensor")
    rank = lax.axis_index("dp")
    size = lax.axis_size("dp")
    core, y = t % 2, t // 2
    core_swap = lambda value: swap(value, "tensor", 1)
    y_swap = lambda value: swap(value, "tensor", 2)
    rows8 = lambda value: jnp.pad(value, ((0, 8 - value.shape[0]), (0, 0)))

    vectors = jnp.stack([norm1_gain, norm1_bias, dense_bias, norm2_gain, norm2_bias, down_bias])
    vec = lax.dynamic_update_slice(jnp.zeros((6, D), BF), vectors, (0, t * SHARE))
    vec = vec + core_swap(vec)
    vec = rows8((vec + y_swap(vec)).astype(F32))

    part = D // size
    cut = lambda w: lax.dynamic_slice_in_dim(w, rank * part, part, 0)
    w_part = y_swap(jnp.concatenate([cut(w_up), cut(w_down)], axis=1))
    w_other = lax.all_gather(w_part, "dp", axis=0, tiled=True)
    b_up_pair = jnp.stack([b_up, y_swap(b_up)]).astype(F32)

    seg = segments.reshape(SEQ)
    index = jnp.arange(SEQ, dtype=jnp.int32)
    first = jnp.zeros((SEQ,), jnp.int32)
    for value in range(1, 4):
        first = jnp.where(seg == value, jnp.sum((seg < value).astype(jnp.int32)), first)
    lowest = jnp.maximum(first, index - (WIN - 1))
    ids = jnp.concatenate(
        [t[None].astype(jnp.int32), lowest[::B] // B, rank[None].astype(jnp.int32)]
    )
    pad_row = rows8(jnp.where(padding.reshape(1, SEQ) == 1, 0.0, NEG).astype(F32))
    heads = t * LH + jnp.arange(LH)
    slopes = jnp.exp2(-8.0 * (heads.astype(F32) + 1.0) / HEADS)
    alibi = rows8(slopes[:, None] * (jnp.arange(STRIP) - (STRIP - 1)).astype(F32)[None, :])

    by_y = lambda value, which: pick(value.reshape(NB // 2, 2, B, value.shape[-1]), 1, which).reshape(
        OWN, value.shape[-1]
    )
    d_own = by_y(out_grad, y)
    d_send = by_y(out_grad, 1 - y)

    p, q, k, v, linv, ctx, a_own, a_par, x1, x2, x3, hm = attention_forward(
        tokens, vec, w_query, w_key, w_value,
        rows8(jnp.stack([b_query, b_value]).astype(F32)), w_dense,
        lowest.reshape(SEQ, 1), pad_row, alibi,
    )
    xs = [tokens, x1, x2, x3]

    d_y = y_swap(d_send)
    ds = [d_own, core_swap(d_own), d_y, core_swap(d_y)]

    bits = dp_bits()
    order_a = bits if size == 8 else bits[::-1]
    order_b = [2, 4, 1] if size == 8 else [bits[-2], bits[-1], *bits[:-2][::-1]]
    mk, ms, gn, h1, gu, su, gd, sd, bs = feed_forward(
        ids, a_own, a_par, xs, ds, vec, rows8(b_up_pair), w_up, w_down, w_other,
        (order_a[0], order_b[0]), part,
    )
    gr = core_swap(gn)
    mr = core_swap(ms)
    gh, gs, out_own, out_send, cs = middle(ids, h1, gn, gr, ds, mk, mr, vec)
    ga = y_swap(gs)
    gb = core_swap(ga)

    out_y = y_swap(out_send)
    pair = jnp.stack([out_own, out_y]).reshape(2, NB // 2, B, SHARE)
    output = jnp.where(y == 0, pair, pair[::-1]).transpose(1, 0, 2, 3).reshape(SEQ, SHARE)

    steps_u = dp_scatter(gu, su, order_a)
    steps_d = dp_scatter(gd, sd, order_b)
    next(steps_u), next(steps_d)
    sent = (steps_u.send(()), steps_d.send(()))

    f0, f1, f2, f3, stats, ghx, ka, sa, kb, sb, qv = attention_backward(
        ids, xs, gh, ga, gb, p, q, linv, ctx, k, v, vec, w_query, w_key, w_value, w_dense,
        (order_a[0], order_b[0]), part, sent,
    )
    add = lambda a, b: (a.astype(F32) + b.astype(F32)).astype(BF)
    away = add(f2, core_swap(f3))
    g_first = add(f0, core_swap(f1)).astype(F32) + y_swap(away).astype(F32)
    sums = stats[0:2]
    sums = sums + core_swap(sums)
    sums = sums + y_swap(sums)
    first, second = sums[0][:, None] / D, sums[1][:, None] / D
    mean, rstd = stats[2][:, None], stats[3][:, None]
    xhat = (tokens.astype(F32) - mean) * rstd
    scaled = g_first * norm1_gain.astype(F32)[None, :]
    tokens_grad = ghx.astype(F32) + rstd * (scaled - first - xhat * second)

    gu = finish(steps_u, (qv,))
    gd = finish(steps_d, (qv,))
    w_up_grad = gu[:, :UNITS] + y_swap(gu[:, UNITS:].astype(BF)).astype(F32)
    w_down_grad = (gd[:, :UNITS] + y_swap(gd[:, UNITS:].astype(BF)).astype(F32)).T
    steps_a = dp_scatter(ka, sa, order_a)
    steps_b = dp_scatter(kb, sb, order_b)
    next(steps_a), next(steps_b)
    g_qk = finish(steps_a, ())
    g_vd = finish(steps_b, ())

    cs4 = pick(cs[0:4].reshape(4, 2, 2, SHARE), 2, core)
    early = jnp.concatenate([pick(cs4, 1, y).reshape(-1), bs[0, :UNITS]])
    apart = jnp.concatenate([pick(cs4, 1, 1 - y).reshape(-1), bs[0, UNITS:]])
    early = early + y_swap(apart)
    late = jnp.concatenate([jnp.sum(g_first * xhat, axis=0), jnp.sum(g_first, axis=0), qv[0], qv[1]])
    packed = jnp.concatenate([early, late, jnp.pad(jnp.max(hm, axis=(1, 2)), (0, 124))])
    summed = lax.broadcasted_iota(jnp.int32, packed.shape, 0) < packed.shape[0] - 128
    for bit in bits:
        other = swap(packed, "dp", bit)
        packed = jnp.where(summed, packed + other, jnp.maximum(packed, other))
    early, late, head_max = jnp.split(packed, (8 * SHARE, 12 * SHARE))
    head_max = head_max[:LH]
    of = lambda value, n: value[n * SHARE : (n + 1) * SHARE]

    column_scale = jnp.repeat(jnp.sqrt(TAU / jnp.maximum(head_max, TAU)), HD)
    return (
        output,
        tokens_grad,
        of(late, 0),
        of(late, 1),
        g_qk[:, :SHARE],
        of(late, 2),
        g_qk[:, SHARE:],
        g_vd[:, :SHARE],
        of(late, 3),
        g_vd[:, SHARE:].T,
        of(early, 2),
        of(early, 0),
        of(early, 1),
        w_up_grad,
        early[4 * SHARE :],
        w_down_grad,
        of(early, 3),
        head_max,
        w_query.astype(F32) * column_scale,
        b_query.astype(F32) * column_scale,
        w_key.astype(F32) * column_scale,
    )


def solution(mesh):
    in_specs = (
        P("dp", "tensor"),
        P("dp", "tensor"),
        P("dp", None),
        P("dp", None),
        P("tensor"),
        P("tensor"),
        P(None, "tensor"),
        P("tensor"),
        P(None, "tensor"),
        P(None, "tensor"),
        P("tensor"),
        P("tensor", None),
        P("tensor"),
        P("tensor"),
        P("tensor"),
        P(None, "tensor"),
        P("tensor"),
        P("tensor", None),
        P("tensor"),
    )
    out_specs = (
        P("dp", "tensor"),
        P("dp", "tensor"),
        P("tensor"),
        P("tensor"),
        P("dp", "tensor"),
        P("tensor"),
        P("dp", "tensor"),
        P("dp", "tensor"),
        P("tensor"),
        P("tensor", "dp"),
        P("tensor"),
        P("tensor"),
        P("tensor"),
        P("dp", "tensor"),
        P("tensor"),
        P("tensor", "dp"),
        P("tensor"),
        P("tensor"),
        P(None, "tensor"),
        P("tensor"),
        P(None, "tensor"),
    )
    return jax.shard_map(shards, mesh=mesh, in_specs=in_specs, out_specs=out_specs, check_vma=False)
```

```python
import functools
import math

import jax
import jax.numpy as jnp
from jax import lax
from jax.experimental import pallas as pl
from jax.experimental.pallas import tpu as pltpu
from jax.sharding import PartitionSpec as P

HEADS = 16
HD = 64
WIN = 1024
D = 1024
FF = 4096
SEQ = 2048
B = 256
NB = SEQ // B
SLOTS = WIN // B + 1
STRIP = SLOTS * B
LH = 4
SHARE = LH * HD
UNITS = FF // 4
TILE = 512
OWN = SEQ // 2

EPS = 1e-05
TAU = 2.0
NEG = -1e30
F32 = jnp.float32
BF = jnp.bfloat16
VMEM_LIMIT = 62 * 2**20


def dot(a, b):
    return jnp.dot(a, b, preferred_element_type=F32)


def dot_nt(a, b):
    return lax.dot_general(a, b, (((1,), (1,)), ((), ())), preferred_element_type=F32)


def params():
    return pltpu.CompilerParams(
        dimension_semantics=("arbitrary",), vmem_limit_bytes=VMEM_LIMIT
    )


def feature_block(rank):
    return pl.ds(pl.multiple_of(rank * SHARE, SHARE), SHARE)


def head_of_lane(shape):
    return lax.broadcasted_iota(jnp.int32, shape, 1) // HD


def ordered(kernel, count):
    return lambda ids, *refs: kernel(ids, *refs[count:])


def waits(after):
    return [pl.BlockSpec(memory_space=pl.ANY)] * len(after)


def row_stats(rows):
    mean = jnp.sum(rows, axis=1, keepdims=True) / D
    square = jnp.sum(rows * rows, axis=1, keepdims=True) / D
    return mean, lax.rsqrt(square - mean * mean + EPS)


def piece(j, bit, chunk):
    inner = bit * chunk
    mine = dp_bit(bit)
    base = (j * 128) // inner * (2 * inner) + (j * 128) % inner
    return [
        pl.ds(pl.multiple_of(base + side * inner, 128), 128) for side in (mine, 1 - mine)
    ]


def dp_bit(bit):
    return lax.rem(lax.div(lax.axis_index("dp"), bit), 2)


def dp_partner(bit):
    return lax.axis_index("dp") + bit - 2 * bit * dp_bit(bit)


def place():
    t = lax.axis_index("tensor")
    core, y = lax.rem(t, 2), lax.div(t, 2)
    return core, y, (t, 2 * y + 1 - core, 2 * (1 - y) + core, 2 * (1 - y) + 1 - core)


def remote(src, dst, send, got, where):
    return pltpu.make_async_remote_copy(
        src_ref=src, dst_ref=dst, send_sem=send, recv_sem=got,
        device_id=where, device_id_type=pl.DeviceIdType.MESH,
    )


def greet(places):
    barrier = pltpu.get_barrier_semaphore()
    for where in places:
        pl.semaphore_signal(
            barrier, inc=1, device_id=where, device_id_type=pl.DeviceIdType.MESH
        )
    pl.semaphore_wait(barrier, len(places))


def block_rows(b):
    return pl.ds(pl.multiple_of(b * B, B), B)


def remote_params(collective_id):
    return pltpu.CompilerParams(
        dimension_semantics=("arbitrary",),
        vmem_limit_bytes=VMEM_LIMIT,
        collective_id=collective_id,
        has_side_effects=True,
    )


def split_store(keep_ref, send_ref, value_ref, core):
    for half in range(2):
        cols = slice(half * SHARE, (half + 1) * SHARE)
        keep_ref[:, cols] = value_ref[:, feature_block(2 * half + core)].astype(keep_ref.dtype)
        send_ref[:, cols] = value_ref[:, feature_block(2 * half + 1 - core)].astype(
            send_ref.dtype
        )


TAIL = 3


def fwd_kernel(
    x_any, x_own, vec, wq, wk, wv, bqv, wd, lo, pad, alibi,
    p_ref, q_ref, k_ref, v_ref, linv_ref, ctx_ref, a_ref, b_ref, x1_ref, x2_ref, x3_ref, xm_ref, hm_ref,
    xs, qm_s, k_s, va_s, u_s, res_s, lo_s,
    xc, xy, xf, part_keep, part_send, part_got, sum_keep, sum_send, sum_got, whole_own, whole_got,
    s_xc, r_xc, s_xy, r_xy, s_xf, r_xf, s_pc, r_pc, s_sy, r_sy, s_wc, r_wc,
):
    step = pl.program_id(0)
    core, y, ranks = place()

    rows = block_rows
    beside, across = {"tensor": ranks[1]}, {"tensor": ranks[2]}

    def to_core(b):
        return remote(x_any.at[rows(b)], xc.at[b], s_xc.at[b], r_xc.at[b], beside)

    def to_y(b):
        return remote(x_any.at[rows(b)], xy.at[b], s_xy.at[b], r_xy.at[b], across)

    def forward(b):
        return remote(xy.at[b], xf.at[b], s_xf.at[b], r_xf.at[b], beside)

    def part_to_core(b):
        return remote(part_send.at[b], part_got.at[b], s_pc.at[b], r_pc.at[b], beside)

    def sum_to_y(j):
        return remote(sum_send.at[j], sum_got.at[j], s_sy.at[j], r_sy.at[j], across)

    def whole_to_core(j):
        return remote(whole_own.at[j], whole_got.at[j], s_wc.at[j], r_wc.at[j], beside)

    @pl.when(step == 0)
    def _():
        greet((beside, across))
        for b in range(3):
            to_y(b).start()
            to_core(b).start()
        to_y(0).wait_recv()
        forward(0).start()
        hm_ref[...] = jnp.full(hm_ref.shape, NEG, F32)

    for b in range(3, NB):

        @pl.when(step == b - 2)
        def _():
            to_y(b).start()
            to_core(b).start()

    row_i = lax.broadcasted_iota(jnp.int32, (B, B), 0)
    col_i = lax.broadcasted_iota(jnp.int32, (B, B), 1)
    lanes = head_of_lane((B, SHARE))

    @pl.when(step < NB - 1)
    def _():
        to_y(step + 1).wait_recv()
        forward(step + 1).start()

    @pl.when(step < NB)
    def _():
        to_core(step).wait_recv()
        forward(step).wait_recv()
        blocks = (x_own[...], xc[step], xy[step], xf[step])
        for rank, block, ref in zip(ranks, blocks, (None, x1_ref, x2_ref, x3_ref)):
            xs[:, feature_block(rank)] = block.astype(F32)
            if ref is not None:
                ref[...] = block
        value = xs[...]

        @pl.when(lax.rem(step, 2) == y)
        def _():
            xm_ref[rows(step // 2), :] = value.astype(BF)

        mean, rstd = row_stats(value)
        n1 = ((value - mean) * rstd * vec[0:1, :] + vec[1:2, :]).astype(BF)
        q = (dot(n1, wq[...]) + bqv[0:1, :]).astype(BF)
        k = dot(n1, wk[...]).astype(BF)
        v = (dot(n1, wv[...]) + bqv[1:2, :]).astype(BF)
        qs = q * jnp.asarray(1.0 / math.sqrt(HD), BF)
        q_ref[...] = qs
        k_ref[...] = k
        v_ref[...] = v
        here = rows(step)
        k_s[here, :] = k
        for h in range(LH):
            qm_s[h] = jnp.where(lanes == h, qs, jnp.zeros_like(qs))
            va_s[h, here, :] = jnp.where(lanes == h, v, jnp.ones_like(v))
        lo_s[...] = jnp.broadcast_to(lo[...], (B, B))

    def attend(nb):
        start = pl.multiple_of((step + 1 - nb) * B, B)

        def head(h, carry):
            qm = qm_s[h]
            top = jnp.full((B, 128), NEG, F32)
            biggest = hm_ref[h]
            for r in range(nb):
                slot = SLOTS - nb + r
                base = pl.multiple_of(start + r * B, B)
                s = dot_nt(qm, k_s[pl.ds(base, B), :])
                inside = col_i + base >= lo_s[...]
                shut = pad[0:1, pl.ds(base, B)]
                if r == nb - 1:
                    s = jnp.where(row_i == col_i, s, s + shut)
                    s = jnp.where(inside & (col_i <= row_i), s, NEG)
                else:
                    s = jnp.where(inside, s + shut, NEG)
                biggest = jnp.maximum(biggest, jnp.max(s.reshape(B // 8, 8, B), axis=0))
                s = s + alibi[pl.ds(h, 1), slot * B : (slot + 1) * B]
                u_s[:, slot * B : (slot + 1) * B] = s
                top = jnp.maximum(top, jnp.maximum(s[:, :128], s[:, 128:]))
            hm_ref[h] = biggest
            top = jnp.max(top, axis=1, keepdims=True)
            for r in range(nb):
                slot = SLOTS - nb + r
                cols = slice(slot * B, (slot + 1) * B)
                p_ref[h, :, cols] = jnp.exp(u_s[:, cols] - top).astype(BF)
            res_s[h] = dot(p_ref[h, :, (SLOTS - nb) * B :], va_s[h, pl.ds(start, nb * B), :])
            return carry

        lax.fori_loop(0, LH, head, 0)

    for nb in range(1, SLOTS):
        pl.when(step == nb - 1)(functools.partial(attend, nb))
    pl.when((step >= SLOTS - 1) & (step < NB))(functools.partial(attend, SLOTS))

    @pl.when(step < NB)
    def _():
        ctx = res_s[0]
        total = res_s[LH - 1]
        for h in range(1, LH):
            ctx = jnp.where(lanes == h, res_s[h], ctx)
            total = jnp.where(lanes == h, res_s[h - 1], total)
        inv = 1.0 / pltpu.roll(total, SHARE - HD, 1)
        linv_ref[...] = inv
        ctx = (ctx * inv).astype(BF)
        ctx_ref[...] = ctx
        xs[...] = dot(ctx, wd[...])
        split_store(part_keep.at[step], part_send.at[step], xs, core)
        part_to_core(step).start()

    @pl.when((step >= 1) & (step <= NB))
    def _():
        b = step - 1
        j = b // 2
        part_to_core(b).wait_recv()
        total = part_keep[b].astype(F32) + part_got[b].astype(F32)

        @pl.when(lax.rem(b, 2) == y)
        def _():
            sum_keep[j] = total

        @pl.when(lax.rem(b, 2) != y)
        def _():
            sum_send[j] = total.astype(BF)
            sum_to_y(j).start()

    @pl.when((step >= TAIL) & (lax.rem(step + NB - TAIL, 2) == y))
    def _():
        j = (step - TAIL) // 2
        sum_to_y(j).wait_recv()
        total = (sum_keep[j] + sum_got[j].astype(F32)).astype(BF)
        whole_own[j] = total
        a_ref[rows(j), :] = total
        whole_to_core(j).start()

    @pl.when(step == NB + TAIL - 1)
    def _():
        for j in range(NB // 2):
            whole_to_core(j).wait_recv()
            b_ref[rows(j), :] = whole_got[j]
        for b in range(NB):
            to_core(b).wait_send()
            to_y(b).wait_send()
            forward(b).wait_send()
            part_to_core(b).wait_send()
        for j in range(NB // 2):
            sum_to_y(j).wait_send()
            whole_to_core(j).wait_send()


def attention_forward(x, vec, wq, wk, wv, bqv, wd, lo, pad, alibi):
    last = lambda s: jnp.minimum(s, NB - 1)
    row = lambda width: pl.BlockSpec((B, width), lambda s: (last(s), 0))
    whole = lambda shape: pl.BlockSpec(shape, lambda s: (0,) * len(shape))
    like = jax.ShapeDtypeStruct
    dma = lambda n: pltpu.SemaphoreType.DMA((n,))
    half = NB // 2
    return pl.pallas_call(
        fwd_kernel,
        grid=(NB + TAIL,),
        in_specs=[pl.BlockSpec(memory_space=pl.ANY), row(SHARE), whole((8, D))]
        + [whole((D, SHARE))] * 3
        + [whole((8, SHARE)), whole((SHARE, D)), row(1), whole((8, SEQ)), whole((8, STRIP))],
        out_specs=[pl.BlockSpec((LH, B, STRIP), lambda s: (0, last(s), 0))]
        + [row(SHARE)] * 5
        + [whole((OWN, D // 2))] * 2
        + [row(SHARE)] * 3
        + [whole((OWN, D)), whole((LH, 8, B))],
        scratch_shapes=[
            pltpu.VMEM((B, D), F32),
            pltpu.VMEM((LH, B, SHARE), BF),
            pltpu.VMEM((SEQ, SHARE), BF),
            pltpu.VMEM((LH, SEQ, SHARE), BF),
            pltpu.VMEM((B, STRIP), F32),
            pltpu.VMEM((LH, B, SHARE), F32),
            pltpu.VMEM((B, B), jnp.int32),
        ]
        + [pltpu.VMEM((NB, B, SHARE), BF)] * 3
        + [pltpu.VMEM((NB, B, D // 2), BF)] * 3
        + [pltpu.VMEM((half, B, D // 2), F32)]
        + [pltpu.VMEM((half, B, D // 2), BF)] * 4
        + [dma(NB)] * 8
        + [dma(half)] * 4,
        out_shape=[like((LH, SEQ, STRIP), BF)]
        + [like((SEQ, SHARE), BF)] * 3
        + [like((SEQ, SHARE), F32), like((SEQ, SHARE), BF)]
        + [like((OWN, D // 2), BF)] * 2
        + [like((SEQ, SHARE), BF)] * 3
        + [like((OWN, D), BF), like((LH, 8, B), F32)],
        compiler_params=remote_params(0),
        cost_estimate=pl.CostEstimate(
            flops=16 * 10**9, bytes_accessed=40 * 2**20, transcendentals=8 * 10**6
        ),
        name="attention_forward",
    )(x, x, vec, wq, wk, wv, bqv, wd, lo, pad, alibi)


def mlp_kernel(
    a_own, a_par, xm, d0, d1, d2, d3, vec, bup, wu0, wu1, wd0, wd1,
    mk_ref, ms_ref, gn_ref, h1_ref, gu_ref, su_ref, gd_ref, sd_ref, bs_ref, ru_ref,
    n2_s, n2t_s, dy_s, dyt_s, am_s, ag_s, act_s, gp_s, us_s, s_u, r_u,
    *, bit, chunk,
):
    i = pl.program_id(0)
    core, y, ranks = place()
    partner = {"dp": dp_partner(bit)}

    def send_up(n):
        return remote(us_s.at[n], ru_ref.at[n], s_u.at[n], r_u.at[n], partner)

    @pl.when(i == 0)
    def _():
        greet((partner,))

        def assemble(rb, carry):
            rows = block_rows(rb)
            h1_ref[rows, :] = xm[rows, :].astype(F32)
            for rank, d in zip(ranks, (d0, d1, d2, d3)):
                dy_s[rows, feature_block(rank)] = d[rows, :]
            for part, a in ((core, a_own), (1 - core, a_par)):
                for half in range(2):
                    cols = feature_block(2 * half + part)
                    h1_ref[rows, cols] += a[rows, half * SHARE : (half + 1) * SHARE].astype(F32)
            value = h1_ref[rows, :] + vec[2:3, :]
            h1_ref[rows, :] = value
            mean, rstd = row_stats(value)
            n2 = ((value - mean) * rstd * vec[3:4, :] + vec[4:5, :]).astype(BF)
            n2_s[rows, :] = n2
            n2t_s[:, rows] = n2.T
            dyt_s[:, rows] = dy_s[rows, :].T
            am_s[rows, :] = jnp.zeros((B, D), F32)
            ag_s[rows, :] = jnp.zeros((B, D), F32)
            return carry

        lax.fori_loop(0, OWN // B, assemble, 0)

    def tile(wu, wd, which):
        bias = bup[which : which + 1, pl.ds(pl.multiple_of(lax.rem(i, 2) * TILE, TILE), TILE)]
        scale = math.sqrt(2.0 / math.pi)

        def rows_of(rb, sums):
            rows = pl.ds(pl.multiple_of(rb * B, B), B)
            pre = dot(n2_s[rows, :], wu[...]) + bias
            back = dot_nt(dy_s[rows, :], wd[...])
            square = pre * pre
            th = jnp.tanh(scale * pre * (1.0 + 0.044715 * square))
            half = 0.5 * (1.0 + th)
            act = (pre * half).astype(BF)
            slope = half + 0.5 * pre * (1.0 - th * th) * (scale + (3 * 0.044715 * scale) * square)
            gp = (slope * back).astype(BF)
            act_s[rows, :] = act
            gp_s[rows, :] = gp
            am_s[rows, :] += dot(act, wd[...])
            ag_s[rows, :] += dot_nt(gp, wu[...])
            return sums + jnp.sum(gp.astype(F32), axis=0, keepdims=True)

        sums = lax.fori_loop(0, OWN // B, rows_of, jnp.zeros((1, TILE), F32))
        bs_ref[...] = jnp.broadcast_to(sums, bs_ref.shape)

        def grads(j, carry):
            to = pl.ds(pl.multiple_of(j * 128, 128), 128)
            mine, other = piece(j, bit, chunk)
            gu_ref[to, :] = dot(n2t_s[mine, :], gp_s[...]).astype(BF)
            gd_ref[to, :] = dot(dyt_s[mine, :], act_s[...]).astype(BF)
            us_s[i, to, :] = dot(n2t_s[other, :], gp_s[...]).astype(BF)
            sd_ref[to, :] = dot(dyt_s[other, :], act_s[...]).astype(BF)
            return carry

        lax.fori_loop(0, D // 256, grads, 0)

        @pl.when(i < 3)
        def _():
            send_up(i).start()

    pl.when(i < 2)(lambda: tile(wu0, wd0, 0))
    pl.when(i >= 2)(lambda: tile(wu1, wd1, 1))

    @pl.when(i == 3)
    def _():
        split_store(mk_ref, ms_ref, am_s, core)
        gn_ref[...] = ag_s[...].astype(BF)
        su_ref[...] = us_s[3]
        for n in range(3):
            send_up(n).wait()


def feed_forward(a_own, a_par, xm, ds, vec, bup, wu0, wd0, w_other, bit, chunk):
    whole = lambda shape: pl.BlockSpec(shape, lambda i: (0,) * len(shape))
    low = lambda i: jnp.minimum(i, 1)
    high = lambda i: jnp.maximum(i - 2, 0)
    like = jax.ShapeDtypeStruct
    tile = pl.BlockSpec((D // 2, TILE), lambda i: (0, i))
    return pl.pallas_call(
        functools.partial(mlp_kernel, bit=bit, chunk=chunk),
        grid=(4,),
        in_specs=[whole((OWN, D // 2))] * 2
        + [whole((OWN, D))]
        + [whole((OWN, SHARE))] * 4
        + [
            whole((8, D)),
            whole((8, UNITS)),
            pl.BlockSpec((D, TILE), lambda i: (0, low(i))),
            pl.BlockSpec((D, TILE), lambda i: (0, high(i))),
            pl.BlockSpec((TILE, D), lambda i: (low(i), 0)),
            pl.BlockSpec((TILE, D), lambda i: (high(i), 1)),
        ],
        out_specs=[whole((OWN, D // 2))] * 2
        + [whole((OWN, D))] * 2
        + [
            tile,
            whole((D // 2, TILE)),
            tile,
            tile,
            pl.BlockSpec((8, TILE), lambda i: (0, i)),
            pl.BlockSpec(memory_space=pl.ANY),
        ],
        scratch_shapes=[
            pltpu.VMEM((OWN, D), BF),
            pltpu.VMEM((D, OWN), BF),
            pltpu.VMEM((OWN, D), BF),
            pltpu.VMEM((D, OWN), BF),
            pltpu.VMEM((OWN, D), F32),
            pltpu.VMEM((OWN, D), F32),
            pltpu.VMEM((OWN, TILE), BF),
            pltpu.VMEM((OWN, TILE), BF),
            pltpu.VMEM((4, D // 2, TILE), BF),
            pltpu.SemaphoreType.DMA((3,)),
            pltpu.SemaphoreType.DMA((3,)),
        ],
        out_shape=[like((OWN, D // 2), BF)] * 2
        + [
            like((OWN, D), BF),
            like((OWN, D), F32),
            like((D // 2, 2 * UNITS), BF),
            like((D // 2, TILE), BF),
            like((D // 2, 2 * UNITS), BF),
            like((D // 2, 2 * UNITS), BF),
            like((8, 2 * UNITS), F32),
            like((3, D // 2, TILE), BF),
        ],
        compiler_params=remote_params(1),
        cost_estimate=pl.CostEstimate(
            flops=26 * 10**9, bytes_accessed=40 * 2**20, transcendentals=2 * 10**6
        ),
        name="feed_forward",
    )(a_own, a_par, xm, *ds, vec, bup, wu0, w_other, wd0, w_other)


LEAD = 2
FIRST = (0, 1, 1, 3, 4, 6, 8, 10)
PAIRS = ((0, 2), (1, 7), (3, 5), (4, 6))
FINAL = 3


def last_step(levels):
    return FIRST[-1] + 2 * (levels - 1) + 1


def bwd_kernel(
    x0, x1, x2, x3, x_late, h1, gn, gn_any, mk, ms_any, d0, d1, d2, d3, gu, gd, ru, su_any, sd_any,
    p_ref, q_ref, linv_ref, ctx_ref, k_ref, v_ref, vec, wq, wk, wv, wd,
    out_ref, tg_ref, wu_ref, wdn_ref, ka_ref, sa_ref, kb_ref, sb_ref, cs_ref, bs_ref, n1_ref,
    w_s, gh_s, gm_s, gt_s, qt_s, dl_s, ds_s, res_s, dkt_s, dvt_s, acc_s,
    gn_got, mr_got, o_send, o_got, gh_own, gh_y, gh_f,
    part_keep, part_send, part_got, sum_keep, sum_send, sum_got, ghx_s, st_keep, st_got, st_sum, st_all,
    gk, g1, y_send, y_got, *rest, order, bit_b, chunk,
):
    levels = len(order)
    stages = [rest[3 * n : 3 * n + 3] for n in range(levels - 1)]
    (
        s_gn, r_gn, s_mr, r_mr, s_o, r_o, s_gy, r_gy, s_gf, r_gf, s_pc, r_pc, s_sy, r_sy,
        s_tc, r_tc, s_ty, r_ty, s_g1, r_g1, s_yy, r_yy, l_g, l_w, *g_sems,
    ) = rest[3 * (levels - 1) :]
    step = pl.program_id(0)
    b = NB - 1 - (step - LEAD)
    core, y, ranks = place()
    beside, across = {"tensor": ranks[1]}, {"tensor": ranks[2]}
    partners = [{"dp": dp_partner(bit)} for bit in order]
    half = NB // 2
    last = last_step(levels)
    lanes = head_of_lane((B, SHARE))

    send_gn = lambda j: remote(gn_any.at[block_rows(j)], gn_got.at[j], s_gn.at[j], r_gn.at[j], beside)
    send_mr = lambda j: remote(ms_any.at[block_rows(j)], mr_got.at[j], s_mr.at[j], r_mr.at[j], beside)
    send_o = lambda j: remote(o_send.at[j], o_got.at[j], s_o.at[j], r_o.at[j], across)
    send_gy = lambda j, side: remote(
        gh_own.at[j, :, feature_block(2 * side + core)],
        gh_y.at[j, :, side * SHARE : (side + 1) * SHARE],
        s_gy.at[2 * j + side], r_gy.at[2 * j + side], across,
    )
    send_gf = lambda j: remote(gh_y.at[j], gh_f.at[j], s_gf.at[j], r_gf.at[j], beside)
    send_part = lambda n: remote(part_send.at[lax.rem(n, 4)], part_got.at[n], s_pc.at[n], r_pc.at[n], beside)
    send_sum = lambda n: remote(sum_send.at[n], sum_got.at[n], s_sy.at[n], r_sy.at[n], across)
    send_tc = lambda n: remote(st_keep.at[n], st_got.at[n], s_tc.at[n], r_tc.at[n], beside)
    send_ty = lambda n: remote(st_sum.at[n], st_all.at[n], s_ty.at[n], r_ty.at[n], across)

    def tile_of(p):
        up = p < 3 or p == 7
        n = (p if p < 3 else 3) if up else p - 3
        return slice(n * TILE, (n + 1) * TILE), up

    def send_first(p):
        cols, up = tile_of(p)
        src = su_any if up else sd_any.at[:, cols]
        return remote(src, g1.at[p - 3], s_g1.at[p - 3], r_g1.at[p - 3], partners[0])

    def load_keep(p):
        cols, up = tile_of(p)
        return pltpu.make_async_copy((gu if up else gd).at[:, cols], gk.at[p % 4], l_g.at[p % 4])

    def send_stage(p, n):
        _, send, got = stages[n - 1]
        return remote(
            send.at[p % 4], got.at[p], g_sems[2 * n - 2].at[p], g_sems[2 * n - 1].at[p], partners[n]
        )

    send_last = lambda n: remote(y_send.at[n], y_got.at[n], s_yy.at[n], r_yy.at[n], across)

    def split(p, n):
        if n == 1:
            load_keep(p).wait()
            keep = lambda rows: gk[p % 4, rows, :]
            if p < 3:
                got = lambda rows: ru[p, rows, :]
            else:
                send_first(p).wait_recv()
                got = lambda rows: g1[p - 3, rows, :]
        else:
            send_stage(p, n - 1).wait_recv()
            keep = lambda rows: stages[n - 2][0][p % 4, rows, :]
            got = lambda rows: stages[n - 2][2][p, rows, :]
        size = D >> n
        following = order[n]
        inner = chunk
        for other in order[n + 1 :]:
            inner *= 2 if other < following else 1
        mine = dp_bit(following)
        if p >= 4:
            send_stage(p - 4, n).wait_send()
        for group in range(size // (2 * inner)):
            to = slice(group * inner, (group + 1) * inner)
            for side, ref in ((mine, stages[n - 1][0]), (1 - mine, stages[n - 1][1])):
                rows = pl.ds(pl.multiple_of(group * 2 * inner + side * inner, inner), inner)
                ref[p % 4, to, :] = (keep(rows).astype(F32) + got(rows).astype(F32)).astype(BF)
        send_stage(p, n).start()

    def whole_tile(p):
        send_stage(p, levels - 1).wait_recv()
        keep, _, got = stages[levels - 2]
        total = keep[p % 4].astype(F32) + got[p].astype(F32)
        for n, (own, other) in enumerate(PAIRS):
            cols, up = tile_of(own)
            if p == own:
                (wu_ref if up else wdn_ref)[:, cols] = total
            if p == other:
                y_send[n] = total.astype(BF)
                send_last(n).start()

    def close(n):
        cols, up = tile_of(PAIRS[n][0])
        send_last(n).wait_recv()
        (wu_ref if up else wdn_ref)[:, cols] += y_got[n].astype(F32)

    @pl.when(step == 0)
    def _():
        greet([beside, across] + partners)
        for j in range(half - 1, -1, -1):
            send_gn(j).start()
            send_mr(j).start()
        for p in range(3, 8):
            send_first(p).start()
        for p in range(4):
            load_keep(p).start()
        cs_ref[...] = jnp.zeros(cs_ref.shape, F32)
        bs_ref[...] = jnp.zeros(bs_ref.shape, F32)
        n1_ref[...] = jnp.zeros(n1_ref.shape, F32)
        dkt_s[...] = jnp.zeros(dkt_s.shape, F32)
        dvt_s[...] = jnp.zeros(dvt_s.shape, F32)
        acc_s[...] = jnp.zeros(acc_s.shape, F32)

    @pl.when(step < half)
    def _():
        j = half - 1 - step
        send_gn(j).wait_recv()
        send_mr(j).wait_recv()
        for rank, d in zip(ranks, (d0, d1, d2, d3)):
            w_s[:, feature_block(rank)] = d[...].astype(F32)
        dy = w_s[...]
        value = h1[...]

        def out(side):
            part = pl.ds(pl.multiple_of(side * SHARE, SHARE), SHARE)
            cols = feature_block(2 * side + core)
            total = mk[:, part].astype(F32) + mr_got[j, :, part].astype(F32)
            return (h1[:, cols] + total + vec[5:6, cols]).astype(BF)

        out_ref[block_rows(2 * j + y), :] = out(y)
        o_send[j] = out(1 - y)
        mean, rstd = row_stats(value)
        xhat = (value - mean) * rstd
        grad = gn[...].astype(F32) + gn_got[j].astype(F32)
        scaled = grad * vec[3:4, :]
        first = jnp.sum(scaled, axis=1, keepdims=True) / D
        second = jnp.sum(scaled * xhat, axis=1, keepdims=True) / D
        gh = dy + rstd * (scaled - first - xhat * second)
        for n, columns in enumerate((grad * xhat, grad, gh, dy)):
            cs_ref[n : n + 1, :] += jnp.sum(columns, axis=0, keepdims=True)
        gh_own[j] = gh.astype(BF)
        send_gy(j, 0).start()
        send_gy(j, 1).start()
        send_o(j).start()

    @pl.when((step >= LEAD) & (step < LEAD + NB))
    def _():
        j = b // 2

        @pl.when(lax.rem(b, 2) == y)
        def _():
            gh_s[...] = gh_own[j]

        @pl.when(lax.rem(b, 2) != y)
        def _():
            send_gf(j).wait_recv()
            for part, ref in ((core, gh_y), (1 - core, gh_f)):
                for side in range(2):
                    gh_s[:, feature_block(2 * side + part)] = ref[j, :, side * SHARE : (side + 1) * SHARE]

        gc = dot_nt(gh_s[...], wd[...]).astype(BF).astype(F32)
        scaled = gc * linv_ref[...]
        gcs = scaled.astype(BF)
        product = scaled * ctx_ref[...].astype(F32)
        qt_s[...] = q_ref[...].T.reshape(LH, HD, B)
        gt_s[...] = gcs.T.reshape(LH, HD, B)
        for h in range(LH):
            gm_s[h] = jnp.where(lanes == h, gcs, jnp.zeros_like(gcs))
            delta = jnp.sum(jnp.where(lanes == h, product, 0.0), axis=1, keepdims=True)
            dl_s[h] = jnp.broadcast_to(delta, (B, 128))

    def attend(nb):
        start = pl.multiple_of((b + 1 - nb) * B, B)

        def head(h, carry):
            gm = gm_s[h]
            delta = jnp.concatenate([dl_s[h]] * 2, axis=1)
            for r in range(nb):
                slot = SLOTS - nb + r
                cols = slice(slot * B, (slot + 1) * B)
                dp = dot_nt(gm, v_ref[pl.ds(pl.multiple_of(start + r * B, B), B), :])
                ds_s[:, cols] = (p_ref[h, :, cols].astype(F32) * (dp - delta)).astype(BF)
            live = slice((SLOTS - nb) * B, STRIP)
            keys = pl.ds(start, nb * B)
            res_s[h] = dot(ds_s[:, live], k_ref[keys, :])
            dkt_s[h, :, keys] += dot(qt_s[h], ds_s[:, live])
            dvt_s[h, :, keys] += dot(gt_s[h], p_ref[h, :, live])
            return carry

        lax.fori_loop(0, LH, head, 0)

    pl.when((step >= LEAD) & (b >= SLOTS - 1))(functools.partial(attend, SLOTS))
    for nb in range(SLOTS - 1, 0, -1):
        pl.when(b == nb - 1)(functools.partial(attend, nb))

    @pl.when((step >= LEAD) & (step < LEAD + NB))
    def _():
        dq = res_s[0]
        for h in range(1, LH):
            dq = jnp.where(lanes == h, res_s[h], dq)
        dq = (dq * (1.0 / math.sqrt(HD))).astype(BF)
        here = block_rows(b)
        dk = dkt_s[:, :, here].reshape(SHARE, B).astype(BF).T
        dv = dvt_s[:, :, here].reshape(SHARE, B).astype(BF).T
        bs_ref[0:1, :] += jnp.sum(dq.astype(F32), axis=0, keepdims=True)
        bs_ref[1:2, :] += jnp.sum(dv.astype(F32), axis=0, keepdims=True)

        for rank, x in zip(ranks, (x0, x1, x2, x3)):
            w_s[:, feature_block(rank)] = x[...].astype(F32)
        value = w_s[...]
        mean, rstd = row_stats(value)
        xhat = (value - mean) * rstd
        n1t = (xhat * vec[0:1, :] + vec[1:2, :]).astype(BF).T
        acc_s[:, 0:SHARE] += dot(n1t, dq)
        acc_s[:, SHARE : 2 * SHARE] += dot(n1t, dk)
        acc_s[:, 2 * SHARE : 3 * SHARE] += dot(n1t, dv)
        acc_s[:, 3 * SHARE :] += dot(gh_s[...].T, ctx_ref[...])

        grad = dot_nt(dq, wq[...]) + dot_nt(dk, wk[...]) + dot_nt(dv, wv[...])
        scaled = grad * vec[0:1, :]
        first = jnp.sum(scaled, axis=1, keepdims=True)
        second = jnp.sum(scaled * xhat, axis=1, keepdims=True)
        column = lax.broadcasted_iota(jnp.int32, (B, 128), 1)
        packed = jnp.where(
            column == 0, first, jnp.where(column == 1, second, jnp.where(column == 2, mean, rstd))
        )
        st_keep[b] = packed.T[0:8, :]
        send_tc(b).start()
        w_s[...] = grad

        @pl.when(step >= LEAD + 4)
        def _():
            send_part(b + 4).wait_send()

        for n, side in enumerate((y, 1 - y)):
            cols = slice(n * SHARE, (n + 1) * SHARE)
            part_keep[lax.rem(b, 2), :, cols] = w_s[:, feature_block(2 * side + core)].astype(BF)
            part_send[lax.rem(b, 4), :, cols] = w_s[:, feature_block(2 * side + 1 - core)].astype(BF)
        send_part(b).start()
        ghx_s[lax.rem(b, 4)] = gh_s[:, feature_block(ranks[0])]

    weights = ((0, ka_ref), (1, sa_ref), (2, kb_ref), (3, sb_ref))

    def store_weights(n, ref, part):
        cols = slice(part * 2 * SHARE, (part + 1) * 2 * SHARE)
        return pltpu.make_async_copy(gn_got.at[n, :, cols], ref.at[block_rows(part)], l_w.at[2 * n + part])

    @pl.when(step == LEAD + NB - 1)
    def _():
        for j in range(D // 256):
            to = slice(j % 2 * 128, (j % 2 + 1) * 128)
            into = slice(j // 2 * 2 * SHARE, (j // 2 + 1) * 2 * SHARE)
            for n, (bit, cols) in enumerate(
                ((order[0], slice(0, 2 * SHARE)), (bit_b, slice(2 * SHARE, 4 * SHARE)))
            ):
                for side, rows in enumerate(piece(j, bit, chunk)):
                    gn_got[2 * n + side, to, into] = acc_s[rows, cols].astype(BF)
        for n, ref in weights:
            for part in range(2):
                store_weights(n, ref, part).start()

    @pl.when((step >= LEAD + 1) & (step < LEAD + 1 + NB))
    def _():
        n = b + 1
        send_part(n).wait_recv()
        send_tc(n).wait_recv()
        keep = part_keep[lax.rem(n, 2)].astype(F32)
        sum_keep[lax.rem(n, 4)] = keep[:, :SHARE] + part_got[n, :, :SHARE].astype(F32)
        sum_send[n] = (keep[:, SHARE:] + part_got[n, :, SHARE:].astype(F32)).astype(BF)
        st_sum[n] = st_keep[n] + st_got[n]
        send_sum(n).start()
        send_ty(n).start()

    @pl.when((step >= LEAD + FINAL) & (step < LEAD + FINAL + NB))
    def _():
        n = b + FINAL
        send_sum(n).wait_recv()
        send_ty(n).wait_recv()
        grad = sum_keep[lax.rem(n, 4)] + sum_got[n].astype(F32)
        row = lax.broadcasted_iota(jnp.int32, (8, B), 0)
        stats = jnp.where(row < 2, st_sum[n] + st_all[n], st_keep[n])
        stats = jnp.concatenate([stats] * 16, axis=0).T
        xhat = (x_late[...].astype(F32) - stats[:, 2:3]) * stats[:, 3:4]
        scaled = grad * vec[0:1, feature_block(ranks[0])]
        inner = scaled - stats[:, 0:1] / D - xhat * (stats[:, 1:2] / D)
        tg_ref[...] = ghx_s[lax.rem(n, 4)].astype(F32) + stats[:, 3:4] * inner
        n1_ref[0:1, :] += jnp.sum(grad * xhat, axis=0, keepdims=True)
        n1_ref[1:2, :] += jnp.sum(grad, axis=0, keepdims=True)

    for j in range(half - 1, -1, -1):

        @pl.when(step == half - j)
        def _():
            send_gy(j, 0).wait_recv()
            send_gy(j, 1).wait_recv()
            send_gf(j).start()

    for p in range(8):
        for n in range(1, levels):
            pl.when(step == FIRST[p] + 2 * (n - 1))(functools.partial(split, p, n))
        if p >= 4:
            pl.when(step == FIRST[p - 4] + 1)(lambda p=p: load_keep(p).start())
        pl.when(step == FIRST[p] + 2 * (levels - 1))(functools.partial(whole_tile, p))
    for n, pair in enumerate(PAIRS):
        pl.when(step == max(FIRST[p] for p in pair) + 2 * (levels - 1) + 1)(functools.partial(close, n))

    @pl.when(step == last)
    def _():
        for j in range(half):
            send_o(j).wait_recv()
            out_ref[block_rows(2 * j + 1 - y), :] = o_got[j]
            for copy in (send_gn, send_mr, send_o, send_gf, send_last, send_part):
                copy(j).wait_send()
            for side in range(2):
                send_gy(j, side).wait_send()
            for level in range(1, levels):
                send_stage(4 + j, level).wait_send()
        for n in range(NB):
            for copy in (send_sum, send_tc, send_ty):
                copy(n).wait_send()
        for p in range(3, 8):
            send_first(p).wait_send()
        for n, ref in weights:
            for part in range(2):
                store_weights(n, ref, part).wait()


def attention_backward(
    xs, h1, gn, mk, ms, ds, gu, gd, ru, su, sd, p, q, linv, ctx, k, v, vec, wq, wk, wv, wd,
    order, bit_b, chunk,
):
    levels = len(order)
    half = NB // 2
    steps = max(last_step(levels), LEAD + FINAL + NB - 1) + 1
    assert steps == last_step(levels) + 1
    block = lambda s: jnp.clip(NB - 1 + LEAD - s, 0, NB - 1)
    late = lambda s: jnp.clip(NB - 1 + LEAD + FINAL - s, 0, NB - 1)
    row = lambda width: pl.BlockSpec((B, width), lambda s: (block(s), 0))
    own = lambda width: pl.BlockSpec((B, width), lambda s: (jnp.maximum(half - 1 - s, 0), 0))
    once = pl.Buffered(1)
    whole = lambda *shape: pl.BlockSpec(shape, lambda s: (0,) * len(shape), pipeline_mode=once)
    anywhere = pl.BlockSpec(memory_space=pl.ANY)
    like = jax.ShapeDtypeStruct
    vmem = lambda *shape, dtype=BF: pltpu.VMEM(shape, dtype)
    dma = lambda n: pltpu.SemaphoreType.DMA((n,))
    final_late = pl.BlockSpec((B, SHARE), lambda s: (late(s), 0))
    return pl.pallas_call(
        functools.partial(bwd_kernel, order=order, bit_b=bit_b, chunk=chunk),
        grid=(steps,),
        in_specs=[row(SHARE)] * 4
        + [final_late, own(D), own(D), anywhere, own(D // 2), anywhere]
        + [own(SHARE)] * 4
        + [anywhere] * 2
        + [whole(3, D // 2, TILE), anywhere, anywhere]
        + [pl.BlockSpec((LH, B, STRIP), lambda s: (0, block(s), 0))]
        + [row(SHARE)] * 3
        + [whole(SEQ, SHARE)] * 2
        + [whole(8, D)]
        + [whole(D, SHARE)] * 3
        + [whole(SHARE, D)],
        out_specs=[whole(SEQ, SHARE), final_late]
        + [whole(chunk, UNITS)] * 2
        + [anywhere] * 4
        + [whole(8, D), whole(8, SHARE), whole(8, SHARE)],
        scratch_shapes=[
            vmem(B, D, dtype=F32),
            vmem(B, D),
            vmem(LH, B, SHARE),
            vmem(LH, HD, B),
            vmem(LH, HD, B),
            vmem(LH, B, 128, dtype=F32),
            vmem(B, STRIP),
            vmem(LH, B, SHARE, dtype=F32),
            vmem(LH, HD, SEQ, dtype=F32),
            vmem(LH, HD, SEQ, dtype=F32),
            vmem(D, 4 * SHARE, dtype=F32),
            vmem(half, B, D),
            vmem(half, B, D // 2),
            vmem(half, B, SHARE),
            vmem(half, B, SHARE),
            vmem(half, B, D),
            vmem(half, B, D // 2),
            vmem(half, B, D // 2),
            vmem(2, B, D // 2),
            vmem(4, B, D // 2),
            vmem(NB, B, D // 2),
            vmem(4, B, SHARE, dtype=F32),
            vmem(NB, B, SHARE),
            vmem(NB, B, SHARE),
            vmem(4, B, SHARE),
            vmem(NB, 8, B, dtype=F32),
            vmem(NB, 8, B, dtype=F32),
            vmem(NB, 8, B, dtype=F32),
            vmem(NB, 8, B, dtype=F32),
            vmem(4, D // 2, TILE),
            vmem(5, D // 2, TILE),
            vmem(half, chunk, TILE),
            vmem(half, chunk, TILE),
        ]
        + [vmem(slots, D >> (n + 1), TILE) for n in range(1, levels) for slots in (4, 4, 8)]
        + [dma(half)] * 6
        + [dma(NB)] * 2
        + [dma(half)] * 2
        + [dma(NB)] * 8
        + [dma(5)] * 2
        + [dma(half)] * 3
        + [dma(8)]
        + [dma(8)] * (2 * (levels - 1)),
        out_shape=[like((SEQ, SHARE), BF), like((SEQ, SHARE), F32)]
        + [like((chunk, UNITS), F32)] * 2
        + [like((D // 2, 2 * SHARE), BF)] * 4
        + [like((8, D), F32), like((8, SHARE), F32), like((8, SHARE), F32)],
        compiler_params=remote_params(2),
        cost_estimate=pl.CostEstimate(
            flops=30 * 10**9, bytes_accessed=50 * 2**20, transcendentals=0
        ),
        name="backward",
    )(
        *xs, xs[0], h1, gn, gn, mk, ms, *ds, gu, gd, ru, su, sd, p, q, linv, ctx, k, v, vec, wq, wk, wv, wd
    )


def swap(value, axis, bit):
    size = lax.axis_size(axis)
    return lax.ppermute(value, axis, [(i, i ^ bit) for i in range(size)])


def dp_bits():
    bits, bit = [], 1
    while bit < lax.axis_size("dp"):
        bits.append(bit)
        bit *= 2
    return bits


def dp_total(value):
    for bit in dp_bits():
        value = value + swap(value, "dp", bit)
    return value


def pick(value, axis, index):
    return lax.dynamic_index_in_dim(value, index, axis, keepdims=False)


def sum_kernel(bit, km, rm, ko, ro, keep_ref, send_ref):
    for a, b, ref in ((km, rm, keep_ref), (ko, ro, send_ref)):
        ref[...] = (a[...].astype(F32) + b[...].astype(F32)).astype(ref.dtype)


def sum_and_split(bit, keep, other, inner, after=()):
    rows, cols = keep.shape
    step = min(inner, 128)
    per = inner // step
    block = lambda side: pl.BlockSpec(
        (step, cols),
        lambda i, bit: (i // per * 2 * per + (bit[0] if side else 1 - bit[0]) * per + i % per, 0),
    )
    out = pl.BlockSpec((step, cols), lambda i, bit: (i, 0))
    return pl.pallas_call(
        ordered(sum_kernel, len(after)),
        grid_spec=pltpu.PrefetchScalarGridSpec(
            num_scalar_prefetch=1,
            grid=(rows // 2 // step,),
            in_specs=waits(after) + [block(True), block(True), block(False), block(False)],
            out_specs=[out, out],
        ),
        out_shape=[jax.ShapeDtypeStruct((rows // 2, cols), BF)] * 2,
        compiler_params=params(),
        cost_estimate=pl.CostEstimate(flops=rows * cols, bytes_accessed=6 * rows * cols, transcendentals=0),
        name="sum_and_split",
    )(bit, *after, keep, other, keep, other)


def dp_scatter(keep, send, order, after=()):
    rank = lax.axis_index("dp")
    chunk = D // lax.axis_size("dp")
    for n, bit in enumerate(order):
        other = swap(send, "dp", bit)
        if n == len(order) - 1:
            yield keep.astype(F32) + other.astype(F32)
            return
        following = order[n + 1]
        inner = chunk
        for b in order[n + 2 :]:
            inner *= 2 if b < following else 1
        wait = yield send
        mine = ((rank // following) % 2)[None]
        keep, send = sum_and_split(mine, keep, other, inner, wait or ())


def finish(steps, after=()):
    try:
        while True:
            value = steps.send(after)
    except StopIteration:
        return value


def shards(
    tokens,
    out_grad,
    segments,
    padding,
    norm1_gain,
    norm1_bias,
    w_query,
    b_query,
    w_key,
    w_value,
    b_value,
    w_dense,
    dense_bias,
    norm2_gain,
    norm2_bias,
    w_up,
    b_up,
    w_down,
    down_bias,
):
    t = lax.axis_index("tensor")
    rank = lax.axis_index("dp")
    size = lax.axis_size("dp")
    core, y = t % 2, t // 2
    core_swap = lambda value: swap(value, "tensor", 1)
    y_swap = lambda value: swap(value, "tensor", 2)
    rows8 = lambda value: jnp.pad(value, ((0, 8 - value.shape[0]), (0, 0)))

    vectors = jnp.stack([norm1_gain, norm1_bias, dense_bias, norm2_gain, norm2_bias, down_bias])
    vec = lax.dynamic_update_slice(jnp.zeros((6, D), BF), vectors, (0, t * SHARE))
    vec = vec + core_swap(vec)
    vec = rows8((vec + y_swap(vec)).astype(F32))

    part = D // size
    cut = lambda w: lax.dynamic_slice_in_dim(w, rank * part, part, 0)
    w_part = y_swap(jnp.concatenate([cut(w_up), cut(w_down)], axis=1))
    w_other = lax.all_gather(w_part, "dp", axis=0, tiled=True)
    b_up_pair = jnp.stack([b_up, y_swap(b_up)]).astype(F32)

    seg = segments.reshape(SEQ)
    index = jnp.arange(SEQ, dtype=jnp.int32)
    first = jnp.zeros((SEQ,), jnp.int32)
    for value in range(1, 4):
        first = jnp.where(seg == value, jnp.sum((seg < value).astype(jnp.int32)), first)
    lowest = jnp.maximum(first, index - (WIN - 1))
    pad_row = rows8(jnp.where(padding.reshape(1, SEQ) == 1, 0.0, NEG).astype(F32))
    heads = t * LH + jnp.arange(LH)
    slopes = jnp.exp2(-8.0 * (heads.astype(F32) + 1.0) / HEADS)
    alibi = rows8(slopes[:, None] * (jnp.arange(STRIP) - (STRIP - 1)).astype(F32)[None, :])

    by_y = lambda value, which: pick(value.reshape(NB // 2, 2, B, value.shape[-1]), 1, which).reshape(
        OWN, value.shape[-1]
    )
    d_own = by_y(out_grad, y)
    d_send = by_y(out_grad, 1 - y)

    p, q, k, v, linv, ctx, a_own, a_par, x1, x2, x3, xm, hm = attention_forward(
        tokens, vec, w_query, w_key, w_value,
        rows8(jnp.stack([b_query, b_value]).astype(F32)), w_dense,
        lowest.reshape(SEQ, 1), pad_row, alibi,
    )
    xs = [tokens, x1, x2, x3]

    d_y = y_swap(d_send)
    ds = [d_own, core_swap(d_own), d_y, core_swap(d_y)]

    bits = dp_bits()
    order_a = bits if size == 8 else bits[::-1]
    order_b = [2, 4, 1] if size == 8 else [bits[-2], bits[-1], *bits[:-2][::-1]]
    mk, ms, gn, h1, gu, su, gd, sd, bs, ru = feed_forward(
        a_own, a_par, xm, ds, vec, rows8(b_up_pair), w_up, w_down, w_other, order_a[0], part
    )
    output, tokens_grad, w_up_grad, w_down_grad, ka, sa, kb, sb, cs, qv, n1s = attention_backward(
        xs, h1, gn, mk, ms, ds, gu, gd, ru, su, sd, p, q, linv, ctx, k, v, vec,
        w_query, w_key, w_value, w_dense, order_a, order_b[0], part,
    )
    w_down_grad = w_down_grad.T

    steps_a = dp_scatter(ka, sa, order_a)
    steps_b = dp_scatter(kb, sb, order_b)
    next(steps_a), next(steps_b)
    g_qk = finish(steps_a, ())
    g_vd = finish(steps_b, ())

    cs4 = pick(cs[0:4].reshape(4, 2, 2, SHARE), 2, core)
    early = jnp.concatenate([pick(cs4, 1, y).reshape(-1), bs[0, :UNITS]])
    apart = jnp.concatenate([pick(cs4, 1, 1 - y).reshape(-1), bs[0, UNITS:]])
    early = early + y_swap(apart)
    late = jnp.concatenate([n1s[0], n1s[1], qv[0], qv[1]])
    packed = jnp.concatenate([early, late, jnp.pad(jnp.max(hm, axis=(1, 2)), (0, 124))])
    summed = lax.broadcasted_iota(jnp.int32, packed.shape, 0) < packed.shape[0] - 128
    for bit in bits:
        other = swap(packed, "dp", bit)
        packed = jnp.where(summed, packed + other, jnp.maximum(packed, other))
    early, late, head_max = jnp.split(packed, (8 * SHARE, 12 * SHARE))
    head_max = head_max[:LH]
    of = lambda value, n: value[n * SHARE : (n + 1) * SHARE]

    column_scale = jnp.repeat(jnp.sqrt(TAU / jnp.maximum(head_max, TAU)), HD)
    return (
        output,
        tokens_grad,
        of(late, 0),
        of(late, 1),
        g_qk[:, :SHARE],
        of(late, 2),
        g_qk[:, SHARE:],
        g_vd[:, :SHARE],
        of(late, 3),
        g_vd[:, SHARE:].T,
        of(early, 2),
        of(early, 0),
        of(early, 1),
        w_up_grad,
        early[4 * SHARE :],
        w_down_grad,
        of(early, 3),
        head_max,
        w_query.astype(F32) * column_scale,
        b_query.astype(F32) * column_scale,
        w_key.astype(F32) * column_scale,
    )


def solution(mesh):
    in_specs = (
        P("dp", "tensor"),
        P("dp", "tensor"),
        P("dp", None),
        P("dp", None),
        P("tensor"),
        P("tensor"),
        P(None, "tensor"),
        P("tensor"),
        P(None, "tensor"),
        P(None, "tensor"),
        P("tensor"),
        P("tensor", None),
        P("tensor"),
        P("tensor"),
        P("tensor"),
        P(None, "tensor"),
        P("tensor"),
        P("tensor", None),
        P("tensor"),
    )
    out_specs = (
        P("dp", "tensor"),
        P("dp", "tensor"),
        P("tensor"),
        P("tensor"),
        P("dp", "tensor"),
        P("tensor"),
        P("dp", "tensor"),
        P("dp", "tensor"),
        P("tensor"),
        P("tensor", "dp"),
        P("tensor"),
        P("tensor"),
        P("tensor"),
        P("dp", "tensor"),
        P("tensor"),
        P("tensor", "dp"),
        P("tensor"),
        P("tensor"),
        P(None, "tensor"),
        P("tensor"),
        P(None, "tensor"),
    )
    return jax.shard_map(shards, mesh=mesh, in_specs=in_specs, out_specs=out_specs, check_vma=False)
```

```python
import functools
import math

import jax
import jax.numpy as jnp
from jax import lax
from jax.experimental import pallas as pl
from jax.experimental.pallas import tpu as pltpu
from jax.sharding import PartitionSpec as P

HEADS = 16
HD = 64
WIN = 1024
D = 1024
FF = 4096
SEQ = 2048
B = 256
NB = SEQ // B
SLOTS = WIN // B + 1
STRIP = SLOTS * B
LH = 4
SHARE = LH * HD
UNITS = FF // 4
TILE = 512
OWN = SEQ // 2

EPS = 1e-05
TAU = 2.0
NEG = -1e30
F32 = jnp.float32
BF = jnp.bfloat16
VMEM_LIMIT = 62 * 2**20


def dot(a, b):
    return jnp.dot(a, b, preferred_element_type=F32)


def dot_nt(a, b):
    return lax.dot_general(a, b, (((1,), (1,)), ((), ())), preferred_element_type=F32)


def params():
    return pltpu.CompilerParams(
        dimension_semantics=("arbitrary",), vmem_limit_bytes=VMEM_LIMIT
    )


def feature_block(rank):
    return pl.ds(pl.multiple_of(rank * SHARE, SHARE), SHARE)


def head_of_lane(shape):
    return lax.broadcasted_iota(jnp.int32, shape, 1) // HD


def ordered(kernel, count):
    return lambda ids, *refs: kernel(ids, *refs[count:])


def waits(after):
    return [pl.BlockSpec(memory_space=pl.ANY)] * len(after)


def row_stats(rows):
    mean = jnp.sum(rows, axis=1, keepdims=True) / D
    square = jnp.sum(rows * rows, axis=1, keepdims=True) / D
    return mean, lax.rsqrt(square - mean * mean + EPS)


def piece(j, bit, chunk):
    inner = bit * chunk
    mine = dp_bit(bit)
    base = (j * 128) // inner * (2 * inner) + (j * 128) % inner
    return [
        pl.ds(pl.multiple_of(base + side * inner, 128), 128) for side in (mine, 1 - mine)
    ]


def dp_bit(bit):
    return lax.rem(lax.div(lax.axis_index("dp"), bit), 2)


def dp_partner(bit):
    return lax.axis_index("dp") + bit - 2 * bit * dp_bit(bit)


def place():
    t = lax.axis_index("tensor")
    core, y = lax.rem(t, 2), lax.div(t, 2)
    return core, y, (t, 2 * y + 1 - core, 2 * (1 - y) + core, 2 * (1 - y) + 1 - core)


def remote(src, dst, send, got, where):
    return pltpu.make_async_remote_copy(
        src_ref=src, dst_ref=dst, send_sem=send, recv_sem=got,
        device_id=where, device_id_type=pl.DeviceIdType.MESH,
    )


def greet(places):
    barrier = pltpu.get_barrier_semaphore()
    for where in places:
        pl.semaphore_signal(
            barrier, inc=1, device_id=where, device_id_type=pl.DeviceIdType.MESH
        )
    pl.semaphore_wait(barrier, len(places))


def block_rows(b):
    return pl.ds(pl.multiple_of(b * B, B), B)


def remote_params(collective_id):
    return pltpu.CompilerParams(
        dimension_semantics=("arbitrary",),
        vmem_limit_bytes=VMEM_LIMIT,
        collective_id=collective_id,
        has_side_effects=True,
    )


def split_store(keep_ref, send_ref, value_ref, core):
    for half in range(2):
        cols = slice(half * SHARE, (half + 1) * SHARE)
        keep_ref[:, cols] = value_ref[:, feature_block(2 * half + core)].astype(keep_ref.dtype)
        send_ref[:, cols] = value_ref[:, feature_block(2 * half + 1 - core)].astype(
            send_ref.dtype
        )


TAIL = 3


def fwd_kernel(
    x_any, g_any, x_own, own_vec, wq, wk, wv, bqv, wd, lo, pad, alibi,
    p_ref, q_ref, k_ref, v_ref, linv_ref, ctx_ref, a_ref, b_ref, x1_ref, x2_ref, x3_ref, xm_ref, hm_ref, vec, bup_ref, dy_any,
    xs, qm_s, k_s, va_s, u_s, res_s, lo_s,
    xc, xy, xf, part_keep, part_send, part_got, sum_keep, sum_send, sum_got, whole_own, whole_got,
    v_all,
    s_xc, r_xc, s_xy, r_xy, s_xf, r_xf, s_pc, r_pc, s_sy, r_sy, s_wc, r_wc,
    s_v, r_v, l_d, s_dc, r_dc, s_dy, r_dy, s_df, r_df,
):
    step = pl.program_id(0)
    core, y, ranks = place()

    rows = block_rows
    beside, across = {"tensor": ranks[1]}, {"tensor": ranks[2]}

    def to_core(b):
        return remote(x_any.at[rows(b)], xc.at[b], s_xc.at[b], r_xc.at[b], beside)

    def to_y(b):
        return remote(x_any.at[rows(b)], xy.at[b], s_xy.at[b], r_xy.at[b], across)

    def forward(b):
        return remote(xy.at[b], xf.at[b], s_xf.at[b], r_xf.at[b], beside)

    def part_to_core(b):
        return remote(part_send.at[b], part_got.at[b], s_pc.at[b], r_pc.at[b], beside)

    def sum_to_y(j):
        return remote(sum_send.at[j], sum_got.at[j], s_sy.at[j], r_sy.at[j], across)

    def whole_to_core(j):
        return remote(whole_own.at[j], whole_got.at[j], s_wc.at[j], r_wc.at[j], beside)

    def vectors(r):
        return remote(v_all.at[0], v_all.at[r], s_v.at[r - 1], r_v.at[r - 1], {"tensor": ranks[r]})

    mine = feature_block(ranks[0])

    def dy_own(j):
        return pltpu.make_async_copy(g_any.at[rows(2 * j + y)], dy_any.at[rows(j), mine], l_d.at[j])

    def dy_core(j):
        return remote(g_any.at[rows(2 * j + y)], dy_any.at[rows(j), mine], s_dc.at[j], r_dc.at[j], beside)

    def dy_y(j):
        return remote(g_any.at[rows(2 * j + 1 - y)], dy_any.at[rows(j), mine], s_dy.at[j], r_dy.at[j], across)

    def dy_forward(j):
        block = dy_any.at[rows(j), feature_block(ranks[2])]
        return remote(block, block, s_df.at[j], r_df.at[j], beside)

    @pl.when(step == 0)
    def _():
        v_all[0] = own_vec[...]
        greet((beside, across, {"tensor": ranks[3]}))
        for r in range(1, 4):
            vectors(r).start()
        for b in range(3):
            to_y(b).start()
            to_core(b).start()
        for r in range(1, 4):
            vectors(r).wait_recv()
        for r in range(4):
            vec[:, feature_block(ranks[r])] = v_all[r, 0:8, :]
        bup_ref[...] = jnp.zeros(bup_ref.shape, F32)
        for n, r in enumerate((0, 2)):
            for part in range(4):
                bup_ref[n : n + 1, part * SHARE : (part + 1) * SHARE] = v_all[r, 8 + part : 9 + part, :]
        to_y(0).wait_recv()
        forward(0).start()
        hm_ref[...] = jnp.full(hm_ref.shape, NEG, F32)

    for b in range(3, NB):

        @pl.when(step == b - 2)
        def _():
            to_y(b).start()
            to_core(b).start()

    row_i = lax.broadcasted_iota(jnp.int32, (B, B), 0)
    col_i = lax.broadcasted_iota(jnp.int32, (B, B), 1)
    lanes = head_of_lane((B, SHARE))

    for j in range(NB // 2):

        @pl.when(step == j + 4)
        def _():
            dy_own(j).start()
            dy_core(j).start()
            dy_y(j).start()

        @pl.when(step == j + 7)
        def _():
            dy_y(j).wait_recv()
            dy_forward(j).start()

    @pl.when(step < NB - 1)
    def _():
        to_y(step + 1).wait_recv()
        forward(step + 1).start()

    @pl.when(step < NB)
    def _():
        to_core(step).wait_recv()
        forward(step).wait_recv()
        blocks = (x_own[...], xc[step], xy[step], xf[step])
        for rank, block, ref in zip(ranks, blocks, (None, x1_ref, x2_ref, x3_ref)):
            xs[:, feature_block(rank)] = block.astype(F32)
            if ref is not None:
                ref[...] = block
        value = xs[...]

        @pl.when(lax.rem(step, 2) == y)
        def _():
            xm_ref[rows(step // 2), :] = value.astype(BF)

        mean, rstd = row_stats(value)
        n1 = ((value - mean) * rstd * vec[0:1, :] + vec[1:2, :]).astype(BF)
        q = (dot(n1, wq[...]) + bqv[0:1, :]).astype(BF)
        k = dot(n1, wk[...]).astype(BF)
        v = (dot(n1, wv[...]) + bqv[1:2, :]).astype(BF)
        qs = q * jnp.asarray(1.0 / math.sqrt(HD), BF)
        q_ref[...] = qs
        k_ref[...] = k
        v_ref[...] = v
        here = rows(step)
        k_s[here, :] = k
        for h in range(LH):
            qm_s[h] = jnp.where(lanes == h, qs, jnp.zeros_like(qs))
            va_s[h, here, :] = jnp.where(lanes == h, v, jnp.ones_like(v))
        lo_s[...] = jnp.broadcast_to(lo[...], (B, B))

    def attend(nb):
        start = pl.multiple_of((step + 1 - nb) * B, B)

        def head(h, carry):
            qm = qm_s[h]
            top = jnp.full((B, 128), NEG, F32)
            biggest = hm_ref[h]
            for r in range(nb):
                slot = SLOTS - nb + r
                base = pl.multiple_of(start + r * B, B)
                s = dot_nt(qm, k_s[pl.ds(base, B), :])
                inside = col_i + base >= lo_s[...]
                shut = pad[0:1, pl.ds(base, B)]
                if r == nb - 1:
                    s = jnp.where(row_i == col_i, s, s + shut)
                    s = jnp.where(inside & (col_i <= row_i), s, NEG)
                else:
                    s = jnp.where(inside, s + shut, NEG)
                biggest = jnp.maximum(biggest, jnp.max(s.reshape(B // 8, 8, B), axis=0))
                s = s + alibi[pl.ds(h, 1), slot * B : (slot + 1) * B]
                u_s[:, slot * B : (slot + 1) * B] = s
                top = jnp.maximum(top, jnp.maximum(s[:, :128], s[:, 128:]))
            hm_ref[h] = biggest
            top = jnp.max(top, axis=1, keepdims=True)
            for r in range(nb):
                slot = SLOTS - nb + r
                cols = slice(slot * B, (slot + 1) * B)
                p_ref[h, :, cols] = jnp.exp(u_s[:, cols] - top).astype(BF)
            res_s[h] = dot(p_ref[h, :, (SLOTS - nb) * B :], va_s[h, pl.ds(start, nb * B), :])
            return carry

        lax.fori_loop(0, LH, head, 0)

    for nb in range(1, SLOTS):
        pl.when(step == nb - 1)(functools.partial(attend, nb))
    pl.when((step >= SLOTS - 1) & (step < NB))(functools.partial(attend, SLOTS))

    @pl.when(step < NB)
    def _():
        ctx = res_s[0]
        total = res_s[LH - 1]
        for h in range(1, LH):
            ctx = jnp.where(lanes == h, res_s[h], ctx)
            total = jnp.where(lanes == h, res_s[h - 1], total)
        inv = 1.0 / pltpu.roll(total, SHARE - HD, 1)
        linv_ref[...] = inv
        ctx = (ctx * inv).astype(BF)
        ctx_ref[...] = ctx
        xs[...] = dot(ctx, wd[...])
        split_store(part_keep.at[step], part_send.at[step], xs, core)
        part_to_core(step).start()

    @pl.when((step >= 1) & (step <= NB))
    def _():
        b = step - 1
        j = b // 2
        part_to_core(b).wait_recv()
        total = part_keep[b].astype(F32) + part_got[b].astype(F32)

        @pl.when(lax.rem(b, 2) == y)
        def _():
            sum_keep[j] = total

        @pl.when(lax.rem(b, 2) != y)
        def _():
            sum_send[j] = total.astype(BF)
            sum_to_y(j).start()

    @pl.when((step >= TAIL) & (lax.rem(step + NB - TAIL, 2) == y))
    def _():
        j = (step - TAIL) // 2
        sum_to_y(j).wait_recv()
        total = (sum_keep[j] + sum_got[j].astype(F32)).astype(BF)
        whole_own[j] = total
        a_ref[rows(j), :] = total
        whole_to_core(j).start()

    @pl.when(step == NB + TAIL - 1)
    def _():
        for j in range(NB // 2):
            whole_to_core(j).wait_recv()
            b_ref[rows(j), :] = whole_got[j]
        for b in range(NB):
            to_core(b).wait_send()
            to_y(b).wait_send()
            forward(b).wait_send()
            part_to_core(b).wait_send()
        for j in range(NB // 2):
            sum_to_y(j).wait_send()
            whole_to_core(j).wait_send()
            dy_own(j).wait()
            dy_core(j).wait()
            dy_y(j).wait_send()
            dy_forward(j).wait()
        for r in range(1, 4):
            vectors(r).wait_send()


def attention_forward(x, g, own_vec, wq, wk, wv, bqv, wd, lo, pad, alibi):
    last = lambda s: jnp.minimum(s, NB - 1)
    row = lambda width: pl.BlockSpec((B, width), lambda s: (last(s), 0))
    whole = lambda shape: pl.BlockSpec(shape, lambda s: (0,) * len(shape))
    like = jax.ShapeDtypeStruct
    dma = lambda n: pltpu.SemaphoreType.DMA((n,))
    half = NB // 2
    return pl.pallas_call(
        fwd_kernel,
        grid=(NB + TAIL,),
        in_specs=[pl.BlockSpec(memory_space=pl.ANY)] * 2
        + [row(SHARE), whole((16, SHARE))]
        + [whole((D, SHARE))] * 3
        + [whole((8, SHARE)), whole((SHARE, D)), row(1), whole((8, SEQ)), whole((8, STRIP))],
        out_specs=[pl.BlockSpec((LH, B, STRIP), lambda s: (0, last(s), 0))]
        + [row(SHARE)] * 5
        + [whole((OWN, D // 2))] * 2
        + [row(SHARE)] * 3
        + [whole((OWN, D)), whole((LH, 8, B)), whole((8, D)), whole((8, UNITS))]
        + [pl.BlockSpec(memory_space=pl.ANY)],
        scratch_shapes=[
            pltpu.VMEM((B, D), F32),
            pltpu.VMEM((LH, B, SHARE), BF),
            pltpu.VMEM((SEQ, SHARE), BF),
            pltpu.VMEM((LH, SEQ, SHARE), BF),
            pltpu.VMEM((B, STRIP), F32),
            pltpu.VMEM((LH, B, SHARE), F32),
            pltpu.VMEM((B, B), jnp.int32),
        ]
        + [pltpu.VMEM((NB, B, SHARE), BF)] * 3
        + [pltpu.VMEM((NB, B, D // 2), BF)] * 3
        + [pltpu.VMEM((half, B, D // 2), F32)]
        + [pltpu.VMEM((half, B, D // 2), BF)] * 4
        + [pltpu.VMEM((4, 16, SHARE), F32)]
        + [dma(NB)] * 8
        + [dma(half)] * 4
        + [dma(3)] * 2
        + [dma(half)] * 7,
        out_shape=[like((LH, SEQ, STRIP), BF)]
        + [like((SEQ, SHARE), BF)] * 3
        + [like((SEQ, SHARE), F32), like((SEQ, SHARE), BF)]
        + [like((OWN, D // 2), BF)] * 2
        + [like((SEQ, SHARE), BF)] * 3
        + [like((OWN, D), BF), like((LH, 8, B), F32), like((8, D), F32), like((8, UNITS), F32)]
        + [like((OWN, D), BF)],
        compiler_params=remote_params(0),
        cost_estimate=pl.CostEstimate(
            flops=16 * 10**9, bytes_accessed=40 * 2**20, transcendentals=8 * 10**6
        ),
        name="attention_forward",
    )(x, g, x, own_vec, wq, wk, wv, bqv, wd, lo, pad, alibi)


def mlp_kernel(
    a_own, a_par, xm, dy_s, vec, bup, wu0, wu1, wd0, wd1,
    mk_ref, ms_ref, gn_ref, h1_ref, gu_ref, su_ref, gd_ref, sd_ref, bs_ref, ru_ref,
    n2_s, n2t_s, dyt_s, am_s, ag_s, act_s, gp_s, us_s, s_u, r_u,
    *, bits, chunk,
):
    i = pl.program_id(0)
    core, y, ranks = place()
    partners = [{"dp": dp_partner(bit)} for bit in bits]

    def send_tile(n, kind):
        return remote(us_s.at[n], ru_ref.at[n], s_u.at[n], r_u.at[n], partners[kind])

    @pl.when(i == 0)
    def _():
        greet(partners)

        def assemble(rb, carry):
            rows = block_rows(rb)
            h1_ref[rows, :] = xm[rows, :].astype(F32)
            for part, a in ((core, a_own), (1 - core, a_par)):
                for half in range(2):
                    cols = feature_block(2 * half + part)
                    h1_ref[rows, cols] += a[rows, half * SHARE : (half + 1) * SHARE].astype(F32)
            value = h1_ref[rows, :] + vec[2:3, :]
            h1_ref[rows, :] = value
            mean, rstd = row_stats(value)
            n2 = ((value - mean) * rstd * vec[3:4, :] + vec[4:5, :]).astype(BF)
            n2_s[rows, :] = n2
            n2t_s[:, rows] = n2.T
            dyt_s[:, rows] = dy_s[rows, :].T
            am_s[rows, :] = jnp.zeros((B, D), F32)
            ag_s[rows, :] = jnp.zeros((B, D), F32)
            return carry

        lax.fori_loop(0, OWN // B, assemble, 0)

    def tile(wu, wd, which):
        bias = bup[which : which + 1, pl.ds(pl.multiple_of(lax.rem(i, 2) * TILE, TILE), TILE)]
        scale = math.sqrt(2.0 / math.pi)

        def rows_of(rb, sums):
            rows = pl.ds(pl.multiple_of(rb * B, B), B)
            pre = dot(n2_s[rows, :], wu[...]) + bias
            back = dot_nt(dy_s[rows, :], wd[...])
            square = pre * pre
            th = jnp.tanh(scale * pre * (1.0 + 0.044715 * square))
            half = 0.5 * (1.0 + th)
            act = (pre * half).astype(BF)
            slope = half + 0.5 * pre * (1.0 - th * th) * (scale + (3 * 0.044715 * scale) * square)
            gp = (slope * back).astype(BF)
            act_s[rows, :] = act
            gp_s[rows, :] = gp
            am_s[rows, :] += dot(act, wd[...])
            ag_s[rows, :] += dot_nt(gp, wu[...])
            return sums + jnp.sum(gp.astype(F32), axis=0, keepdims=True)

        sums = lax.fori_loop(0, OWN // B, rows_of, jnp.zeros((1, TILE), F32))
        bs_ref[...] = jnp.broadcast_to(sums, bs_ref.shape)

        def grads(left, right, keep, send, bit):
            def rows_of(j, carry):
                to = pl.ds(pl.multiple_of(j * 128, 128), 128)
                mine, other = piece(j, bit, chunk)
                keep[to, :] = dot(left[mine, :], right[...]).astype(BF)
                send[to, :] = dot(left[other, :], right[...]).astype(BF)
                return carry

            lax.fori_loop(0, D // 256, rows_of, 0)

        first = which == 0
        grads(n2t_s, gp_s, gu_ref, us_s.at[i] if first else su_ref, bits[0])
        if first:
            send_tile(i, 0).start()
        grads(dyt_s, act_s, gd_ref, us_s.at[2 + i] if first else sd_ref, bits[1] if first else bits[0])
        if first:
            send_tile(2 + i, 1).start()

    pl.when(i < 2)(lambda: tile(wu0, wd0, 0))
    pl.when(i >= 2)(lambda: tile(wu1, wd1, 1))

    @pl.when(i == 3)
    def _():
        split_store(mk_ref, ms_ref, am_s, core)
        gn_ref[...] = ag_s[...].astype(BF)
        for n in range(4):
            send_tile(n, n // 2).wait()


def feed_forward(a_own, a_par, xm, dy, vec, bup, wu0, wd0, w_other, bits, chunk):
    whole = lambda shape: pl.BlockSpec(shape, lambda i: (0,) * len(shape))
    low = lambda i: jnp.minimum(i, 1)
    high = lambda i: jnp.maximum(i - 2, 0)
    like = jax.ShapeDtypeStruct
    tile = pl.BlockSpec((D // 2, TILE), lambda i: (0, i))
    return pl.pallas_call(
        functools.partial(mlp_kernel, bits=bits, chunk=chunk),
        grid=(4,),
        in_specs=[whole((OWN, D // 2))] * 2
        + [whole((OWN, D))] * 2
        + [
            whole((8, D)),
            whole((8, UNITS)),
            pl.BlockSpec((D, TILE), lambda i: (0, low(i))),
            pl.BlockSpec((D, TILE), lambda i: (0, high(i))),
            pl.BlockSpec((TILE, D), lambda i: (low(i), 0)),
            pl.BlockSpec((TILE, D), lambda i: (high(i), 1)),
        ],
        out_specs=[whole((OWN, D // 2))] * 2
        + [whole((OWN, D))] * 2
        + [
            tile,
            pl.BlockSpec((D // 2, TILE), lambda i: (0, high(i))),
            tile,
            pl.BlockSpec((D // 2, TILE), lambda i: (0, high(i))),
            pl.BlockSpec((8, TILE), lambda i: (0, i)),
            pl.BlockSpec(memory_space=pl.ANY),
        ],
        scratch_shapes=[
            pltpu.VMEM((OWN, D), BF),
            pltpu.VMEM((D, OWN), BF),
            pltpu.VMEM((D, OWN), BF),
            pltpu.VMEM((OWN, D), F32),
            pltpu.VMEM((OWN, D), F32),
            pltpu.VMEM((OWN, TILE), BF),
            pltpu.VMEM((OWN, TILE), BF),
            pltpu.VMEM((4, D // 2, TILE), BF),
            pltpu.SemaphoreType.DMA((4,)),
            pltpu.SemaphoreType.DMA((4,)),
        ],
        out_shape=[like((OWN, D // 2), BF)] * 2
        + [
            like((OWN, D), BF),
            like((OWN, D), F32),
            like((D // 2, 2 * UNITS), BF),
            like((D // 2, UNITS), BF),
            like((D // 2, 2 * UNITS), BF),
            like((D // 2, UNITS), BF),
            like((8, 2 * UNITS), F32),
            like((4, D // 2, TILE), BF),
        ],
        compiler_params=remote_params(1),
        cost_estimate=pl.CostEstimate(
            flops=26 * 10**9, bytes_accessed=40 * 2**20, transcendentals=2 * 10**6
        ),
        name="feed_forward",
    )(a_own, a_par, xm, dy, vec, bup, wu0, w_other, wd0, w_other)


LEAD = 2
FINAL = 3
TILES = (("u", 0), ("u", 1), ("d", 0), ("d", 1), ("u", 2), ("d", 2), ("d", 3), ("u", 3), ("a", 0), ("a", 1))
OTHER_ORDER = (2, 3, 9)
FIRST = (0, 1, 0, 2, 3, 4, 6, 7)
USE = sorted(range(8), key=lambda p: (FIRST[p], p)) + [8, 9]
PAIRS = ((0, 4), (1, 7), (2, 5), (3, 6))
DRAIN = LEAD + FINAL + NB


def step_of(p, n):
    return FIRST[p] + 3 * (n - 1) if p < 8 else DRAIN + n - 1


def last_step(levels):
    return max(step_of(7, levels), step_of(8, levels))


def bwd_kernel(
    x0, x1, x2, x3, x_late, h1, gn, gn_any, mk, ms_any, dy_in, gu, gd, ru, su_any, sd_any, up_sums, hm,
    p_ref, q_ref, linv_ref, ctx_ref, k_ref, v_ref, vec, wq, wk, wv, wd,
    oo_ref, os_ref, tg_ref, wu_ref, wdn_ref, wqk_ref, wvd_ref, vt_ref,
    w_s, gh_s, gm_s, gt_s, qt_s, dl_s, ds_s, res_s, dkt_s, dvt_s, acc_s,
    gn_got, mr_got, gh_own, gh_y, gh_f,
    part_keep, part_send, part_got, sum_keep, sum_send, sum_got, ghx_s, st_keep, st_got, st_sum, st_all,
    gk, ru_s, g1, y_send, y_got, cs_ref, bs_ref, n1_ref, v_keep, v_send, v_away, v_sum, v_got,
    *rest, orders, chunk,
):
    levels = len(orders[0])
    stages = [rest[3 * n : 3 * n + 3] for n in range(levels - 1)]
    (
        s_gn, r_gn, s_mr, r_mr, s_gy, r_gy, s_gf, r_gf, s_pc, r_pc, s_sy, r_sy,
        s_tc, r_tc, s_ty, r_ty, s_g1, r_g1, s_yy, r_yy, l_g, l_r, s_gw, r_gw, s_va, r_va, s_vt, r_vt, *g_sems,
    ) = rest[3 * (levels - 1) :]
    step = pl.program_id(0)
    b = NB - 1 - (step - LEAD)
    core, y, ranks = place()
    beside, across = {"tensor": ranks[1]}, {"tensor": ranks[2]}
    order_of = lambda p: orders[1 if p in OTHER_ORDER else 0]
    partner = lambda bit: {"dp": dp_partner(bit)}
    half = NB // 2
    last = last_step(levels)
    lanes = head_of_lane((B, SHARE))

    send_gn = lambda j: remote(gn_any.at[block_rows(j)], gn_got.at[j], s_gn.at[j], r_gn.at[j], beside)
    send_mr = lambda j: remote(ms_any.at[block_rows(j)], mr_got.at[j], s_mr.at[j], r_mr.at[j], beside)
    send_gy = lambda j, side: remote(
        gh_own.at[j, :, feature_block(2 * side + core)],
        gh_y.at[j, :, side * SHARE : (side + 1) * SHARE],
        s_gy.at[2 * j + side], r_gy.at[2 * j + side], across,
    )
    send_gf = lambda j: remote(gh_y.at[j], gh_f.at[j], s_gf.at[j], r_gf.at[j], beside)
    send_part = lambda n: remote(part_send.at[lax.rem(n, 3)], part_got.at[n], s_pc.at[n], r_pc.at[n], beside)
    send_sum = lambda n: remote(sum_send.at[n], sum_got.at[n], s_sy.at[n], r_sy.at[n], across)
    send_tc = lambda n: remote(st_keep.at[n], st_got.at[n], s_tc.at[n], r_tc.at[n], beside)
    send_ty = lambda n: remote(st_sum.at[n], st_all.at[n], s_ty.at[n], r_ty.at[n], across)

    def tile_of(p):
        kind, n = TILES[p]
        return slice(n * TILE, (n + 1) * TILE), kind == "u"

    def send_first(p):
        cols, up = tile_of(p)
        src = (su_any if up else sd_any).at[:, slice(cols.start - UNITS, cols.stop - UNITS)]
        return remote(src, g1.at[p - 4], s_g1.at[p - 4], r_g1.at[p - 4], partner(order_of(p)[0]))

    def send_weights(p, part):
        n = 2 * (p - 8) + part
        return remote(
            gn_got.at[p - 8, :, slice(part * TILE, (part + 1) * TILE)], g1.at[p - 4, block_rows(part)],
            s_gw.at[n], r_gw.at[n], partner(order_of(p)[0]),
        )

    slot = [USE.index(p) % 2 for p in range(10)]

    def load_keep(p):
        cols, up = tile_of(p)
        return pltpu.make_async_copy((gu if up else gd).at[:, cols], gk.at[slot[p]], l_g.at[slot[p]])

    def load_got(p):
        return pltpu.make_async_copy(ru.at[p], ru_s.at[slot[p]], l_r.at[slot[p]])

    def send_stage(p, n):
        _, send, got = stages[n - 1]
        return remote(
            send.at[p % 4], got.at[p], g_sems[2 * n - 2].at[p], g_sems[2 * n - 1].at[p], partner(order_of(p)[n])
        )

    send_last = lambda n: remote(y_send.at[n], y_got.at[n], s_yy.at[n], r_yy.at[n], across)

    def split(p, n):
        order = order_of(p)
        if n == 1:
            keep = lambda rows: gk[slot[p], rows, :]
            if p < 4:
                load_got(p).wait()
                got = lambda rows: ru_s[slot[p], rows, :]
            else:
                got = lambda rows: g1[p - 4, rows, :]
            if p < 8:
                load_keep(p).wait()
            if 4 <= p < 8:
                send_first(p).wait_recv()
            if p >= 8:
                send_weights(p, 0).wait_recv()
                send_weights(p, 1).wait_recv()
        else:
            send_stage(p, n - 1).wait_recv()
            keep = lambda rows: stages[n - 2][0][p % 4, rows, :]
            got = lambda rows: stages[n - 2][2][p, rows, :]
        size = D >> n
        following = order[n]
        inner = chunk
        for other in order[n + 1 :]:
            inner *= 2 if other < following else 1
        mine = dp_bit(following)
        if p >= 4:
            send_stage(p - 4, n).wait_send()
        for group in range(size // (2 * inner)):
            to = slice(group * inner, (group + 1) * inner)
            for side, ref in ((mine, stages[n - 1][0]), (1 - mine, stages[n - 1][1])):
                rows = pl.ds(pl.multiple_of(group * 2 * inner + side * inner, inner), inner)
                ref[p % 4, to, :] = (keep(rows).astype(F32) + got(rows).astype(F32)).astype(BF)
        send_stage(p, n).start()

    def whole_tile(p):
        send_stage(p, levels - 1).wait_recv()
        keep, _, got = stages[levels - 2]
        total = keep[p % 4].astype(F32) + got[p].astype(F32)
        if p >= 8:
            (wqk_ref, wvd_ref)[p - 8][...] = total
        for n, (own, other) in enumerate(PAIRS):
            cols, up = tile_of(own)
            if p == own:
                (wu_ref if up else wdn_ref)[:, cols] = total
            if p == other:
                y_send[n] = total.astype(BF)
                send_last(n).start()

    def close(n):
        cols, up = tile_of(PAIRS[n][0])
        send_last(n).wait_recv()
        (wu_ref if up else wdn_ref)[:, cols] += y_got[n].astype(F32)

    @pl.when(step == 0)
    def _():
        greet([beside, across] + [partner(bit) for bit in orders[0]])
        for j in range(half - 1, -1, -1):
            send_gn(j).start()
            send_mr(j).start()
        for p in range(4, 8):
            send_first(p).start()
        for p in USE[:2]:
            load_keep(p).start()
            load_got(p).start()
        cs_ref[...] = jnp.zeros(cs_ref.shape, F32)
        bs_ref[...] = jnp.zeros(bs_ref.shape, F32)
        n1_ref[...] = jnp.zeros(n1_ref.shape, F32)
        dkt_s[...] = jnp.zeros(dkt_s.shape, F32)
        dvt_s[...] = jnp.zeros(dvt_s.shape, F32)
        acc_s[...] = jnp.zeros(acc_s.shape, F32)

    @pl.when(step < half)
    def _():
        j = half - 1 - step
        send_gn(j).wait_recv()
        send_mr(j).wait_recv()
        dy = dy_in[...].astype(F32)
        value = h1[...]

        def out(side):
            part = pl.ds(pl.multiple_of(side * SHARE, SHARE), SHARE)
            cols = feature_block(2 * side + core)
            total = mk[:, part].astype(F32) + mr_got[j, :, part].astype(F32)
            return (h1[:, cols] + total + vec[5:6, cols]).astype(BF)

        oo_ref[...] = out(y)
        os_ref[...] = out(1 - y)
        mean, rstd = row_stats(value)
        xhat = (value - mean) * rstd
        grad = gn[...].astype(F32) + gn_got[j].astype(F32)
        scaled = grad * vec[3:4, :]
        first = jnp.sum(scaled, axis=1, keepdims=True) / D
        second = jnp.sum(scaled * xhat, axis=1, keepdims=True) / D
        gh = dy + rstd * (scaled - first - xhat * second)
        for n, columns in enumerate((grad * xhat, grad, gh, dy)):
            cs_ref[n : n + 1, :] += jnp.sum(columns, axis=0, keepdims=True)
        gh_own[j] = gh.astype(BF)
        send_gy(j, 0).start()
        send_gy(j, 1).start()

    @pl.when((step >= LEAD) & (step < LEAD + NB))
    def _():
        j = b // 2

        @pl.when(lax.rem(b, 2) == y)
        def _():
            gh_s[...] = gh_own[j]

        @pl.when(lax.rem(b, 2) != y)
        def _():
            send_gf(j).wait_recv()
            for part, ref in ((core, gh_y), (1 - core, gh_f)):
                for side in range(2):
                    gh_s[:, feature_block(2 * side + part)] = ref[j, :, side * SHARE : (side + 1) * SHARE]

        gc = dot_nt(gh_s[...], wd[...]).astype(BF).astype(F32)
        scaled = gc * linv_ref[...]
        gcs = scaled.astype(BF)
        product = scaled * ctx_ref[...].astype(F32)
        qt_s[...] = q_ref[...].T.reshape(LH, HD, B)
        gt_s[...] = gcs.T.reshape(LH, HD, B)
        for h in range(LH):
            gm_s[h] = jnp.where(lanes == h, gcs, jnp.zeros_like(gcs))
            delta = jnp.sum(jnp.where(lanes == h, product, 0.0), axis=1, keepdims=True)
            dl_s[h] = jnp.broadcast_to(delta, (B, 128))

    def attend(nb):
        start = pl.multiple_of((b + 1 - nb) * B, B)

        def head(h, carry):
            gm = gm_s[h]
            delta = jnp.concatenate([dl_s[h]] * 2, axis=1)
            for r in range(nb):
                slot = SLOTS - nb + r
                cols = slice(slot * B, (slot + 1) * B)
                dp = dot_nt(gm, v_ref[pl.ds(pl.multiple_of(start + r * B, B), B), :])
                ds_s[:, cols] = (p_ref[h, :, cols].astype(F32) * (dp - delta)).astype(BF)
            live = slice((SLOTS - nb) * B, STRIP)
            keys = pl.ds(start, nb * B)
            res_s[h] = dot(ds_s[:, live], k_ref[keys, :])
            dkt_s[h, :, keys] += dot(qt_s[h], ds_s[:, live])
            dvt_s[h, :, keys] += dot(gt_s[h], p_ref[h, :, live])
            return carry

        lax.fori_loop(0, LH, head, 0)

    pl.when((step >= LEAD) & (b >= SLOTS - 1))(functools.partial(attend, SLOTS))
    for nb in range(SLOTS - 1, 0, -1):
        pl.when(b == nb - 1)(functools.partial(attend, nb))

    @pl.when((step >= LEAD) & (step < LEAD + NB))
    def _():
        dq = res_s[0]
        for h in range(1, LH):
            dq = jnp.where(lanes == h, res_s[h], dq)
        dq = (dq * (1.0 / math.sqrt(HD))).astype(BF)
        here = block_rows(b)
        dk = dkt_s[:, :, here].reshape(SHARE, B).astype(BF).T
        dv = dvt_s[:, :, here].reshape(SHARE, B).astype(BF).T
        bs_ref[0:1, :] += jnp.sum(dq.astype(F32), axis=0, keepdims=True)
        bs_ref[1:2, :] += jnp.sum(dv.astype(F32), axis=0, keepdims=True)

        for rank, x in zip(ranks, (x0, x1, x2, x3)):
            w_s[:, feature_block(rank)] = x[...].astype(F32)
        value = w_s[...]
        mean, rstd = row_stats(value)
        xhat = (value - mean) * rstd
        n1t = (xhat * vec[0:1, :] + vec[1:2, :]).astype(BF).T
        acc_s[:, 0:SHARE] += dot(n1t, dq)
        acc_s[:, SHARE : 2 * SHARE] += dot(n1t, dk)
        acc_s[:, 2 * SHARE : 3 * SHARE] += dot(n1t, dv)
        acc_s[:, 3 * SHARE :] += dot(gh_s[...].T, ctx_ref[...])

        grad = dot_nt(dq, wq[...]) + dot_nt(dk, wk[...]) + dot_nt(dv, wv[...])
        scaled = grad * vec[0:1, :]
        first = jnp.sum(scaled, axis=1, keepdims=True)
        second = jnp.sum(scaled * xhat, axis=1, keepdims=True)
        column = lax.broadcasted_iota(jnp.int32, (B, 128), 1)
        packed = jnp.where(
            column == 0, first, jnp.where(column == 1, second, jnp.where(column == 2, mean, rstd))
        )
        st_keep[b] = packed.T[0:8, :]
        send_tc(b).start()
        w_s[...] = grad

        @pl.when(step >= LEAD + 3)
        def _():
            send_part(b + 3).wait_send()

        for n, side in enumerate((y, 1 - y)):
            cols = slice(n * SHARE, (n + 1) * SHARE)
            part_keep[lax.rem(b, 2), :, cols] = w_s[:, feature_block(2 * side + core)].astype(BF)
            part_send[lax.rem(b, 3), :, cols] = w_s[:, feature_block(2 * side + 1 - core)].astype(BF)
        send_part(b).start()
        ghx_s[lax.rem(b, 4)] = gh_s[:, feature_block(ranks[0])]

    @pl.when(step == LEAD + NB - 1)
    def _():
        for p in (8, 9):
            cols = slice((p - 8) * TILE, (p - 7) * TILE)
            for j in range(D // 256):
                mine, other = piece(j, order_of(p)[0], chunk)
                gk[slot[p], j * 128 : (j + 1) * 128, :] = acc_s[mine, cols].astype(BF)
                into = slice(j // 2 * TILE, (j // 2 + 1) * TILE)
                gn_got[p - 8, j % 2 * 128 : (j % 2 + 1) * 128, into] = acc_s[other, cols].astype(BF)
            for part in range(2):
                send_weights(p, part).start()

    send_away = lambda: remote(v_send, v_away, s_va.at[0], r_va.at[0], across)
    send_total = lambda n: remote(
        v_sum.at[n], v_got.at[n], s_vt.at[n], r_vt.at[n], partner(orders[0][n])
    )

    @pl.when(step == half)
    def _():
        for ref, rank, side in ((v_keep, ranks[0], 0), (v_send, ranks[2], UNITS)):
            ref[0:4, :] = cs_ref[0:4, feature_block(rank)]
            for n in range(4):
                ref[4 + n : 5 + n, :] = up_sums[0:1, side + n * SHARE : side + (n + 1) * SHARE]
        send_away().start()

    @pl.when(step == half + 4)
    def _():
        send_away().wait_recv()
        v_sum[0, 0:8, :] = v_keep[...] + v_away[...]

    @pl.when((step >= LEAD + 1) & (step < LEAD + 1 + NB))
    def _():
        n = b + 1
        send_part(n).wait_recv()
        send_tc(n).wait_recv()
        keep = part_keep[lax.rem(n, 2)].astype(F32)
        sum_keep[lax.rem(n, 3)] = keep[:, :SHARE] + part_got[n, :, :SHARE].astype(F32)
        sum_send[n] = (keep[:, SHARE:] + part_got[n, :, SHARE:].astype(F32)).astype(BF)
        st_sum[n] = st_keep[n] + st_got[n]
        send_sum(n).start()
        send_ty(n).start()

    @pl.when((step >= LEAD + FINAL) & (step < LEAD + FINAL + NB))
    def _():
        n = b + FINAL
        send_sum(n).wait_recv()
        send_ty(n).wait_recv()
        grad = sum_keep[lax.rem(n, 3)] + sum_got[n].astype(F32)
        row = lax.broadcasted_iota(jnp.int32, (8, B), 0)
        stats = jnp.where(row < 2, st_sum[n] + st_all[n], st_keep[n])
        stats = jnp.concatenate([stats] * 16, axis=0).T
        xhat = (x_late[...].astype(F32) - stats[:, 2:3]) * stats[:, 3:4]
        scaled = grad * vec[0:1, feature_block(ranks[0])]
        inner = scaled - stats[:, 0:1] / D - xhat * (stats[:, 1:2] / D)
        tg_ref[...] = ghx_s[lax.rem(n, 4)].astype(F32) + stats[:, 3:4] * inner
        n1_ref[0:1, :] += jnp.sum(grad * xhat, axis=0, keepdims=True)
        n1_ref[1:2, :] += jnp.sum(grad, axis=0, keepdims=True)

    row16 = lax.broadcasted_iota(jnp.int32, (16, SHARE), 0)

    @pl.when(step == DRAIN - 1)
    def _():
        v_sum[0, 8:10, :] = n1_ref[0:2, :]
        v_sum[0, 10:12, :] = bs_ref[0:2, :]
        lane = lax.broadcasted_iota(jnp.int32, (4, SHARE), 1)
        top = jnp.full((4, SHARE), NEG, F32)
        for h in range(LH):
            top = jnp.where(lane == h, jnp.max(hm[h]), top)
        v_sum[0, 12:16, :] = top
        send_total(0).start()

    for n in range(levels):

        @pl.when(step == DRAIN + n)
        def _():
            send_total(n).wait_recv()
            mine, other = v_sum[n], v_got[n]
            total = jnp.where(row16 < 12, mine + other, jnp.maximum(mine, other))
            if n == levels - 1:
                vt_ref[...] = total
            else:
                v_sum[n + 1] = total
                send_total(n + 1).start()

    for j in range(half - 1, -1, -1):

        @pl.when(step == half - j)
        def _():
            send_gy(j, 0).wait_recv()
            send_gy(j, 1).wait_recv()
            send_gf(j).start()

    for p in range(10):
        for n in range(1, levels):
            pl.when(step == step_of(p, n))(functools.partial(split, p, n))
        pl.when(step == step_of(p, levels))(functools.partial(whole_tile, p))

    def load_next(p):
        load_keep(p).start()
        if p < 4:
            load_got(p).start()

    for n in range(2, 8):
        pl.when(step == FIRST[USE[n - 2]])(functools.partial(load_next, USE[n]))

    @pl.when(step == last)
    def _():
        for j in range(half):
            close(j)
            for copy in (send_gn, send_mr, send_gf, send_last):
                copy(j).wait_send()
            for side in range(2):
                send_gy(j, side).wait_send()
            for level in range(1, levels):
                send_stage(6 + j, level).wait_send()
        for n in range(NB):
            for copy in (send_sum, send_tc, send_ty):
                copy(n).wait_send()
        for n in range(3):
            send_part(n).wait_send()
        for p in range(4, 8):
            send_first(p).wait_send()
        for p in (8, 9):
            for part in range(2):
                send_weights(p, part).wait_send()
        send_away().wait_send()
        for n in range(levels):
            send_total(n).wait_send()


def attention_backward(
    xs, h1, gn, mk, ms, dy, gu, gd, ru, su, sd, up_sums, hm, p, q, linv, ctx, k, v, vec, wq, wk, wv, wd,
    orders, chunk,
):
    levels = len(orders[0])
    half = NB // 2
    block = lambda s: jnp.clip(NB - 1 + LEAD - s, 0, NB - 1)
    late = lambda s: jnp.clip(NB - 1 + LEAD + FINAL - s, 0, NB - 1)
    row = lambda width: pl.BlockSpec((B, width), lambda s: (block(s), 0))
    own = lambda width: pl.BlockSpec((B, width), lambda s: (jnp.maximum(half - 1 - s, 0), 0))
    once = pl.Buffered(1)
    whole = lambda *shape: pl.BlockSpec(shape, lambda s: (0,) * len(shape), pipeline_mode=once)
    anywhere = pl.BlockSpec(memory_space=pl.ANY)
    like = jax.ShapeDtypeStruct
    vmem = lambda *shape, dtype=BF: pltpu.VMEM(shape, dtype)
    dma = lambda n: pltpu.SemaphoreType.DMA((n,))
    final_late = pl.BlockSpec((B, SHARE), lambda s: (late(s), 0))
    return pl.pallas_call(
        functools.partial(bwd_kernel, orders=orders, chunk=chunk),
        grid=(last_step(levels) + 1,),
        in_specs=[row(SHARE)] * 4
        + [final_late, own(D), own(D), anywhere, own(D // 2), anywhere]
        + [own(D)]
        + [anywhere] * 2
        + [anywhere] * 3
        + [whole(8, 2 * UNITS), whole(LH, 8, B)]
        + [pl.BlockSpec((LH, B, STRIP), lambda s: (0, block(s), 0))]
        + [row(SHARE)] * 3
        + [whole(SEQ, SHARE)] * 2
        + [whole(8, D)]
        + [whole(D, SHARE)] * 3
        + [whole(SHARE, D)],
        out_specs=[own(SHARE), own(SHARE), final_late]
        + [whole(chunk, UNITS)] * 2
        + [whole(chunk, TILE)] * 2
        + [whole(16, SHARE)],
        scratch_shapes=[
            vmem(B, D, dtype=F32),
            vmem(B, D),
            vmem(LH, B, SHARE),
            vmem(LH, HD, B),
            vmem(LH, HD, B),
            vmem(LH, B, 128, dtype=F32),
            vmem(B, STRIP),
            vmem(LH, B, SHARE, dtype=F32),
            vmem(LH, HD, SEQ, dtype=F32),
            vmem(LH, HD, SEQ, dtype=F32),
            vmem(D, 4 * SHARE, dtype=F32),
            vmem(half, B, D),
            vmem(half, B, D // 2),
            vmem(half, B, D),
            vmem(half, B, D // 2),
            vmem(half, B, D // 2),
            vmem(2, B, D // 2),
            vmem(3, B, D // 2),
            vmem(NB, B, D // 2),
            vmem(3, B, SHARE, dtype=F32),
            vmem(NB, B, SHARE),
            vmem(NB, B, SHARE),
            vmem(4, B, SHARE),
            vmem(NB, 8, B, dtype=F32),
            vmem(NB, 8, B, dtype=F32),
            vmem(NB, 8, B, dtype=F32),
            vmem(NB, 8, B, dtype=F32),
            vmem(2, D // 2, TILE),
            vmem(2, D // 2, TILE),
            vmem(6, D // 2, TILE),
            vmem(half, chunk, TILE),
            vmem(half, chunk, TILE),
            vmem(8, D, dtype=F32),
            vmem(8, SHARE, dtype=F32),
            vmem(8, SHARE, dtype=F32),
            vmem(8, SHARE, dtype=F32),
            vmem(8, SHARE, dtype=F32),
            vmem(8, SHARE, dtype=F32),
            vmem(levels, 16, SHARE, dtype=F32),
            vmem(levels, 16, SHARE, dtype=F32),
        ]
        + [vmem(slots, D >> (n + 1), TILE) for n in range(1, levels) for slots in (4, 4, 10)]
        + [dma(half)] * 4
        + [dma(NB)] * 2
        + [dma(half)] * 2
        + [dma(NB)] * 8
        + [dma(4)] * 2
        + [dma(half)] * 2
        + [dma(2)] * 2
        + [dma(4)] * 2
        + [dma(1)] * 2
        + [dma(levels)] * 2
        + [dma(10)] * (2 * (levels - 1)),
        out_shape=[like((OWN, SHARE), BF)] * 2
        + [like((SEQ, SHARE), F32)]
        + [like((chunk, UNITS), F32)] * 2
        + [like((chunk, TILE), F32)] * 2
        + [like((16, SHARE), F32)],
        compiler_params=remote_params(2),
        cost_estimate=pl.CostEstimate(
            flops=30 * 10**9, bytes_accessed=50 * 2**20, transcendentals=0
        ),
        name="backward",
    )(
        *xs, xs[0], h1, gn, gn, mk, ms, dy, gu, gd, ru, su, sd, up_sums, hm, p, q, linv, ctx, k, v, vec, wq, wk, wv, wd
    )


def swap(value, axis, bit):
    size = lax.axis_size(axis)
    return lax.ppermute(value, axis, [(i, i ^ bit) for i in range(size)])


def dp_bits():
    bits, bit = [], 1
    while bit < lax.axis_size("dp"):
        bits.append(bit)
        bit *= 2
    return bits


def pick(value, axis, index):
    return lax.dynamic_index_in_dim(value, index, axis, keepdims=False)


def shards(
    tokens,
    out_grad,
    segments,
    padding,
    norm1_gain,
    norm1_bias,
    w_query,
    b_query,
    w_key,
    w_value,
    b_value,
    w_dense,
    dense_bias,
    norm2_gain,
    norm2_bias,
    w_up,
    b_up,
    w_down,
    down_bias,
):
    t = lax.axis_index("tensor")
    rank = lax.axis_index("dp")
    size = lax.axis_size("dp")
    core, y = t % 2, t // 2
    core_swap = lambda value: swap(value, "tensor", 1)
    y_swap = lambda value: swap(value, "tensor", 2)
    rows8 = lambda value: jnp.pad(value, ((0, 8 - value.shape[0]), (0, 0)))

    own_vec = jnp.concatenate(
        [
            jnp.stack([norm1_gain, norm1_bias, dense_bias, norm2_gain, norm2_bias, down_bias, down_bias, down_bias]),
            b_up.reshape(4, SHARE),
            b_up.reshape(4, SHARE),
        ]
    ).astype(F32)

    part = D // size
    cut = lambda w: lax.dynamic_slice_in_dim(w, rank * part, part, 0)
    w_part = y_swap(jnp.concatenate([cut(w_up), cut(w_down)], axis=1))
    w_other = lax.all_gather(w_part, "dp", axis=0, tiled=True)
    seg = segments.reshape(SEQ)
    index = jnp.arange(SEQ, dtype=jnp.int32)
    first = jnp.zeros((SEQ,), jnp.int32)
    for value in range(1, 4):
        first = jnp.where(seg == value, jnp.sum((seg < value).astype(jnp.int32)), first)
    lowest = jnp.maximum(first, index - (WIN - 1))
    pad_row = rows8(jnp.where(padding.reshape(1, SEQ) == 1, 0.0, NEG).astype(F32))
    heads = t * LH + jnp.arange(LH)
    slopes = jnp.exp2(-8.0 * (heads.astype(F32) + 1.0) / HEADS)
    alibi = rows8(slopes[:, None] * (jnp.arange(STRIP) - (STRIP - 1)).astype(F32)[None, :])

    p, q, k, v, linv, ctx, a_own, a_par, x1, x2, x3, xm, hm, vec, b_up_pair, dy = attention_forward(
        tokens, out_grad, own_vec, w_query, w_key, w_value,
        rows8(jnp.stack([b_query, b_value]).astype(F32)), w_dense,
        lowest.reshape(SEQ, 1), pad_row, alibi,
    )
    xs = [tokens, x1, x2, x3]

    bits = dp_bits()
    order_a = bits if size == 8 else bits[::-1]
    order_b = [2, 4, 1] if size == 8 else [bits[-2], bits[-1], *bits[:-2][::-1]]
    mk, ms, gn, h1, gu, su, gd, sd, up_sums, ru = feed_forward(
        a_own, a_par, xm, dy, vec, b_up_pair, w_up, w_down, w_other, (order_a[0], order_b[0]), part
    )
    out_own, out_send, tokens_grad, w_up_grad, w_down_grad, g_qk, g_vd, sums = attention_backward(
        xs, h1, gn, mk, ms, dy, gu, gd, ru, su, sd, up_sums, hm, p, q, linv, ctx, k, v, vec,
        w_query, w_key, w_value, w_dense, (order_a, order_b), part,
    )
    w_down_grad = w_down_grad.T
    out_y = y_swap(out_send)
    pair = jnp.stack([out_own, out_y]).reshape(2, NB // 2, B, SHARE)
    output = jnp.where(y == 0, pair, pair[::-1]).transpose(1, 0, 2, 3).reshape(SEQ, SHARE)

    head_max = sums[12, :LH]
    column_scale = jnp.repeat(jnp.sqrt(TAU / jnp.maximum(head_max, TAU)), HD)
    return (
        output,
        tokens_grad,
        sums[8],
        sums[9],
        g_qk[:, :SHARE],
        sums[10],
        g_qk[:, SHARE:],
        g_vd[:, :SHARE],
        sums[11],
        g_vd[:, SHARE:].T,
        sums[2],
        sums[0],
        sums[1],
        w_up_grad,
        sums[4:8].reshape(UNITS),
        w_down_grad,
        sums[3],
        head_max,
        w_query.astype(F32) * column_scale,
        b_query.astype(F32) * column_scale,
        w_key.astype(F32) * column_scale,
    )


def solution(mesh):
    in_specs = (
        P("dp", "tensor"),
        P("dp", "tensor"),
        P("dp", None),
        P("dp", None),
        P("tensor"),
        P("tensor"),
        P(None, "tensor"),
        P("tensor"),
        P(None, "tensor"),
        P(None, "tensor"),
        P("tensor"),
        P("tensor", None),
        P("tensor"),
        P("tensor"),
        P("tensor"),
        P(None, "tensor"),
        P("tensor"),
        P("tensor", None),
        P("tensor"),
    )
    out_specs = (
        P("dp", "tensor"),
        P("dp", "tensor"),
        P("tensor"),
        P("tensor"),
        P("dp", "tensor"),
        P("tensor"),
        P("dp", "tensor"),
        P("dp", "tensor"),
        P("tensor"),
        P("tensor", "dp"),
        P("tensor"),
        P("tensor"),
        P("tensor"),
        P("dp", "tensor"),
        P("tensor"),
        P("tensor", "dp"),
        P("tensor"),
        P("tensor"),
        P(None, "tensor"),
        P("tensor"),
        P(None, "tensor"),
    )
    return jax.shard_map(shards, mesh=mesh, in_specs=in_specs, out_specs=out_specs, check_vma=False)
```

```python
import functools
import math

import jax
import jax.numpy as jnp
from jax import lax
from jax.experimental import pallas as pl
from jax.experimental.pallas import tpu as pltpu
from jax.sharding import PartitionSpec as P

HEADS = 16
HD = 64
WIN = 1024
D = 1024
FF = 4096
SEQ = 2048
B = 256
NB = SEQ // B
SLOTS = WIN // B + 1
STRIP = SLOTS * B
LH = 4
SHARE = LH * HD
UNITS = FF // 4
TILE = 512
OWN = SEQ // 2

EPS = 1e-05
TAU = 2.0
NEG = -1e30
F32 = jnp.float32
BF = jnp.bfloat16
VMEM_LIMIT = 62 * 2**20


def dot(a, b):
    return jnp.dot(a, b, preferred_element_type=F32)


def dot_nt(a, b):
    return lax.dot_general(a, b, (((1,), (1,)), ((), ())), preferred_element_type=F32)


def params():
    return pltpu.CompilerParams(
        dimension_semantics=("arbitrary",), vmem_limit_bytes=VMEM_LIMIT
    )


def feature_block(rank):
    return pl.ds(pl.multiple_of(rank * SHARE, SHARE), SHARE)


def head_of_lane(shape):
    return lax.broadcasted_iota(jnp.int32, shape, 1) // HD


def ordered(kernel, count):
    return lambda ids, *refs: kernel(ids, *refs[count:])


def waits(after):
    return [pl.BlockSpec(memory_space=pl.ANY)] * len(after)


def row_stats(rows):
    mean = jnp.sum(rows, axis=1, keepdims=True) / D
    square = jnp.sum(rows * rows, axis=1, keepdims=True) / D
    return mean, lax.rsqrt(square - mean * mean + EPS)


def piece(j, bit, chunk):
    inner = bit * chunk
    mine = dp_bit(bit)
    base = (j * 128) // inner * (2 * inner) + (j * 128) % inner
    return [
        pl.ds(pl.multiple_of(base + side * inner, 128), 128) for side in (mine, 1 - mine)
    ]


def dp_bit(bit):
    return lax.rem(lax.div(lax.axis_index("dp"), bit), 2)


def dp_partner(bit):
    return lax.axis_index("dp") + bit - 2 * bit * dp_bit(bit)


def place():
    t = lax.axis_index("tensor")
    core, y = lax.rem(t, 2), lax.div(t, 2)
    return core, y, (t, 2 * y + 1 - core, 2 * (1 - y) + core, 2 * (1 - y) + 1 - core)


def remote(src, dst, send, got, where):
    return pltpu.make_async_remote_copy(
        src_ref=src, dst_ref=dst, send_sem=send, recv_sem=got,
        device_id=where, device_id_type=pl.DeviceIdType.MESH,
    )


def greet(places):
    barrier = pltpu.get_barrier_semaphore()
    for where in places:
        pl.semaphore_signal(
            barrier, inc=1, device_id=where, device_id_type=pl.DeviceIdType.MESH
        )
    pl.semaphore_wait(barrier, len(places))


def block_rows(b):
    return pl.ds(pl.multiple_of(b * B, B), B)


def remote_params(collective_id):
    return pltpu.CompilerParams(
        dimension_semantics=("arbitrary",),
        vmem_limit_bytes=VMEM_LIMIT,
        collective_id=collective_id,
        has_side_effects=True,
    )


def split_store(keep_ref, send_ref, value_ref, core):
    for half in range(2):
        cols = slice(half * SHARE, (half + 1) * SHARE)
        keep_ref[:, cols] = value_ref[:, feature_block(2 * half + core)].astype(keep_ref.dtype)
        send_ref[:, cols] = value_ref[:, feature_block(2 * half + 1 - core)].astype(
            send_ref.dtype
        )


TAIL = 3


def fwd_kernel(
    x_any, g_any, x_own, own_vec, wq, wk, wv, bqv, wd, lo, pad, alibi,
    p_ref, q_ref, k_ref, v_ref, linv_ref, ctx_ref, a_ref, b_ref, x1_ref, x2_ref, x3_ref, xm_ref, hm_ref, vec, bup_ref, dy_any,
    xs, qm_s, k_s, va_s, u_s, res_s, lo_s,
    xc, xy, xf, part_keep, part_send, part_got, sum_keep, sum_send, sum_got, whole_own, whole_got,
    v_all,
    s_xc, r_xc, s_xy, r_xy, s_xf, r_xf, s_pc, r_pc, s_sy, r_sy, s_wc, r_wc,
    s_v, r_v, l_d, s_dc, r_dc, s_dy, r_dy, s_df, r_df,
):
    step = pl.program_id(0)
    core, y, ranks = place()

    rows = block_rows
    beside, across = {"tensor": ranks[1]}, {"tensor": ranks[2]}

    def to_core(b):
        return remote(x_any.at[rows(b)], xc.at[b], s_xc.at[b], r_xc.at[b], beside)

    def to_y(b):
        return remote(x_any.at[rows(b)], xy.at[b], s_xy.at[b], r_xy.at[b], across)

    def forward(b):
        return remote(xy.at[b], xf.at[b], s_xf.at[b], r_xf.at[b], beside)

    def part_to_core(b):
        return remote(part_send.at[b], part_got.at[b], s_pc.at[b], r_pc.at[b], beside)

    def sum_to_y(j):
        return remote(sum_send.at[j], sum_got.at[j], s_sy.at[j], r_sy.at[j], across)

    def whole_to_core(j):
        return remote(whole_own.at[j], whole_got.at[j], s_wc.at[j], r_wc.at[j], beside)

    def vectors(r):
        return remote(v_all.at[0], v_all.at[r], s_v.at[r - 1], r_v.at[r - 1], {"tensor": ranks[r]})

    mine = feature_block(ranks[0])

    def dy_own(j):
        return pltpu.make_async_copy(g_any.at[rows(2 * j + y)], dy_any.at[rows(j), mine], l_d.at[j])

    def dy_core(j):
        return remote(g_any.at[rows(2 * j + y)], dy_any.at[rows(j), mine], s_dc.at[j], r_dc.at[j], beside)

    def dy_y(j):
        return remote(g_any.at[rows(2 * j + 1 - y)], dy_any.at[rows(j), mine], s_dy.at[j], r_dy.at[j], across)

    def dy_forward(j):
        block = dy_any.at[rows(j), feature_block(ranks[2])]
        return remote(block, block, s_df.at[j], r_df.at[j], beside)

    @pl.when(step == 0)
    def _():
        v_all[0] = own_vec[...]
        greet((beside, across, {"tensor": ranks[3]}))
        for r in range(1, 4):
            vectors(r).start()
        for b in range(3):
            to_y(b).start()
            to_core(b).start()
        for r in range(1, 4):
            vectors(r).wait_recv()
        for r in range(4):
            vec[:, feature_block(ranks[r])] = v_all[r, 0:8, :]
        bup_ref[...] = jnp.zeros(bup_ref.shape, F32)
        for n, r in enumerate((0, 2)):
            for part in range(4):
                bup_ref[n : n + 1, part * SHARE : (part + 1) * SHARE] = v_all[r, 8 + part : 9 + part, :]
        to_y(0).wait_recv()
        forward(0).start()
        hm_ref[...] = jnp.full(hm_ref.shape, NEG, F32)

    for b in range(3, NB):

        @pl.when(step == b - 2)
        def _():
            to_y(b).start()
            to_core(b).start()

    row_i = lax.broadcasted_iota(jnp.int32, (B, B), 0)
    col_i = lax.broadcasted_iota(jnp.int32, (B, B), 1)
    lanes = head_of_lane((B, SHARE))

    for j in range(NB // 2):

        @pl.when(step == j + 4)
        def _():
            dy_own(j).start()
            dy_core(j).start()
            dy_y(j).start()

        @pl.when(step == j + 7)
        def _():
            dy_y(j).wait_recv()
            dy_forward(j).start()

    @pl.when(step < NB - 1)
    def _():
        to_y(step + 1).wait_recv()
        forward(step + 1).start()

    @pl.when(step < NB)
    def _():
        to_core(step).wait_recv()
        forward(step).wait_recv()
        blocks = (x_own[...], xc[step], xy[step], xf[step])
        for rank, block, ref in zip(ranks, blocks, (None, x1_ref, x2_ref, x3_ref)):
            xs[:, feature_block(rank)] = block.astype(F32)
            if ref is not None:
                ref[...] = block
        value = xs[...]

        @pl.when(lax.rem(step, 2) == y)
        def _():
            xm_ref[rows(step // 2), :] = value.astype(BF)

        mean, rstd = row_stats(value)
        n1 = ((value - mean) * rstd * vec[0:1, :] + vec[1:2, :]).astype(BF)
        q = (dot(n1, wq[...]) + bqv[0:1, :]).astype(BF)
        k = dot(n1, wk[...]).astype(BF)
        v = (dot(n1, wv[...]) + bqv[1:2, :]).astype(BF)
        qs = q * jnp.asarray(1.0 / math.sqrt(HD), BF)
        q_ref[...] = qs
        k_ref[...] = k
        v_ref[...] = v
        here = rows(step)
        k_s[here, :] = k
        for h in range(LH):
            qm_s[h] = jnp.where(lanes == h, qs, jnp.zeros_like(qs))
            va_s[h, here, :] = jnp.where(lanes == h, v, jnp.ones_like(v))
        lo_s[...] = jnp.broadcast_to(lo[...], (B, B))

    def attend(nb):
        start = pl.multiple_of((step + 1 - nb) * B, B)

        def head(h, carry):
            qm = qm_s[h]
            top = jnp.full((B, 128), NEG, F32)
            biggest = hm_ref[h]
            for r in range(nb):
                slot = SLOTS - nb + r
                base = pl.multiple_of(start + r * B, B)
                s = dot_nt(qm, k_s[pl.ds(base, B), :])
                inside = col_i + base >= lo_s[...]
                shut = pad[0:1, pl.ds(base, B)]
                if r == nb - 1:
                    s = jnp.where(row_i == col_i, s, s + shut)
                    s = jnp.where(inside & (col_i <= row_i), s, NEG)
                else:
                    s = jnp.where(inside, s + shut, NEG)
                biggest = jnp.maximum(biggest, jnp.max(s.reshape(B // 8, 8, B), axis=0))
                s = s + alibi[pl.ds(h, 1), slot * B : (slot + 1) * B]
                u_s[:, slot * B : (slot + 1) * B] = s
                top = jnp.maximum(top, jnp.maximum(s[:, :128], s[:, 128:]))
            hm_ref[h] = biggest
            top = jnp.max(top, axis=1, keepdims=True)
            for r in range(nb):
                slot = SLOTS - nb + r
                cols = slice(slot * B, (slot + 1) * B)
                p_ref[h, :, cols] = jnp.exp(u_s[:, cols] - top).astype(BF)
            res_s[h] = dot(p_ref[h, :, (SLOTS - nb) * B :], va_s[h, pl.ds(start, nb * B), :])
            return carry

        lax.fori_loop(0, LH, head, 0, unroll=True)

    for nb in range(1, SLOTS):
        pl.when(step == nb - 1)(functools.partial(attend, nb))
    pl.when((step >= SLOTS - 1) & (step < NB))(functools.partial(attend, SLOTS))

    @pl.when(step < NB)
    def _():
        ctx = res_s[0]
        total = res_s[LH - 1]
        for h in range(1, LH):
            ctx = jnp.where(lanes == h, res_s[h], ctx)
            total = jnp.where(lanes == h, res_s[h - 1], total)
        inv = 1.0 / pltpu.roll(total, SHARE - HD, 1)
        linv_ref[...] = inv
        ctx = (ctx * inv).astype(BF)
        ctx_ref[...] = ctx
        xs[...] = dot(ctx, wd[...])
        split_store(part_keep.at[step], part_send.at[step], xs, core)
        part_to_core(step).start()

    @pl.when((step >= 1) & (step <= NB))
    def _():
        b = step - 1
        j = b // 2
        part_to_core(b).wait_recv()
        total = part_keep[b].astype(F32) + part_got[b].astype(F32)

        @pl.when(lax.rem(b, 2) == y)
        def _():
            sum_keep[j] = total

        @pl.when(lax.rem(b, 2) != y)
        def _():
            sum_send[j] = total.astype(BF)
            sum_to_y(j).start()

    @pl.when((step >= TAIL) & (lax.rem(step + NB - TAIL, 2) == y))
    def _():
        j = (step - TAIL) // 2
        sum_to_y(j).wait_recv()
        total = (sum_keep[j] + sum_got[j].astype(F32)).astype(BF)
        whole_own[j] = total
        a_ref[rows(j), :] = total
        whole_to_core(j).start()

    @pl.when(step == NB + TAIL - 1)
    def _():
        for j in range(NB // 2):
            whole_to_core(j).wait_recv()
            b_ref[rows(j), :] = whole_got[j]
        for b in range(NB):
            to_core(b).wait_send()
            to_y(b).wait_send()
            forward(b).wait_send()
            part_to_core(b).wait_send()
        for j in range(NB // 2):
            sum_to_y(j).wait_send()
            whole_to_core(j).wait_send()
            dy_own(j).wait()
            dy_core(j).wait()
            dy_y(j).wait_send()
            dy_forward(j).wait()
        for r in range(1, 4):
            vectors(r).wait_send()


def attention_forward(x, g, own_vec, wq, wk, wv, bqv, wd, lo, pad, alibi):
    last = lambda s: jnp.minimum(s, NB - 1)
    row = lambda width: pl.BlockSpec((B, width), lambda s: (last(s), 0))
    whole = lambda shape: pl.BlockSpec(shape, lambda s: (0,) * len(shape))
    like = jax.ShapeDtypeStruct
    dma = lambda n: pltpu.SemaphoreType.DMA((n,))
    half = NB // 2
    return pl.pallas_call(
        fwd_kernel,
        grid=(NB + TAIL,),
        in_specs=[pl.BlockSpec(memory_space=pl.ANY)] * 2
        + [row(SHARE), whole((16, SHARE))]
        + [whole((D, SHARE))] * 3
        + [whole((8, SHARE)), whole((SHARE, D)), row(1), whole((8, SEQ)), whole((8, STRIP))],
        out_specs=[pl.BlockSpec((LH, B, STRIP), lambda s: (0, last(s), 0))]
        + [row(SHARE)] * 5
        + [whole((OWN, D // 2))] * 2
        + [row(SHARE)] * 3
        + [whole((OWN, D)), whole((LH, 8, B)), whole((8, D)), whole((8, UNITS))]
        + [pl.BlockSpec(memory_space=pl.ANY)],
        scratch_shapes=[
            pltpu.VMEM((B, D), F32),
            pltpu.VMEM((LH, B, SHARE), BF),
            pltpu.VMEM((SEQ, SHARE), BF),
            pltpu.VMEM((LH, SEQ, SHARE), BF),
            pltpu.VMEM((B, STRIP), F32),
            pltpu.VMEM((LH, B, SHARE), F32),
            pltpu.VMEM((B, B), jnp.int32),
        ]
        + [pltpu.VMEM((NB, B, SHARE), BF)] * 3
        + [pltpu.VMEM((NB, B, D // 2), BF)] * 3
        + [pltpu.VMEM((half, B, D // 2), F32)]
        + [pltpu.VMEM((half, B, D // 2), BF)] * 4
        + [pltpu.VMEM((4, 16, SHARE), F32)]
        + [dma(NB)] * 8
        + [dma(half)] * 4
        + [dma(3)] * 2
        + [dma(half)] * 7,
        out_shape=[like((LH, SEQ, STRIP), BF)]
        + [like((SEQ, SHARE), BF)] * 3
        + [like((SEQ, SHARE), F32), like((SEQ, SHARE), BF)]
        + [like((OWN, D // 2), BF)] * 2
        + [like((SEQ, SHARE), BF)] * 3
        + [like((OWN, D), BF), like((LH, 8, B), F32), like((8, D), F32), like((8, UNITS), F32)]
        + [like((OWN, D), BF)],
        compiler_params=remote_params(0),
        cost_estimate=pl.CostEstimate(
            flops=16 * 10**9, bytes_accessed=40 * 2**20, transcendentals=8 * 10**6
        ),
        name="attention_forward",
    )(x, g, x, own_vec, wq, wk, wv, bqv, wd, lo, pad, alibi)


def mlp_kernel(
    a_own, a_par, xm, dy_s, vec, bup, wu0, wu1, wd0, wd1,
    mk_ref, ms_ref, gn_ref, h1_ref, gu_ref, su_ref, gd_ref, sd_ref, bs_ref, ru_ref,
    n2_s, n2t_s, dyt_s, dyo_s, am_s, ag_s, act_s, gp_s, us_s, s_u, r_u,
    *, bits, chunk,
):
    i = pl.program_id(0)
    core, y, ranks = place()
    partners = [{"dp": dp_partner(bit)} for bit in bits]

    def send_tile(n, kind):
        return remote(us_s.at[n], ru_ref.at[n], s_u.at[n], r_u.at[n], partners[kind])

    @pl.when(i == 0)
    def _():
        greet(partners)

        def assemble(rb, carry):
            rows = block_rows(rb)
            h1_ref[rows, :] = xm[rows, :].astype(F32)
            for part, a in ((core, a_own), (1 - core, a_par)):
                for half in range(2):
                    cols = feature_block(2 * half + part)
                    h1_ref[rows, cols] += a[rows, half * SHARE : (half + 1) * SHARE].astype(F32)
            value = h1_ref[rows, :] + vec[2:3, :]
            h1_ref[rows, :] = value
            mean, rstd = row_stats(value)
            n2 = ((value - mean) * rstd * vec[3:4, :] + vec[4:5, :]).astype(BF)
            n2_s[rows, :] = n2
            for source, turned, bit in (
                (n2_s, n2t_s, bits[0]), (dy_s, dyt_s, bits[0]), (dy_s, dyo_s, bits[1])
            ):
                for j in range(D // 256):
                    for side, cols in enumerate(piece(j, bit, chunk)):
                        to = slice(side * (D // 2) + j * 128, side * (D // 2) + (j + 1) * 128)
                        turned[to, rows] = source[rows, cols].T
            am_s[rows, :] = jnp.zeros((B, D), F32)
            ag_s[rows, :] = jnp.zeros((B, D), F32)
            return carry

        lax.fori_loop(0, OWN // B, assemble, 0)

    def tile(wu, wd, which):
        bias = bup[which : which + 1, pl.ds(pl.multiple_of(lax.rem(i, 2) * TILE, TILE), TILE)]
        scale = math.sqrt(2.0 / math.pi)

        def rows_of(rb, sums):
            rows = pl.ds(pl.multiple_of(rb * B, B), B)
            pre = dot(n2_s[rows, :], wu[...]) + bias
            back = dot_nt(dy_s[rows, :], wd[...])
            square = pre * pre
            th = jnp.tanh(scale * pre * (1.0 + 0.044715 * square))
            half = 0.5 * (1.0 + th)
            act = (pre * half).astype(BF)
            slope = half + 0.5 * pre * (1.0 - th * th) * (scale + (3 * 0.044715 * scale) * square)
            gp = (slope * back).astype(BF)
            act_s[rows, :] = act
            gp_s[rows, :] = gp
            am_s[rows, :] += dot(act, wd[...])
            ag_s[rows, :] += dot_nt(gp, wu[...])
            return sums + jnp.sum(gp.astype(F32), axis=0, keepdims=True)

        sums = lax.fori_loop(0, OWN // B, rows_of, jnp.zeros((1, TILE), F32))
        bs_ref[...] = jnp.broadcast_to(sums, bs_ref.shape)

        def grads(left, right, keep, send):
            keep[...] = dot(left[0 : D // 2, :], right[...]).astype(BF)
            send[...] = dot(left[D // 2 :, :], right[...]).astype(BF)

        first = which == 0
        grads(n2t_s, gp_s, gu_ref, us_s.at[i] if first else su_ref)
        if first:
            send_tile(i, 0).start()
        grads(dyo_s if first else dyt_s, act_s, gd_ref, us_s.at[2 + i] if first else sd_ref)
        if first:
            send_tile(2 + i, 1).start()

    pl.when(i < 2)(lambda: tile(wu0, wd0, 0))
    pl.when(i >= 2)(lambda: tile(wu1, wd1, 1))

    @pl.when(i == 3)
    def _():
        split_store(mk_ref, ms_ref, am_s, core)
        gn_ref[...] = ag_s[...].astype(BF)
        for n in range(4):
            send_tile(n, n // 2).wait()


def feed_forward(a_own, a_par, xm, dy, vec, bup, wu0, wd0, w_other, bits, chunk):
    whole = lambda shape: pl.BlockSpec(shape, lambda i: (0,) * len(shape))
    low = lambda i: jnp.minimum(i, 1)
    high = lambda i: jnp.maximum(i - 2, 0)
    like = jax.ShapeDtypeStruct
    tile = pl.BlockSpec((D // 2, TILE), lambda i: (0, i))
    return pl.pallas_call(
        functools.partial(mlp_kernel, bits=bits, chunk=chunk),
        grid=(4,),
        in_specs=[whole((OWN, D // 2))] * 2
        + [whole((OWN, D))] * 2
        + [
            whole((8, D)),
            whole((8, UNITS)),
            pl.BlockSpec((D, TILE), lambda i: (0, low(i))),
            pl.BlockSpec((D, TILE), lambda i: (0, high(i))),
            pl.BlockSpec((TILE, D), lambda i: (low(i), 0)),
            pl.BlockSpec((TILE, D), lambda i: (high(i), 1)),
        ],
        out_specs=[whole((OWN, D // 2))] * 2
        + [whole((OWN, D))] * 2
        + [
            tile,
            pl.BlockSpec((D // 2, TILE), lambda i: (0, high(i))),
            tile,
            pl.BlockSpec((D // 2, TILE), lambda i: (0, high(i))),
            pl.BlockSpec((8, TILE), lambda i: (0, i)),
            pl.BlockSpec(memory_space=pl.ANY),
        ],
        scratch_shapes=[
            pltpu.VMEM((OWN, D), BF),
            pltpu.VMEM((D, OWN), BF),
            pltpu.VMEM((D, OWN), BF),
            pltpu.VMEM((D, OWN), BF),
            pltpu.VMEM((OWN, D), F32),
            pltpu.VMEM((OWN, D), F32),
            pltpu.VMEM((OWN, TILE), BF),
            pltpu.VMEM((OWN, TILE), BF),
            pltpu.VMEM((4, D // 2, TILE), BF),
            pltpu.SemaphoreType.DMA((4,)),
            pltpu.SemaphoreType.DMA((4,)),
        ],
        out_shape=[like((OWN, D // 2), BF)] * 2
        + [
            like((OWN, D), BF),
            like((OWN, D), F32),
            like((D // 2, 2 * UNITS), BF),
            like((D // 2, UNITS), BF),
            like((D // 2, 2 * UNITS), BF),
            like((D // 2, UNITS), BF),
            like((8, 2 * UNITS), F32),
            like((4, D // 2, TILE), BF),
        ],
        compiler_params=remote_params(1),
        cost_estimate=pl.CostEstimate(
            flops=26 * 10**9, bytes_accessed=40 * 2**20, transcendentals=2 * 10**6
        ),
        name="feed_forward",
    )(a_own, a_par, xm, dy, vec, bup, wu0, w_other, wd0, w_other)


LEAD = 2
FINAL = 3
TILES = (("u", 0), ("u", 1), ("d", 0), ("d", 1), ("u", 2), ("d", 2), ("d", 3), ("u", 3), ("a", 0), ("a", 1))
OTHER_ORDER = (2, 3, 9)
FIRST = (0, 1, 0, 2, 3, 4, 6, 7)
USE = sorted(range(8), key=lambda p: (FIRST[p], p)) + [8, 9]
PAIRS = ((0, 4), (1, 7), (2, 5), (3, 6))
DRAIN = LEAD + FINAL + NB


def step_of(p, n):
    return FIRST[p] + 3 * (n - 1) if p < 8 else DRAIN + n - 1


def last_step(levels):
    return max(step_of(7, levels), step_of(8, levels))


def bwd_kernel(
    x0, x1, x2, x3, x_late, h1, gn, gn_any, mk, ms_any, dy_in, gu, gd, ru, su_any, sd_any, up_sums, hm,
    p_ref, q_ref, linv_ref, ctx_ref, k_ref, v_ref, vec, wq, wk, wv, wd,
    out_any, os_any, tg_ref, wu_ref, wdn_ref, wqk_ref, wvd_ref, vt_ref,
    w_s, gh_s, gm_s, gt_s, qt_s, dl_s, ds_s, res_s, dkt_s, dvt_s, acc_s,
    o_s, gn_got, mr_got, gh_own, gh_y, gh_f,
    part_keep, part_send, part_got, sum_keep, sum_send, sum_got, ghx_s, st_keep, st_got, st_sum, st_all,
    gk, ru_s, g1, y_send, y_got, cs_ref, bs_ref, n1_ref, v_keep, v_send, v_away, v_sum, v_got,
    *rest, orders, chunk,
):
    levels = len(orders[0])
    stages = [rest[3 * n : 3 * n + 3] for n in range(levels - 1)]
    (
        s_gn, r_gn, s_mr, r_mr, s_gy, r_gy, s_gf, r_gf, s_pc, r_pc, s_sy, r_sy,
        s_tc, r_tc, s_ty, r_ty, s_g1, r_g1, s_yy, r_yy, l_g, l_r, s_gw, r_gw, s_va, r_va, s_vt, r_vt, l_o, s_o, r_o, *g_sems,
    ) = rest[3 * (levels - 1) :]
    step = pl.program_id(0)
    b = NB - 1 - (step - LEAD)
    core, y, ranks = place()
    beside, across = {"tensor": ranks[1]}, {"tensor": ranks[2]}
    order_of = lambda p: orders[1 if p in OTHER_ORDER else 0]
    partner = lambda bit: {"dp": dp_partner(bit)}
    half = NB // 2
    last = last_step(levels)
    lanes = head_of_lane((B, SHARE))

    send_gn = lambda j: remote(gn_any.at[block_rows(j)], gn_got.at[j], s_gn.at[j], r_gn.at[j], beside)
    send_mr = lambda j: remote(ms_any.at[block_rows(j)], mr_got.at[j], s_mr.at[j], r_mr.at[j], beside)
    send_gy = lambda j, side: remote(
        gh_own.at[j, :, feature_block(2 * side + core)],
        gh_y.at[j, :, side * SHARE : (side + 1) * SHARE],
        s_gy.at[2 * j + side], r_gy.at[2 * j + side], across,
    )
    send_gf = lambda j: remote(gh_y.at[j], gh_f.at[j], s_gf.at[j], r_gf.at[j], beside)
    store_out = lambda j, side: pltpu.make_async_copy(
        o_s.at[lax.rem(j, 2), side],
        (out_any.at[block_rows(2 * j + y)], os_any.at[block_rows(j)])[side],
        l_o.at[2 * lax.rem(j, 2) + side],
    )
    send_out = lambda j: remote(
        os_any.at[block_rows(j)], out_any.at[block_rows(2 * j + y)], s_o.at[j], r_o.at[j], across
    )
    send_part = lambda n: remote(part_send.at[lax.rem(n, 3)], part_got.at[n], s_pc.at[n], r_pc.at[n], beside)
    send_sum = lambda n: remote(sum_send.at[n], sum_got.at[n], s_sy.at[n], r_sy.at[n], across)
    send_tc = lambda n: remote(st_keep.at[n], st_got.at[n], s_tc.at[n], r_tc.at[n], beside)
    send_ty = lambda n: remote(st_sum.at[n], st_all.at[n], s_ty.at[n], r_ty.at[n], across)

    def tile_of(p):
        kind, n = TILES[p]
        return slice(n * TILE, (n + 1) * TILE), kind == "u"

    def send_first(p):
        cols, up = tile_of(p)
        src = (su_any if up else sd_any).at[:, slice(cols.start - UNITS, cols.stop - UNITS)]
        return remote(src, g1.at[p - 4], s_g1.at[p - 4], r_g1.at[p - 4], partner(order_of(p)[0]))

    def send_weights(p, part):
        n = 2 * (p - 8) + part
        return remote(
            gn_got.at[p - 8, :, slice(part * TILE, (part + 1) * TILE)], g1.at[p - 4, block_rows(part)],
            s_gw.at[n], r_gw.at[n], partner(order_of(p)[0]),
        )

    slot = [USE.index(p) % 2 for p in range(10)]

    def load_keep(p):
        cols, up = tile_of(p)
        return pltpu.make_async_copy((gu if up else gd).at[:, cols], gk.at[slot[p]], l_g.at[slot[p]])

    def load_got(p):
        return pltpu.make_async_copy(ru.at[p], ru_s.at[slot[p]], l_r.at[slot[p]])

    def send_stage(p, n):
        _, send, got = stages[n - 1]
        return remote(
            send.at[p % 4], got.at[p], g_sems[2 * n - 2].at[p], g_sems[2 * n - 1].at[p], partner(order_of(p)[n])
        )

    send_last = lambda n: remote(y_send.at[n], y_got.at[n], s_yy.at[n], r_yy.at[n], across)

    def split(p, n):
        order = order_of(p)
        if n == 1:
            keep = lambda rows: gk[slot[p], rows, :]
            if p < 4:
                load_got(p).wait()
                got = lambda rows: ru_s[slot[p], rows, :]
            else:
                got = lambda rows: g1[p - 4, rows, :]
            if p < 8:
                load_keep(p).wait()
            if 4 <= p < 8:
                send_first(p).wait_recv()
            if p >= 8:
                send_weights(p, 0).wait_recv()
                send_weights(p, 1).wait_recv()
        else:
            send_stage(p, n - 1).wait_recv()
            keep = lambda rows: stages[n - 2][0][p % 4, rows, :]
            got = lambda rows: stages[n - 2][2][p, rows, :]
        size = D >> n
        following = order[n]
        inner = chunk
        for other in order[n + 1 :]:
            inner *= 2 if other < following else 1
        mine = dp_bit(following)
        if p >= 4:
            send_stage(p - 4, n).wait_send()
        for group in range(size // (2 * inner)):
            to = slice(group * inner, (group + 1) * inner)
            for side, ref in ((mine, stages[n - 1][0]), (1 - mine, stages[n - 1][1])):
                rows = pl.ds(pl.multiple_of(group * 2 * inner + side * inner, inner), inner)
                ref[p % 4, to, :] = (keep(rows).astype(F32) + got(rows).astype(F32)).astype(BF)
        send_stage(p, n).start()

    def whole_tile(p):
        send_stage(p, levels - 1).wait_recv()
        keep, _, got = stages[levels - 2]
        total = keep[p % 4].astype(F32) + got[p].astype(F32)
        if p >= 8:
            (wqk_ref, wvd_ref)[p - 8][...] = total
        for n, (own, other) in enumerate(PAIRS):
            cols, up = tile_of(own)
            if p == own:
                (wu_ref if up else wdn_ref)[:, cols] = total
            if p == other:
                y_send[n] = total.astype(BF)
                send_last(n).start()

    def close(n):
        cols, up = tile_of(PAIRS[n][0])
        send_last(n).wait_recv()
        (wu_ref if up else wdn_ref)[:, cols] += y_got[n].astype(F32)

    @pl.when(step == 0)
    def _():
        greet([beside, across] + [partner(bit) for bit in orders[0]])
        for j in range(half - 1, -1, -1):
            send_gn(j).start()
            send_mr(j).start()
        for p in range(4, 8):
            send_first(p).start()
        for p in USE[:2]:
            load_keep(p).start()
            load_got(p).start()
        cs_ref[...] = jnp.zeros(cs_ref.shape, F32)
        bs_ref[...] = jnp.zeros(bs_ref.shape, F32)
        n1_ref[...] = jnp.zeros(n1_ref.shape, F32)
        dkt_s[...] = jnp.zeros(dkt_s.shape, F32)
        dvt_s[...] = jnp.zeros(dvt_s.shape, F32)
        acc_s[...] = jnp.zeros(acc_s.shape, F32)

    @pl.when(step < half)
    def _():
        j = half - 1 - step
        send_gn(j).wait_recv()
        send_mr(j).wait_recv()
        dy = dy_in[...].astype(F32)
        value = h1[...]

        def out(side):
            part = pl.ds(pl.multiple_of(side * SHARE, SHARE), SHARE)
            cols = feature_block(2 * side + core)
            total = mk[:, part].astype(F32) + mr_got[j, :, part].astype(F32)
            return (h1[:, cols] + total + vec[5:6, cols]).astype(BF)


        @pl.when(step >= 2)
        def _():
            for side in range(2):
                store_out(j + 2, side).wait()

        for side, which in enumerate((y, 1 - y)):
            o_s[lax.rem(j, 2), side] = out(which)
            store_out(j, side).start()
        mean, rstd = row_stats(value)
        xhat = (value - mean) * rstd
        grad = gn[...].astype(F32) + gn_got[j].astype(F32)
        scaled = grad * vec[3:4, :]
        first = jnp.sum(scaled, axis=1, keepdims=True) / D
        second = jnp.sum(scaled * xhat, axis=1, keepdims=True) / D
        gh = dy + rstd * (scaled - first - xhat * second)
        for n, columns in enumerate((grad * xhat, grad, gh, dy)):
            cs_ref[n : n + 1, :] += jnp.sum(columns, axis=0, keepdims=True)
        gh_own[j] = gh.astype(BF)
        send_gy(j, 0).start()
        send_gy(j, 1).start()

    @pl.when((step >= LEAD) & (step < LEAD + NB))
    def _():
        j = b // 2

        @pl.when(lax.rem(b, 2) == y)
        def _():
            gh_s[...] = gh_own[j]

        @pl.when(lax.rem(b, 2) != y)
        def _():
            send_gf(j).wait_recv()
            for part, ref in ((core, gh_y), (1 - core, gh_f)):
                for side in range(2):
                    gh_s[:, feature_block(2 * side + part)] = ref[j, :, side * SHARE : (side + 1) * SHARE]

        gc = dot_nt(gh_s[...], wd[...]).astype(BF).astype(F32)
        scaled = gc * linv_ref[...]
        gcs = scaled.astype(BF)
        product = scaled * ctx_ref[...].astype(F32)
        qt_s[...] = q_ref[...].T.reshape(LH, HD, B)
        gt_s[...] = gcs.T.reshape(LH, HD, B)
        for h in range(LH):
            gm_s[h] = jnp.where(lanes == h, gcs, jnp.zeros_like(gcs))
            delta = jnp.sum(jnp.where(lanes == h, product, 0.0), axis=1, keepdims=True)
            dl_s[h] = jnp.broadcast_to(delta, (B, 128))

    def attend(nb):
        start = pl.multiple_of((b + 1 - nb) * B, B)

        def head(h, carry):
            gm = gm_s[h]
            delta = jnp.concatenate([dl_s[h]] * 2, axis=1)
            for r in range(nb):
                slot = SLOTS - nb + r
                cols = slice(slot * B, (slot + 1) * B)
                dp = dot_nt(gm, v_ref[pl.ds(pl.multiple_of(start + r * B, B), B), :])
                ds_s[:, cols] = (p_ref[h, :, cols].astype(F32) * (dp - delta)).astype(BF)
            live = slice((SLOTS - nb) * B, STRIP)
            keys = pl.ds(start, nb * B)
            res_s[h] = dot(ds_s[:, live], k_ref[keys, :])
            dkt_s[h, :, keys] += dot(qt_s[h], ds_s[:, live])
            dvt_s[h, :, keys] += dot(gt_s[h], p_ref[h, :, live])
            return carry

        lax.fori_loop(0, LH, head, 0, unroll=2)

    pl.when((step >= LEAD) & (b >= SLOTS - 1))(functools.partial(attend, SLOTS))
    for nb in range(SLOTS - 1, 0, -1):
        pl.when(b == nb - 1)(functools.partial(attend, nb))

    @pl.when((step >= LEAD) & (step < LEAD + NB))
    def _():
        dq = res_s[0]
        for h in range(1, LH):
            dq = jnp.where(lanes == h, res_s[h], dq)
        dq = (dq * (1.0 / math.sqrt(HD))).astype(BF)
        here = block_rows(b)
        dk = dkt_s[:, :, here].reshape(SHARE, B).astype(BF).T
        dv = dvt_s[:, :, here].reshape(SHARE, B).astype(BF).T
        bs_ref[0:1, :] += jnp.sum(dq.astype(F32), axis=0, keepdims=True)
        bs_ref[1:2, :] += jnp.sum(dv.astype(F32), axis=0, keepdims=True)

        for rank, x in zip(ranks, (x0, x1, x2, x3)):
            w_s[:, feature_block(rank)] = x[...].astype(F32)
        value = w_s[...]
        mean, rstd = row_stats(value)
        xhat = (value - mean) * rstd
        n1t = (xhat * vec[0:1, :] + vec[1:2, :]).astype(BF).T
        acc_s[:, 0:SHARE] += dot(n1t, dq)
        acc_s[:, SHARE : 2 * SHARE] += dot(n1t, dk)
        acc_s[:, 2 * SHARE : 3 * SHARE] += dot(n1t, dv)
        acc_s[:, 3 * SHARE :] += dot(gh_s[...].T, ctx_ref[...])

        grad = dot_nt(dq, wq[...]) + dot_nt(dk, wk[...]) + dot_nt(dv, wv[...])
        scaled = grad * vec[0:1, :]
        first = jnp.sum(scaled, axis=1, keepdims=True)
        second = jnp.sum(scaled * xhat, axis=1, keepdims=True)
        column = lax.broadcasted_iota(jnp.int32, (B, 128), 1)
        packed = jnp.where(
            column == 0, first, jnp.where(column == 1, second, jnp.where(column == 2, mean, rstd))
        )
        st_keep[b] = packed.T[0:8, :]
        send_tc(b).start()
        w_s[...] = grad

        @pl.when(step >= LEAD + 3)
        def _():
            send_part(b + 3).wait_send()

        for n, side in enumerate((y, 1 - y)):
            cols = slice(n * SHARE, (n + 1) * SHARE)
            part_keep[lax.rem(b, 2), :, cols] = w_s[:, feature_block(2 * side + core)].astype(BF)
            part_send[lax.rem(b, 3), :, cols] = w_s[:, feature_block(2 * side + 1 - core)].astype(BF)
        send_part(b).start()
        ghx_s[lax.rem(b, 4)] = gh_s[:, feature_block(ranks[0])]

    @pl.when(step == LEAD + NB - 1)
    def _():
        for p in (8, 9):
            cols = slice((p - 8) * TILE, (p - 7) * TILE)
            for j in range(D // 256):
                mine, other = piece(j, order_of(p)[0], chunk)
                gk[slot[p], j * 128 : (j + 1) * 128, :] = acc_s[mine, cols].astype(BF)
                into = slice(j // 2 * TILE, (j // 2 + 1) * TILE)
                gn_got[p - 8, j % 2 * 128 : (j % 2 + 1) * 128, into] = acc_s[other, cols].astype(BF)
            for part in range(2):
                send_weights(p, part).start()
        for j in range(half):
            send_out(j).start()

    send_away = lambda: remote(v_send, v_away, s_va.at[0], r_va.at[0], across)
    send_total = lambda n: remote(
        v_sum.at[n], v_got.at[n], s_vt.at[n], r_vt.at[n], partner(orders[0][n])
    )

    @pl.when(step == half)
    def _():
        for j in range(2):
            for side in range(2):
                store_out(j, side).wait()
        for ref, rank, side in ((v_keep, ranks[0], 0), (v_send, ranks[2], UNITS)):
            ref[0:4, :] = cs_ref[0:4, feature_block(rank)]
            for n in range(4):
                ref[4 + n : 5 + n, :] = up_sums[0:1, side + n * SHARE : side + (n + 1) * SHARE]
        send_away().start()

    @pl.when(step == half + 4)
    def _():
        send_away().wait_recv()
        v_sum[0, 0:8, :] = v_keep[...] + v_away[...]

    @pl.when((step >= LEAD + 1) & (step < LEAD + 1 + NB))
    def _():
        n = b + 1
        send_part(n).wait_recv()
        send_tc(n).wait_recv()
        keep = part_keep[lax.rem(n, 2)].astype(F32)
        sum_keep[lax.rem(n, 3)] = keep[:, :SHARE] + part_got[n, :, :SHARE].astype(F32)
        sum_send[n] = (keep[:, SHARE:] + part_got[n, :, SHARE:].astype(F32)).astype(BF)
        st_sum[n] = st_keep[n] + st_got[n]
        send_sum(n).start()
        send_ty(n).start()

    @pl.when((step >= LEAD + FINAL) & (step < LEAD + FINAL + NB))
    def _():
        n = b + FINAL
        send_sum(n).wait_recv()
        send_ty(n).wait_recv()
        grad = sum_keep[lax.rem(n, 3)] + sum_got[n].astype(F32)
        row = lax.broadcasted_iota(jnp.int32, (8, B), 0)
        stats = jnp.where(row < 2, st_sum[n] + st_all[n], st_keep[n])
        stats = jnp.concatenate([stats] * 16, axis=0).T
        xhat = (x_late[...].astype(F32) - stats[:, 2:3]) * stats[:, 3:4]
        scaled = grad * vec[0:1, feature_block(ranks[0])]
        inner = scaled - stats[:, 0:1] / D - xhat * (stats[:, 1:2] / D)
        tg_ref[...] = ghx_s[lax.rem(n, 4)].astype(F32) + stats[:, 3:4] * inner
        n1_ref[0:1, :] += jnp.sum(grad * xhat, axis=0, keepdims=True)
        n1_ref[1:2, :] += jnp.sum(grad, axis=0, keepdims=True)

    row16 = lax.broadcasted_iota(jnp.int32, (16, SHARE), 0)

    @pl.when(step == DRAIN - 1)
    def _():
        v_sum[0, 8:10, :] = n1_ref[0:2, :]
        v_sum[0, 10:12, :] = bs_ref[0:2, :]
        lane = lax.broadcasted_iota(jnp.int32, (4, SHARE), 1)
        top = jnp.full((4, SHARE), NEG, F32)
        for h in range(LH):
            top = jnp.where(lane == h, jnp.max(hm[h]), top)
        v_sum[0, 12:16, :] = top
        send_total(0).start()

    for n in range(levels):

        @pl.when(step == DRAIN + n)
        def _():
            send_total(n).wait_recv()
            mine, other = v_sum[n], v_got[n]
            total = jnp.where(row16 < 12, mine + other, jnp.maximum(mine, other))
            if n == levels - 1:
                vt_ref[...] = total
            else:
                v_sum[n + 1] = total
                send_total(n + 1).start()

    for j in range(half - 1, -1, -1):

        @pl.when(step == half - j)
        def _():
            send_gy(j, 0).wait_recv()
            send_gy(j, 1).wait_recv()
            send_gf(j).start()

    for p in range(10):
        for n in range(1, levels):
            pl.when(step == step_of(p, n))(functools.partial(split, p, n))
        pl.when(step == step_of(p, levels))(functools.partial(whole_tile, p))

    def load_next(p):
        load_keep(p).start()
        if p < 4:
            load_got(p).start()

    for n in range(2, 8):
        pl.when(step == FIRST[USE[n - 2]])(functools.partial(load_next, USE[n]))

    @pl.when(step == last)
    def _():
        for j in range(half):
            close(j)
            send_out(j).wait()
            for copy in (send_gn, send_mr, send_gf, send_last):
                copy(j).wait_send()
            for side in range(2):
                send_gy(j, side).wait_send()
            for level in range(1, levels):
                send_stage(6 + j, level).wait_send()
        for n in range(NB):
            for copy in (send_sum, send_tc, send_ty):
                copy(n).wait_send()
        for n in range(3):
            send_part(n).wait_send()
        for p in range(4, 8):
            send_first(p).wait_send()
        for p in (8, 9):
            for part in range(2):
                send_weights(p, part).wait_send()
        send_away().wait_send()
        for n in range(levels):
            send_total(n).wait_send()


def attention_backward(
    xs, h1, gn, mk, ms, dy, gu, gd, ru, su, sd, up_sums, hm, p, q, linv, ctx, k, v, vec, wq, wk, wv, wd,
    orders, chunk,
):
    levels = len(orders[0])
    half = NB // 2
    block = lambda s: jnp.clip(NB - 1 + LEAD - s, 0, NB - 1)
    late = lambda s: jnp.clip(NB - 1 + LEAD + FINAL - s, 0, NB - 1)
    row = lambda width: pl.BlockSpec((B, width), lambda s: (block(s), 0))
    own = lambda width: pl.BlockSpec((B, width), lambda s: (jnp.maximum(half - 1 - s, 0), 0))
    once = pl.Buffered(1)
    whole = lambda *shape: pl.BlockSpec(shape, lambda s: (0,) * len(shape), pipeline_mode=once)
    anywhere = pl.BlockSpec(memory_space=pl.ANY)
    like = jax.ShapeDtypeStruct
    vmem = lambda *shape, dtype=BF: pltpu.VMEM(shape, dtype)
    dma = lambda n: pltpu.SemaphoreType.DMA((n,))
    final_late = pl.BlockSpec((B, SHARE), lambda s: (late(s), 0))
    return pl.pallas_call(
        functools.partial(bwd_kernel, orders=orders, chunk=chunk),
        grid=(last_step(levels) + 1,),
        in_specs=[row(SHARE)] * 4
        + [final_late, own(D), own(D), anywhere, own(D // 2), anywhere]
        + [own(D)]
        + [anywhere] * 2
        + [anywhere] * 3
        + [whole(8, 2 * UNITS), whole(LH, 8, B)]
        + [pl.BlockSpec((LH, B, STRIP), lambda s: (0, block(s), 0))]
        + [row(SHARE)] * 3
        + [whole(SEQ, SHARE)] * 2
        + [whole(8, D)]
        + [whole(D, SHARE)] * 3
        + [whole(SHARE, D)],
        out_specs=[anywhere, anywhere, final_late]
        + [whole(chunk, UNITS)] * 2
        + [whole(chunk, TILE)] * 2
        + [whole(16, SHARE)],
        scratch_shapes=[
            vmem(B, D, dtype=F32),
            vmem(B, D),
            vmem(LH, B, SHARE),
            vmem(LH, HD, B),
            vmem(LH, HD, B),
            vmem(LH, B, 128, dtype=F32),
            vmem(B, STRIP),
            vmem(LH, B, SHARE, dtype=F32),
            vmem(LH, HD, SEQ, dtype=F32),
            vmem(LH, HD, SEQ, dtype=F32),
            vmem(D, 4 * SHARE, dtype=F32),
            vmem(2, 2, B, SHARE),
            vmem(half, B, D),
            vmem(half, B, D // 2),
            vmem(half, B, D),
            vmem(half, B, D // 2),
            vmem(half, B, D // 2),
            vmem(2, B, D // 2),
            vmem(3, B, D // 2),
            vmem(NB, B, D // 2),
            vmem(3, B, SHARE, dtype=F32),
            vmem(NB, B, SHARE),
            vmem(NB, B, SHARE),
            vmem(4, B, SHARE),
            vmem(NB, 8, B, dtype=F32),
            vmem(NB, 8, B, dtype=F32),
            vmem(NB, 8, B, dtype=F32),
            vmem(NB, 8, B, dtype=F32),
            vmem(2, D // 2, TILE),
            vmem(2, D // 2, TILE),
            vmem(6, D // 2, TILE),
            vmem(half, chunk, TILE),
            vmem(half, chunk, TILE),
            vmem(8, D, dtype=F32),
            vmem(8, SHARE, dtype=F32),
            vmem(8, SHARE, dtype=F32),
            vmem(8, SHARE, dtype=F32),
            vmem(8, SHARE, dtype=F32),
            vmem(8, SHARE, dtype=F32),
            vmem(levels, 16, SHARE, dtype=F32),
            vmem(levels, 16, SHARE, dtype=F32),
        ]
        + [vmem(slots, D >> (n + 1), TILE) for n in range(1, levels) for slots in (4, 4, 10)]
        + [dma(half)] * 4
        + [dma(NB)] * 2
        + [dma(half)] * 2
        + [dma(NB)] * 8
        + [dma(4)] * 2
        + [dma(half)] * 2
        + [dma(2)] * 2
        + [dma(4)] * 2
        + [dma(1)] * 2
        + [dma(levels)] * 2
        + [dma(half)] * 3
        + [dma(10)] * (2 * (levels - 1)),
        out_shape=[like((SEQ, SHARE), BF), like((OWN, SHARE), BF)]
        + [like((SEQ, SHARE), F32)]
        + [like((chunk, UNITS), F32)] * 2
        + [like((chunk, TILE), F32)] * 2
        + [like((16, SHARE), F32)],
        compiler_params=remote_params(2),
        cost_estimate=pl.CostEstimate(
            flops=30 * 10**9, bytes_accessed=50 * 2**20, transcendentals=0
        ),
        name="backward",
    )(
        *xs, xs[0], h1, gn, gn, mk, ms, dy, gu, gd, ru, su, sd, up_sums, hm, p, q, linv, ctx, k, v, vec, wq, wk, wv, wd
    )


def swap(value, axis, bit):
    size = lax.axis_size(axis)
    return lax.ppermute(value, axis, [(i, i ^ bit) for i in range(size)])


def dp_bits():
    bits, bit = [], 1
    while bit < lax.axis_size("dp"):
        bits.append(bit)
        bit *= 2
    return bits


def pick(value, axis, index):
    return lax.dynamic_index_in_dim(value, index, axis, keepdims=False)


def shards(
    tokens,
    out_grad,
    segments,
    padding,
    norm1_gain,
    norm1_bias,
    w_query,
    b_query,
    w_key,
    w_value,
    b_value,
    w_dense,
    dense_bias,
    norm2_gain,
    norm2_bias,
    w_up,
    b_up,
    w_down,
    down_bias,
):
    t = lax.axis_index("tensor")
    rank = lax.axis_index("dp")
    size = lax.axis_size("dp")
    core, y = t % 2, t // 2
    core_swap = lambda value: swap(value, "tensor", 1)
    y_swap = lambda value: swap(value, "tensor", 2)
    rows8 = lambda value: jnp.pad(value, ((0, 8 - value.shape[0]), (0, 0)))

    own_vec = jnp.concatenate(
        [
            jnp.stack([norm1_gain, norm1_bias, dense_bias, norm2_gain, norm2_bias, down_bias, down_bias, down_bias]),
            b_up.reshape(4, SHARE),
            b_up.reshape(4, SHARE),
        ]
    ).astype(F32)

    part = D // size
    cut = lambda w: lax.dynamic_slice_in_dim(w, rank * part, part, 0)
    w_part = y_swap(jnp.concatenate([cut(w_up), cut(w_down)], axis=1))
    seg = segments.reshape(SEQ)
    index = jnp.arange(SEQ, dtype=jnp.int32)
    first = jnp.zeros((SEQ,), jnp.int32)
    for value in range(1, 4):
        first = jnp.where(seg == value, jnp.sum((seg < value).astype(jnp.int32)), first)
    lowest = jnp.maximum(first, index - (WIN - 1))
    pad_row = rows8(jnp.where(padding.reshape(1, SEQ) == 1, 0.0, NEG).astype(F32))
    heads = t * LH + jnp.arange(LH)
    slopes = jnp.exp2(-8.0 * (heads.astype(F32) + 1.0) / HEADS)
    alibi = rows8(slopes[:, None] * (jnp.arange(STRIP) - (STRIP - 1)).astype(F32)[None, :])

    b_qv = rows8(jnp.stack([b_query, b_value]).astype(F32))
    lows = lowest.reshape(SEQ, 1)
    w_part, own_vec, b_qv, lows, pad_row, alibi = lax.optimization_barrier(
        (w_part, own_vec, b_qv, lows, pad_row, alibi)
    )
    w_other = lax.all_gather(w_part, "dp", axis=0, tiled=True)

    p, q, k, v, linv, ctx, a_own, a_par, x1, x2, x3, xm, hm, vec, b_up_pair, dy = attention_forward(
        tokens, out_grad, own_vec, w_query, w_key, w_value,
        b_qv, w_dense, lows, pad_row, alibi,
    )
    xs = [tokens, x1, x2, x3]

    bits = dp_bits()
    order_a = bits if size == 8 else bits[::-1]
    order_b = [2, 4, 1] if size == 8 else [bits[-2], bits[-1], *bits[:-2][::-1]]
    mk, ms, gn, h1, gu, su, gd, sd, up_sums, ru = feed_forward(
        a_own, a_par, xm, dy, vec, b_up_pair, w_up, w_down, w_other, (order_a[0], order_b[0]), part
    )
    output, _, tokens_grad, w_up_grad, w_down_grad, g_qk, g_vd, sums = attention_backward(
        xs, h1, gn, mk, ms, dy, gu, gd, ru, su, sd, up_sums, hm, p, q, linv, ctx, k, v, vec,
        w_query, w_key, w_value, w_dense, (order_a, order_b), part,
    )
    w_down_grad = w_down_grad.T
    head_max = sums[12, :LH]
    column_scale = jnp.repeat(jnp.sqrt(TAU / jnp.maximum(head_max, TAU)), HD)
    return (
        output,
        tokens_grad,
        sums[8],
        sums[9],
        g_qk[:, :SHARE],
        sums[10],
        g_qk[:, SHARE:],
        g_vd[:, :SHARE],
        sums[11],
        g_vd[:, SHARE:].T,
        sums[2],
        sums[0],
        sums[1],
        w_up_grad,
        sums[4:8].reshape(UNITS),
        w_down_grad,
        sums[3],
        head_max,
        w_query.astype(F32) * column_scale,
        b_query.astype(F32) * column_scale,
        w_key.astype(F32) * column_scale,
    )


def solution(mesh):
    in_specs = (
        P("dp", "tensor"),
        P("dp", "tensor"),
        P("dp", None),
        P("dp", None),
        P("tensor"),
        P("tensor"),
        P(None, "tensor"),
        P("tensor"),
        P(None, "tensor"),
        P(None, "tensor"),
        P("tensor"),
        P("tensor", None),
        P("tensor"),
        P("tensor"),
        P("tensor"),
        P(None, "tensor"),
        P("tensor"),
        P("tensor", None),
        P("tensor"),
    )
    out_specs = (
        P("dp", "tensor"),
        P("dp", "tensor"),
        P("tensor"),
        P("tensor"),
        P("dp", "tensor"),
        P("tensor"),
        P("dp", "tensor"),
        P("dp", "tensor"),
        P("tensor"),
        P("tensor", "dp"),
        P("tensor"),
        P("tensor"),
        P("tensor"),
        P("dp", "tensor"),
        P("tensor"),
        P("tensor", "dp"),
        P("tensor"),
        P("tensor"),
        P(None, "tensor"),
        P("tensor"),
        P(None, "tensor"),
    )
    return jax.shard_map(shards, mesh=mesh, in_specs=in_specs, out_specs=out_specs, check_vma=False)
```

```python
import functools
import math

import jax
import jax.numpy as jnp
from jax import lax
from jax.experimental import pallas as pl
from jax.experimental.pallas import tpu as pltpu
from jax.sharding import PartitionSpec as P

HEADS = 16
HD = 64
WIN = 1024
D = 1024
FF = 4096
SEQ = 2048
B = 256
NB = SEQ // B
SLOTS = WIN // B + 1
STRIP = SLOTS * B
LH = 4
SHARE = LH * HD
UNITS = FF // 4
TILE = 512
OWN = SEQ // 2

EPS = 1e-05
TAU = 2.0
NEG = -1e30
F32 = jnp.float32
BF = jnp.bfloat16
VMEM_LIMIT = 62 * 2**20


def dot(a, b):
    return jnp.dot(a, b, preferred_element_type=F32)


def dot_nt(a, b):
    return lax.dot_general(a, b, (((1,), (1,)), ((), ())), preferred_element_type=F32)


def params():
    return pltpu.CompilerParams(
        dimension_semantics=("arbitrary",), vmem_limit_bytes=VMEM_LIMIT
    )


def feature_block(rank):
    return pl.ds(pl.multiple_of(rank * SHARE, SHARE), SHARE)


def head_of_lane(shape):
    return lax.broadcasted_iota(jnp.int32, shape, 1) // HD


def ordered(kernel, count):
    return lambda ids, *refs: kernel(ids, *refs[count:])


def waits(after):
    return [pl.BlockSpec(memory_space=pl.ANY)] * len(after)


def row_stats(rows):
    mean = jnp.sum(rows, axis=1, keepdims=True) / D
    square = jnp.sum(rows * rows, axis=1, keepdims=True) / D
    return mean, lax.rsqrt(square - mean * mean + EPS)


def piece(j, bit, chunk):
    inner = bit * chunk
    mine = dp_bit(bit)
    base = (j * 128) // inner * (2 * inner) + (j * 128) % inner
    return [
        pl.ds(pl.multiple_of(base + side * inner, 128), 128) for side in (mine, 1 - mine)
    ]


def dp_bit(bit):
    return lax.rem(lax.div(lax.axis_index("dp"), bit), 2)


def dp_partner(bit):
    return lax.axis_index("dp") + bit - 2 * bit * dp_bit(bit)


def place():
    t = lax.axis_index("tensor")
    core, y = lax.rem(t, 2), lax.div(t, 2)
    return core, y, (t, 2 * y + 1 - core, 2 * (1 - y) + core, 2 * (1 - y) + 1 - core)


def remote(src, dst, send, got, where):
    return pltpu.make_async_remote_copy(
        src_ref=src, dst_ref=dst, send_sem=send, recv_sem=got,
        device_id=where, device_id_type=pl.DeviceIdType.MESH,
    )


def greet(places):
    barrier = pltpu.get_barrier_semaphore()
    for where in places:
        pl.semaphore_signal(
            barrier, inc=1, device_id=where, device_id_type=pl.DeviceIdType.MESH
        )
    pl.semaphore_wait(barrier, len(places))


def block_rows(b):
    return pl.ds(pl.multiple_of(b * B, B), B)


def remote_params(collective_id):
    return pltpu.CompilerParams(
        dimension_semantics=("arbitrary",),
        vmem_limit_bytes=VMEM_LIMIT,
        collective_id=collective_id,
        has_side_effects=True,
    )


def split_store(keep_ref, send_ref, value_ref, core):
    for half in range(2):
        cols = slice(half * SHARE, (half + 1) * SHARE)
        keep_ref[:, cols] = value_ref[:, feature_block(2 * half + core)].astype(keep_ref.dtype)
        send_ref[:, cols] = value_ref[:, feature_block(2 * half + 1 - core)].astype(
            send_ref.dtype
        )


TAIL = 3


def fwd_kernel(
    x_any, g_any, x_own, own_vec, wq, wk, wv, bqv, wd, lo, pad, alibi,
    p_ref, q_ref, k_ref, v_ref, linv_ref, ctx_ref, a_ref, b_ref, x1_ref, x2_ref, x3_ref, xm_ref, hm_ref, vec, bup_ref, dy_any,
    xs, qm_s, k_s, va_s, u_s, res_s, lo_s,
    xc, xy, xf, part_keep, part_send, part_got, sum_keep, sum_send, sum_got, whole_own, whole_got,
    v_all,
    s_xc, r_xc, s_xy, r_xy, s_xf, r_xf, s_pc, r_pc, s_sy, r_sy, s_wc, r_wc,
    s_v, r_v, l_d, s_dc, r_dc, s_dy, r_dy, s_df, r_df,
):
    step = pl.program_id(0)
    core, y, ranks = place()

    rows = block_rows
    beside, across = {"tensor": ranks[1]}, {"tensor": ranks[2]}

    def to_core(b):
        return remote(x_any.at[rows(b)], xc.at[b], s_xc.at[b], r_xc.at[b], beside)

    def to_y(b):
        return remote(x_any.at[rows(b)], xy.at[b], s_xy.at[b], r_xy.at[b], across)

    def forward(b):
        return remote(xy.at[b], xf.at[b], s_xf.at[b], r_xf.at[b], beside)

    def part_to_core(b):
        return remote(part_send.at[b], part_got.at[b], s_pc.at[b], r_pc.at[b], beside)

    def sum_to_y(j):
        return remote(sum_send.at[j], sum_got.at[j], s_sy.at[j], r_sy.at[j], across)

    def whole_to_core(j):
        return remote(whole_own.at[j], whole_got.at[j], s_wc.at[j], r_wc.at[j], beside)

    def vectors(r):
        return remote(v_all.at[0], v_all.at[r], s_v.at[r - 1], r_v.at[r - 1], {"tensor": ranks[r]})

    mine = feature_block(ranks[0])

    def dy_own(j):
        return pltpu.make_async_copy(g_any.at[rows(2 * j + y)], dy_any.at[rows(j), mine], l_d.at[j])

    def dy_core(j):
        return remote(g_any.at[rows(2 * j + y)], dy_any.at[rows(j), mine], s_dc.at[j], r_dc.at[j], beside)

    def dy_y(j):
        return remote(g_any.at[rows(2 * j + 1 - y)], dy_any.at[rows(j), mine], s_dy.at[j], r_dy.at[j], across)

    def dy_forward(j):
        block = dy_any.at[rows(j), feature_block(ranks[2])]
        return remote(block, block, s_df.at[j], r_df.at[j], beside)

    @pl.when(step == 0)
    def _():
        v_all[0] = own_vec[...]
        greet((beside, across, {"tensor": ranks[3]}))
        for r in range(1, 4):
            vectors(r).start()
        for b in range(5):
            to_y(b).start()
            to_core(b).start()
        for r in range(1, 4):
            vectors(r).wait_recv()
        for r in range(4):
            vec[:, feature_block(ranks[r])] = v_all[r, 0:8, :]
        bup_ref[...] = jnp.zeros(bup_ref.shape, F32)
        for n, r in enumerate((0, 2)):
            for part in range(4):
                bup_ref[n : n + 1, part * SHARE : (part + 1) * SHARE] = v_all[r, 8 + part : 9 + part, :]
        to_y(0).wait_recv()
        forward(0).start()
        hm_ref[...] = jnp.full(hm_ref.shape, NEG, F32)

    for b in range(5, NB):

        @pl.when(step == b - 4)
        def _():
            to_y(b).start()
            to_core(b).start()

    row_i = lax.broadcasted_iota(jnp.int32, (B, B), 0)
    col_i = lax.broadcasted_iota(jnp.int32, (B, B), 1)
    lanes = head_of_lane((B, SHARE))

    for j in range(NB // 2):

        @pl.when(step == j + 4)
        def _():
            dy_own(j).start()
            dy_core(j).start()
            dy_y(j).start()

        @pl.when(step == j + 7)
        def _():
            dy_y(j).wait_recv()
            dy_forward(j).start()

    @pl.when(step < NB - 1)
    def _():
        to_y(step + 1).wait_recv()
        forward(step + 1).start()

    @pl.when(step < NB)
    def _():
        to_core(step).wait_recv()
        forward(step).wait_recv()
        blocks = (x_own[...], xc[step], xy[step], xf[step])
        for rank, block, ref in zip(ranks, blocks, (None, x1_ref, x2_ref, x3_ref)):
            xs[:, feature_block(rank)] = block.astype(F32)
            if ref is not None:
                ref[...] = block
        value = xs[...]

        @pl.when(lax.rem(step, 2) == y)
        def _():
            xm_ref[rows(step // 2), :] = value.astype(BF)

        mean, rstd = row_stats(value)
        n1 = ((value - mean) * rstd * vec[0:1, :] + vec[1:2, :]).astype(BF)
        q = (dot(n1, wq[...]) + bqv[0:1, :]).astype(BF)
        k = dot(n1, wk[...]).astype(BF)
        v = (dot(n1, wv[...]) + bqv[1:2, :]).astype(BF)
        qs = q * jnp.asarray(1.0 / math.sqrt(HD), BF)
        q_ref[...] = qs
        k_ref[...] = k
        v_ref[...] = v
        here = rows(step)
        k_s[here, :] = k
        for h in range(LH):
            qm_s[h] = jnp.where(lanes == h, qs, jnp.zeros_like(qs))
            va_s[h, here, :] = jnp.where(lanes == h, v, jnp.ones_like(v))
        lo_s[...] = jnp.broadcast_to(lo[...], (B, B))

    def attend(nb):
        start = pl.multiple_of((step + 1 - nb) * B, B)

        def head(h, carry):
            qm = qm_s[h]
            top = jnp.full((B, 128), NEG, F32)
            biggest = hm_ref[h]
            for r in range(nb):
                slot = SLOTS - nb + r
                base = pl.multiple_of(start + r * B, B)
                s = dot_nt(qm, k_s[pl.ds(base, B), :])
                inside = col_i + base >= lo_s[...]
                shut = pad[0:1, pl.ds(base, B)]
                if r == nb - 1:
                    s = jnp.where(row_i == col_i, s, s + shut)
                    s = jnp.where(inside & (col_i <= row_i), s, NEG)
                else:
                    s = jnp.where(inside, s + shut, NEG)
                biggest = jnp.maximum(biggest, jnp.max(s.reshape(B // 8, 8, B), axis=0))
                s = s + alibi[pl.ds(h, 1), slot * B : (slot + 1) * B]
                u_s[:, slot * B : (slot + 1) * B] = s
                top = jnp.maximum(top, jnp.maximum(s[:, :128], s[:, 128:]))
            hm_ref[h] = biggest
            top = jnp.max(top, axis=1, keepdims=True)
            for r in range(nb):
                slot = SLOTS - nb + r
                cols = slice(slot * B, (slot + 1) * B)
                p_ref[h, :, cols] = jnp.exp(u_s[:, cols] - top).astype(BF)
            res_s[h] = dot(p_ref[h, :, (SLOTS - nb) * B :], va_s[h, pl.ds(start, nb * B), :])
            return carry

        lax.fori_loop(0, LH, head, 0, unroll=True)

    for nb in range(1, SLOTS):
        pl.when(step == nb - 1)(functools.partial(attend, nb))
    pl.when((step >= SLOTS - 1) & (step < NB))(functools.partial(attend, SLOTS))

    @pl.when(step < NB)
    def _():
        ctx = res_s[0]
        total = res_s[LH - 1]
        for h in range(1, LH):
            ctx = jnp.where(lanes == h, res_s[h], ctx)
            total = jnp.where(lanes == h, res_s[h - 1], total)
        inv = 1.0 / pltpu.roll(total, SHARE - HD, 1)
        linv_ref[...] = inv
        ctx = (ctx * inv).astype(BF)
        ctx_ref[...] = ctx
        xs[...] = dot(ctx, wd[...])
        split_store(part_keep.at[step], part_send.at[step], xs, core)
        part_to_core(step).start()

    @pl.when((step >= 1) & (step <= NB))
    def _():
        b = step - 1
        j = b // 2
        part_to_core(b).wait_recv()
        total = part_keep[b].astype(F32) + part_got[b].astype(F32)

        @pl.when(lax.rem(b, 2) == y)
        def _():
            sum_keep[j] = total

        @pl.when(lax.rem(b, 2) != y)
        def _():
            sum_send[j] = total.astype(BF)
            sum_to_y(j).start()

    @pl.when((step >= TAIL) & (lax.rem(step + NB - TAIL, 2) == y))
    def _():
        j = (step - TAIL) // 2
        sum_to_y(j).wait_recv()
        total = (sum_keep[j] + sum_got[j].astype(F32)).astype(BF)
        whole_own[j] = total
        a_ref[rows(j), :] = total
        whole_to_core(j).start()

    @pl.when(step == NB + TAIL - 1)
    def _():
        for j in range(NB // 2):
            whole_to_core(j).wait_recv()
            b_ref[rows(j), :] = whole_got[j]
        for b in range(NB):
            to_core(b).wait_send()
            to_y(b).wait_send()
            forward(b).wait_send()
            part_to_core(b).wait_send()
        for j in range(NB // 2):
            sum_to_y(j).wait_send()
            whole_to_core(j).wait_send()
            dy_own(j).wait()
            dy_core(j).wait()
            dy_y(j).wait_send()
            dy_forward(j).wait()
        for r in range(1, 4):
            vectors(r).wait_send()


def attention_forward(x, g, own_vec, wq, wk, wv, bqv, wd, lo, pad, alibi):
    last = lambda s: jnp.minimum(s, NB - 1)
    row = lambda width: pl.BlockSpec((B, width), lambda s: (last(s), 0))
    whole = lambda shape: pl.BlockSpec(shape, lambda s: (0,) * len(shape))
    like = jax.ShapeDtypeStruct
    dma = lambda n: pltpu.SemaphoreType.DMA((n,))
    half = NB // 2
    return pl.pallas_call(
        fwd_kernel,
        grid=(NB + TAIL,),
        in_specs=[pl.BlockSpec(memory_space=pl.ANY)] * 2
        + [row(SHARE), whole((16, SHARE))]
        + [whole((D, SHARE))] * 3
        + [whole((8, SHARE)), whole((SHARE, D)), row(1), whole((8, SEQ)), whole((8, STRIP))],
        out_specs=[pl.BlockSpec((LH, B, STRIP), lambda s: (0, last(s), 0))]
        + [row(SHARE)] * 5
        + [whole((OWN, D // 2))] * 2
        + [row(SHARE)] * 3
        + [whole((OWN, D)), whole((LH, 8, B)), whole((8, D)), whole((8, UNITS))]
        + [pl.BlockSpec(memory_space=pl.ANY)],
        scratch_shapes=[
            pltpu.VMEM((B, D), F32),
            pltpu.VMEM((LH, B, SHARE), BF),
            pltpu.VMEM((SEQ, SHARE), BF),
            pltpu.VMEM((LH, SEQ, SHARE), BF),
            pltpu.VMEM((B, STRIP), F32),
            pltpu.VMEM((LH, B, SHARE), F32),
            pltpu.VMEM((B, B), jnp.int32),
        ]
        + [pltpu.VMEM((NB, B, SHARE), BF)] * 3
        + [pltpu.VMEM((NB, B, D // 2), BF)] * 3
        + [pltpu.VMEM((half, B, D // 2), F32)]
        + [pltpu.VMEM((half, B, D // 2), BF)] * 4
        + [pltpu.VMEM((4, 16, SHARE), F32)]
        + [dma(NB)] * 8
        + [dma(half)] * 4
        + [dma(3)] * 2
        + [dma(half)] * 7,
        out_shape=[like((LH, SEQ, STRIP), BF)]
        + [like((SEQ, SHARE), BF)] * 3
        + [like((SEQ, SHARE), F32), like((SEQ, SHARE), BF)]
        + [like((OWN, D // 2), BF)] * 2
        + [like((SEQ, SHARE), BF)] * 3
        + [like((OWN, D), BF), like((LH, 8, B), F32), like((8, D), F32), like((8, UNITS), F32)]
        + [like((OWN, D), BF)],
        compiler_params=remote_params(0),
        cost_estimate=pl.CostEstimate(
            flops=16 * 10**9, bytes_accessed=40 * 2**20, transcendentals=8 * 10**6
        ),
        name="attention_forward",
    )(x, g, x, own_vec, wq, wk, wv, bqv, wd, lo, pad, alibi)


def mlp_kernel(
    a_own, a_par, xm, dy_s, vec, bup, wu0, wu1, wd0, wd1,
    mk_ref, ms_ref, gn_ref, h1_ref, gu_ref, su_ref, gd_ref, sd_ref, bs_ref, ru_ref,
    n2_s, n2t_s, dyt_s, dyo_s, am_s, ag_s, act_s, gp_s, us_s, s_u, r_u,
    *, bits, chunk,
):
    i = pl.program_id(0)
    core, y, ranks = place()
    partners = [{"dp": dp_partner(bit)} for bit in bits]

    def send_tile(n, kind):
        return remote(us_s.at[n], ru_ref.at[n], s_u.at[n], r_u.at[n], partners[kind])

    @pl.when(i == 0)
    def _():
        greet(partners)

        def assemble(rb, carry):
            rows = block_rows(rb)
            h1_ref[rows, :] = xm[rows, :].astype(F32)
            for part, a in ((core, a_own), (1 - core, a_par)):
                for half in range(2):
                    cols = feature_block(2 * half + part)
                    h1_ref[rows, cols] += a[rows, half * SHARE : (half + 1) * SHARE].astype(F32)
            value = h1_ref[rows, :] + vec[2:3, :]
            h1_ref[rows, :] = value
            mean, rstd = row_stats(value)
            n2 = ((value - mean) * rstd * vec[3:4, :] + vec[4:5, :]).astype(BF)
            n2_s[rows, :] = n2
            for source, turned, bit in (
                (n2_s, n2t_s, bits[0]), (dy_s, dyt_s, bits[0]), (dy_s, dyo_s, bits[1])
            ):
                for j in range(D // 256):
                    for side, cols in enumerate(piece(j, bit, chunk)):
                        to = slice(side * (D // 2) + j * 128, side * (D // 2) + (j + 1) * 128)
                        turned[to, rows] = source[rows, cols].T
            am_s[rows, :] = jnp.zeros((B, D), F32)
            ag_s[rows, :] = jnp.zeros((B, D), F32)
            return carry

        lax.fori_loop(0, OWN // B, assemble, 0)

    def tile(wu, wd, which):
        bias = bup[which : which + 1, pl.ds(pl.multiple_of(lax.rem(i, 2) * TILE, TILE), TILE)]
        scale = math.sqrt(2.0 / math.pi)

        def rows_of(rb, sums):
            rows = pl.ds(pl.multiple_of(rb * B, B), B)
            pre = dot(n2_s[rows, :], wu[...]) + bias
            back = dot_nt(dy_s[rows, :], wd[...])
            square = pre * pre
            th = jnp.tanh(scale * pre * (1.0 + 0.044715 * square))
            half = 0.5 * (1.0 + th)
            act = (pre * half).astype(BF)
            slope = half + 0.5 * pre * (1.0 - th * th) * (scale + (3 * 0.044715 * scale) * square)
            gp = (slope * back).astype(BF)
            act_s[rows, :] = act
            gp_s[rows, :] = gp
            am_s[rows, :] += dot(act, wd[...])
            ag_s[rows, :] += dot_nt(gp, wu[...])
            return sums + jnp.sum(gp.astype(F32), axis=0, keepdims=True)

        sums = lax.fori_loop(0, OWN // B, rows_of, jnp.zeros((1, TILE), F32))
        bs_ref[...] = jnp.broadcast_to(sums, bs_ref.shape)

        def grads(left, right, keep, send):
            keep[...] = dot(left[0 : D // 2, :], right[...]).astype(BF)
            send[...] = dot(left[D // 2 :, :], right[...]).astype(BF)

        first = which == 0
        grads(n2t_s, gp_s, gu_ref, us_s.at[i] if first else su_ref)
        if first:
            send_tile(i, 0).start()
        grads(dyo_s if first else dyt_s, act_s, gd_ref, us_s.at[2 + i] if first else sd_ref)
        if first:
            send_tile(2 + i, 1).start()

    pl.when(i < 2)(lambda: tile(wu0, wd0, 0))
    pl.when(i >= 2)(lambda: tile(wu1, wd1, 1))

    @pl.when(i == 3)
    def _():
        split_store(mk_ref, ms_ref, am_s, core)
        gn_ref[...] = ag_s[...].astype(BF)
        for n in range(4):
            send_tile(n, n // 2).wait()


def feed_forward(a_own, a_par, xm, dy, vec, bup, wu0, wd0, w_other, bits, chunk):
    whole = lambda shape: pl.BlockSpec(shape, lambda i: (0,) * len(shape))
    low = lambda i: jnp.minimum(i, 1)
    high = lambda i: jnp.maximum(i - 2, 0)
    like = jax.ShapeDtypeStruct
    tile = pl.BlockSpec((D // 2, TILE), lambda i: (0, i))
    return pl.pallas_call(
        functools.partial(mlp_kernel, bits=bits, chunk=chunk),
        grid=(4,),
        in_specs=[whole((OWN, D // 2))] * 2
        + [whole((OWN, D))] * 2
        + [
            whole((8, D)),
            whole((8, UNITS)),
            pl.BlockSpec((D, TILE), lambda i: (0, low(i))),
            pl.BlockSpec((D, TILE), lambda i: (0, high(i))),
            pl.BlockSpec((TILE, D), lambda i: (low(i), 0)),
            pl.BlockSpec((TILE, D), lambda i: (high(i), 1)),
        ],
        out_specs=[whole((OWN, D // 2))] * 2
        + [whole((OWN, D))] * 2
        + [
            tile,
            pl.BlockSpec((D // 2, TILE), lambda i: (0, high(i))),
            tile,
            pl.BlockSpec((D // 2, TILE), lambda i: (0, high(i))),
            pl.BlockSpec((8, TILE), lambda i: (0, i)),
            pl.BlockSpec(memory_space=pl.ANY),
        ],
        scratch_shapes=[
            pltpu.VMEM((OWN, D), BF),
            pltpu.VMEM((D, OWN), BF),
            pltpu.VMEM((D, OWN), BF),
            pltpu.VMEM((D, OWN), BF),
            pltpu.VMEM((OWN, D), F32),
            pltpu.VMEM((OWN, D), F32),
            pltpu.VMEM((OWN, TILE), BF),
            pltpu.VMEM((OWN, TILE), BF),
            pltpu.VMEM((4, D // 2, TILE), BF),
            pltpu.SemaphoreType.DMA((4,)),
            pltpu.SemaphoreType.DMA((4,)),
        ],
        out_shape=[like((OWN, D // 2), BF)] * 2
        + [
            like((OWN, D), BF),
            like((OWN, D), F32),
            like((D // 2, 2 * UNITS), BF),
            like((D // 2, UNITS), BF),
            like((D // 2, 2 * UNITS), BF),
            like((D // 2, UNITS), BF),
            like((8, 2 * UNITS), F32),
            like((4, D // 2, TILE), BF),
        ],
        compiler_params=remote_params(1),
        cost_estimate=pl.CostEstimate(
            flops=26 * 10**9, bytes_accessed=40 * 2**20, transcendentals=2 * 10**6
        ),
        name="feed_forward",
    )(a_own, a_par, xm, dy, vec, bup, wu0, w_other, wd0, w_other)


LEAD = 2
FINAL = 3
TILES = (("u", 0), ("u", 1), ("d", 0), ("d", 1), ("u", 2), ("d", 2), ("d", 3), ("u", 3), *(("a", n) for n in range(4)))
OTHER_ORDER = (2, 3, 11)
FIRST = (0, 1, 0, 2, 3, 4, 6, 7)
USE = sorted(range(8), key=lambda p: (FIRST[p], p))
SLOT = [USE.index(p) % 2 for p in range(8)] + [0, 0, 1, 1]
PAIRS = ((0, 4), (1, 7), (2, 5), (3, 6))
DRAIN = LEAD + FINAL + NB


def step_of(p, n, levels):
    if p < 8:
        return FIRST[p] + 3 * (n - 1)
    if n <= 2:
        return ((11, 12, 13, 11), (13, 14, 14, 13))[n - 1][p - 8]
    free = step_of(p - 4, n + 1, levels) if n < levels else 0
    return max(step_of(p, n - 1, levels) + 1, free)


def last_step(levels):
    return max(DRAIN + levels - 1, max(step_of(p, levels, levels) for p in range(7, 12)))


def bwd_kernel(
    x0, x1, x2, x3, x_late, h1, gn, gn_any, mk, ms_any, dy_in, gu, gd, ru, su_any, sd_any, up_sums, hm,
    p_ref, q_ref, linv_ref, ctx_ref, k_ref, v_ref, vec, wq, wk, wv, wd,
    out_any, os_any, tg_ref, wu_ref, wdn_ref, wqk_ref, wvd_ref, vt_ref,
    w_s, gh_s, gm_s, gt_s, qt_s, dl_s, ds_s, res_s, dkt_s, dvt_s, acc_s,
    o_s, gn_got, mr_got, gh_own, gh_y, gh_f,
    part_keep, part_send, part_got, sum_keep, sum_send, sum_got, ghx_s, st_keep, st_got, st_sum, st_all,
    gk, ru_s, g1, y_send, y_got, cs_ref, bs_ref, n1_ref, v_keep, v_send, v_away, v_sum, v_got,
    *rest, orders, chunk,
):
    levels = len(orders[0])
    stages = [rest[3 * n : 3 * n + 3] for n in range(levels - 1)]
    (
        s_gn, r_gn, s_mr, r_mr, s_gy, r_gy, s_gf, r_gf, s_pc, r_pc, s_sy, r_sy,
        s_tc, r_tc, s_ty, r_ty, s_g1, r_g1, s_yy, r_yy, l_g, l_r, s_gw, r_gw, s_va, r_va, s_vt, r_vt, l_o, s_o, r_o, *g_sems,
    ) = rest[3 * (levels - 1) :]
    step = pl.program_id(0)
    b = NB - 1 - (step - LEAD)
    core, y, ranks = place()
    beside, across = {"tensor": ranks[1]}, {"tensor": ranks[2]}
    order_of = lambda p: orders[1 if p in OTHER_ORDER else 0]
    partner = lambda bit: {"dp": dp_partner(bit)}
    half = NB // 2
    last = last_step(levels)
    lanes = head_of_lane((B, SHARE))

    send_gn = lambda j: remote(gn_any.at[block_rows(j)], gn_got.at[j], s_gn.at[j], r_gn.at[j], beside)
    send_mr = lambda j: remote(ms_any.at[block_rows(j)], mr_got.at[j], s_mr.at[j], r_mr.at[j], beside)
    send_gy = lambda j, side: remote(
        gh_own.at[j, :, feature_block(2 * side + core)],
        gh_y.at[j, :, side * SHARE : (side + 1) * SHARE],
        s_gy.at[2 * j + side], r_gy.at[2 * j + side], across,
    )
    send_gf = lambda j: remote(gh_y.at[j], gh_f.at[j], s_gf.at[j], r_gf.at[j], beside)
    store_out = lambda j, side: pltpu.make_async_copy(
        o_s.at[lax.rem(j, 2), side],
        (out_any.at[block_rows(2 * j + y)], os_any.at[block_rows(j)])[side],
        l_o.at[2 * lax.rem(j, 2) + side],
    )
    send_out = lambda j: remote(
        os_any.at[block_rows(j)], out_any.at[block_rows(2 * j + y)], s_o.at[j], r_o.at[j], across
    )
    send_part = lambda n: remote(part_send.at[lax.rem(n, 3)], part_got.at[n], s_pc.at[n], r_pc.at[n], beside)
    send_sum = lambda n: remote(sum_send.at[n], sum_got.at[n], s_sy.at[n], r_sy.at[n], across)
    send_tc = lambda n: remote(st_keep.at[n], st_got.at[n], s_tc.at[n], r_tc.at[n], beside)
    send_ty = lambda n: remote(st_sum.at[n], st_all.at[n], s_ty.at[n], r_ty.at[n], across)

    def tile_of(p):
        kind, n = TILES[p]
        return slice(n * TILE, (n + 1) * TILE), kind == "u"

    span = lambda p: slice(0, TILE) if p < 8 else slice((p - 8) % 2 * SHARE, ((p - 8) % 2 + 1) * SHARE)
    wide = lambda p: slice(0, TILE if p < 8 else SHARE)
    shared = lambda p: p if p < 8 else 8 + (p - 8) // 2

    def send_first(p):
        cols, up = tile_of(p)
        src = (su_any if up else sd_any).at[:, slice(cols.start - UNITS, cols.stop - UNITS)]
        return remote(src, g1.at[p - 4], s_g1.at[p - 4], r_g1.at[p - 4], partner(order_of(p)[0]))

    def send_weights(p, part):
        n = 2 * (p - 8) + part
        return remote(
            gn_got.at[p - 8, :, slice(part * SHARE, (part + 1) * SHARE)],
            g1.at[4 + (p - 8) // 2, block_rows(part), span(p)],
            s_gw.at[n], r_gw.at[n], partner(order_of(p)[0]),
        )

    slot = SLOT

    def load_keep(p):
        cols, up = tile_of(p)
        return pltpu.make_async_copy((gu if up else gd).at[:, cols], gk.at[slot[p]], l_g.at[slot[p]])

    def load_got(p):
        return pltpu.make_async_copy(ru.at[p], ru_s.at[slot[p]], l_r.at[slot[p]])

    def send_stage(p, n):
        _, send, got = stages[n - 1]
        return remote(
            send.at[p % 4, :, wide(p)], got.at[shared(p), :, span(p)], g_sems[2 * n - 2].at[p], g_sems[2 * n - 1].at[p], partner(order_of(p)[n])
        )

    send_last = lambda n: remote(y_send.at[n], y_got.at[n], s_yy.at[n], r_yy.at[n], across)

    def split(p, n):
        order = order_of(p)
        if n == 1:
            keep = lambda rows: gk[slot[p], rows, span(p)]
            if p < 4:
                load_got(p).wait()
                got = lambda rows: ru_s[slot[p], rows, :]
            else:
                got = lambda rows: g1[shared(p) - 4, rows, span(p)]
            if p < 8:
                load_keep(p).wait()
            if 4 <= p < 8:
                send_first(p).wait_recv()
            if p >= 8:
                send_weights(p, 0).wait_recv()
                send_weights(p, 1).wait_recv()
        else:
            send_stage(p, n - 1).wait_recv()
            keep = lambda rows: stages[n - 2][0][p % 4, rows, wide(p)]
            got = lambda rows: stages[n - 2][2][shared(p), rows, span(p)]
        size = D >> n
        following = order[n]
        inner = chunk
        for other in order[n + 1 :]:
            inner *= 2 if other < following else 1
        mine = dp_bit(following)
        if p >= 4:
            send_stage(p - 4, n).wait_send()
        for group in range(size // (2 * inner)):
            to = slice(group * inner, (group + 1) * inner)
            for side, ref in ((mine, stages[n - 1][0]), (1 - mine, stages[n - 1][1])):
                rows = pl.ds(pl.multiple_of(group * 2 * inner + side * inner, inner), inner)
                ref[p % 4, to, wide(p)] = (keep(rows).astype(F32) + got(rows).astype(F32)).astype(BF)
        send_stage(p, n).start()

    def whole_tile(p):
        send_stage(p, levels - 1).wait_recv()
        keep, _, got = stages[levels - 2]
        total = keep[p % 4, :, wide(p)].astype(F32) + got[shared(p), :, span(p)].astype(F32)
        if p >= 8:
            (wqk_ref, wvd_ref)[(p - 8) // 2][:, span(p)] = total
        for n, (own, other) in enumerate(PAIRS):
            cols, up = tile_of(own)
            if p == own:
                (wu_ref if up else wdn_ref)[:, cols] = total
            if p == other:
                y_send[n] = total.astype(BF)
                send_last(n).start()

    def close(n):
        cols, up = tile_of(PAIRS[n][0])
        send_last(n).wait_recv()
        (wu_ref if up else wdn_ref)[:, cols] += y_got[n].astype(F32)

    @pl.when(step == 0)
    def _():
        greet([beside, across] + [partner(bit) for bit in orders[0]])
        for j in range(half - 1, -1, -1):
            send_gn(j).start()
            send_mr(j).start()
        for p in range(4, 8):
            send_first(p).start()
        for p in USE[:2]:
            load_keep(p).start()
            load_got(p).start()
        cs_ref[...] = jnp.zeros(cs_ref.shape, F32)
        bs_ref[...] = jnp.zeros(bs_ref.shape, F32)
        n1_ref[...] = jnp.zeros(n1_ref.shape, F32)

    @pl.when(step == 1)
    def _():
        dkt_s[...] = jnp.zeros(dkt_s.shape, F32)
        dvt_s[...] = jnp.zeros(dvt_s.shape, F32)
        acc_s[...] = jnp.zeros(acc_s.shape, F32)

    @pl.when(step < half)
    def _():
        j = half - 1 - step
        send_gn(j).wait_recv()
        send_mr(j).wait_recv()
        dy = dy_in[...].astype(F32)
        value = h1[...]

        def out(side):
            part = pl.ds(pl.multiple_of(side * SHARE, SHARE), SHARE)
            cols = feature_block(2 * side + core)
            total = mk[:, part].astype(F32) + mr_got[j, :, part].astype(F32)
            return (h1[:, cols] + total + vec[5:6, cols]).astype(BF)


        @pl.when(step >= 2)
        def _():
            for side in range(2):
                store_out(j + 2, side).wait()

        for side, which in enumerate((y, 1 - y)):
            o_s[lax.rem(j, 2), side] = out(which)
            store_out(j, side).start()
        mean, rstd = row_stats(value)
        xhat = (value - mean) * rstd
        grad = gn[...].astype(F32) + gn_got[j].astype(F32)
        scaled = grad * vec[3:4, :]
        first = jnp.sum(scaled, axis=1, keepdims=True) / D
        second = jnp.sum(scaled * xhat, axis=1, keepdims=True) / D
        gh = dy + rstd * (scaled - first - xhat * second)
        for n, columns in enumerate((grad * xhat, grad, gh, dy)):
            cs_ref[n : n + 1, :] += jnp.sum(columns, axis=0, keepdims=True)
        gh_own[j] = gh.astype(BF)
        send_gy(j, 0).start()
        send_gy(j, 1).start()

    @pl.when((step >= LEAD) & (step < LEAD + NB))
    def _():
        j = b // 2

        @pl.when(lax.rem(b, 2) == y)
        def _():
            gh_s[...] = gh_own[j]

        @pl.when(lax.rem(b, 2) != y)
        def _():
            send_gf(j).wait_recv()
            for part, ref in ((core, gh_y), (1 - core, gh_f)):
                for side in range(2):
                    gh_s[:, feature_block(2 * side + part)] = ref[j, :, side * SHARE : (side + 1) * SHARE]

        gc = dot_nt(gh_s[...], wd[...]).astype(BF).astype(F32)
        scaled = gc * linv_ref[...]
        gcs = scaled.astype(BF)
        product = scaled * ctx_ref[...].astype(F32)
        qt_s[...] = q_ref[...].T.reshape(LH, HD, B)
        gt_s[...] = gcs.T.reshape(LH, HD, B)
        for h in range(LH):
            gm_s[h] = jnp.where(lanes == h, gcs, jnp.zeros_like(gcs))
            delta = jnp.sum(jnp.where(lanes == h, product, 0.0), axis=1, keepdims=True)
            dl_s[h] = jnp.broadcast_to(delta, (B, 128))

    def attend(nb):
        start = pl.multiple_of((b + 1 - nb) * B, B)

        def head(h, carry):
            gm = gm_s[h]
            delta = jnp.concatenate([dl_s[h]] * 2, axis=1)
            for r in range(nb):
                slot = SLOTS - nb + r
                cols = slice(slot * B, (slot + 1) * B)
                dp = dot_nt(gm, v_ref[pl.ds(pl.multiple_of(start + r * B, B), B), :])
                ds_s[:, cols] = (p_ref[h, :, cols].astype(F32) * (dp - delta)).astype(BF)
            live = slice((SLOTS - nb) * B, STRIP)
            keys = pl.ds(start, nb * B)
            res_s[h] = dot(ds_s[:, live], k_ref[keys, :])
            dkt_s[h, :, keys] += dot(qt_s[h], ds_s[:, live])
            dvt_s[h, :, keys] += dot(gt_s[h], p_ref[h, :, live])
            return carry

        lax.fori_loop(0, LH, head, 0, unroll=2)

    pl.when((step >= LEAD) & (b >= SLOTS - 1))(functools.partial(attend, SLOTS))
    for nb in range(SLOTS - 1, 0, -1):
        pl.when(b == nb - 1)(functools.partial(attend, nb))

    @pl.when((step >= LEAD) & (step < LEAD + NB))
    def _():
        dq = res_s[0]
        for h in range(1, LH):
            dq = jnp.where(lanes == h, res_s[h], dq)
        dq = (dq * (1.0 / math.sqrt(HD))).astype(BF)
        here = block_rows(b)
        dk = dkt_s[:, :, here].reshape(SHARE, B).astype(BF).T
        dv = dvt_s[:, :, here].reshape(SHARE, B).astype(BF).T
        bs_ref[0:1, :] += jnp.sum(dq.astype(F32), axis=0, keepdims=True)
        bs_ref[1:2, :] += jnp.sum(dv.astype(F32), axis=0, keepdims=True)

        for rank, x in zip(ranks, (x0, x1, x2, x3)):
            w_s[:, feature_block(rank)] = x[...].astype(F32)
        value = w_s[...]
        mean, rstd = row_stats(value)
        xhat = (value - mean) * rstd
        n1t = (xhat * vec[0:1, :] + vec[1:2, :]).astype(BF).T
        acc_s[:, 0:SHARE] += dot(n1t, dq)
        acc_s[:, SHARE : 2 * SHARE] += dot(n1t, dk)
        acc_s[:, 2 * SHARE : 3 * SHARE] += dot(n1t, dv)
        acc_s[:, 3 * SHARE :] += dot(gh_s[...].T, ctx_ref[...])

        grad = dot_nt(dq, wq[...]) + dot_nt(dk, wk[...]) + dot_nt(dv, wv[...])
        scaled = grad * vec[0:1, :]
        first = jnp.sum(scaled, axis=1, keepdims=True)
        second = jnp.sum(scaled * xhat, axis=1, keepdims=True)
        column = lax.broadcasted_iota(jnp.int32, (B, 128), 1)
        packed = jnp.where(
            column == 0, first, jnp.where(column == 1, second, jnp.where(column == 2, mean, rstd))
        )
        st_keep[b] = packed.T[0:8, :]
        send_tc(b).start()
        w_s[...] = grad

        @pl.when(step >= LEAD + 3)
        def _():
            send_part(b + 3).wait_send()

        for n, side in enumerate((y, 1 - y)):
            cols = slice(n * SHARE, (n + 1) * SHARE)
            part_keep[lax.rem(b, 2), :, cols] = w_s[:, feature_block(2 * side + core)].astype(BF)
            part_send[lax.rem(b, 3), :, cols] = w_s[:, feature_block(2 * side + 1 - core)].astype(BF)
        send_part(b).start()
        ghx_s[lax.rem(b, 4)] = gh_s[:, feature_block(ranks[0])]

    @pl.when(step == LEAD + NB - 1)
    def _():
        for p in (11, 8, 9, 10):
            cols = slice((p - 8) * SHARE, (p - 7) * SHARE)
            for j in range(D // 256):
                mine, other = piece(j, order_of(p)[0], chunk)
                gk[slot[p], j * 128 : (j + 1) * 128, span(p)] = acc_s[mine, cols].astype(BF)
                into = slice(j // 2 * SHARE, (j // 2 + 1) * SHARE)
                gn_got[p - 8, j % 2 * 128 : (j % 2 + 1) * 128, into] = acc_s[other, cols].astype(BF)
            for part in range(2):
                send_weights(p, part).start()
        for j in range(half):
            send_out(j).start()

    send_away = lambda: remote(v_send, v_away, s_va.at[0], r_va.at[0], across)
    send_total = lambda n: remote(
        v_sum.at[n], v_got.at[n], s_vt.at[n], r_vt.at[n], partner(orders[0][n])
    )

    @pl.when(step == half)
    def _():
        for j in range(2):
            for side in range(2):
                store_out(j, side).wait()
        for ref, rank, side in ((v_keep, ranks[0], 0), (v_send, ranks[2], UNITS)):
            ref[0:4, :] = cs_ref[0:4, feature_block(rank)]
            for n in range(4):
                ref[4 + n : 5 + n, :] = up_sums[0:1, side + n * SHARE : side + (n + 1) * SHARE]
        send_away().start()

    @pl.when(step == half + 4)
    def _():
        send_away().wait_recv()
        v_sum[0, 0:8, :] = v_keep[...] + v_away[...]

    @pl.when((step >= LEAD + 1) & (step < LEAD + 1 + NB))
    def _():
        n = b + 1
        send_part(n).wait_recv()
        send_tc(n).wait_recv()
        keep = part_keep[lax.rem(n, 2)].astype(F32)
        sum_keep[lax.rem(n, 3)] = keep[:, :SHARE] + part_got[n, :, :SHARE].astype(F32)
        sum_send[n] = (keep[:, SHARE:] + part_got[n, :, SHARE:].astype(F32)).astype(BF)
        st_sum[n] = st_keep[n] + st_got[n]
        send_sum(n).start()
        send_ty(n).start()

    @pl.when((step >= LEAD + FINAL) & (step < LEAD + FINAL + NB))
    def _():
        n = b + FINAL
        send_sum(n).wait_recv()
        send_ty(n).wait_recv()
        grad = sum_keep[lax.rem(n, 3)] + sum_got[n].astype(F32)
        row = lax.broadcasted_iota(jnp.int32, (8, B), 0)
        stats = jnp.where(row < 2, st_sum[n] + st_all[n], st_keep[n])
        stats = jnp.concatenate([stats] * 16, axis=0).T
        xhat = (x_late[...].astype(F32) - stats[:, 2:3]) * stats[:, 3:4]
        scaled = grad * vec[0:1, feature_block(ranks[0])]
        inner = scaled - stats[:, 0:1] / D - xhat * (stats[:, 1:2] / D)
        tg_ref[...] = ghx_s[lax.rem(n, 4)].astype(F32) + stats[:, 3:4] * inner
        n1_ref[0:1, :] += jnp.sum(grad * xhat, axis=0, keepdims=True)
        n1_ref[1:2, :] += jnp.sum(grad, axis=0, keepdims=True)

    row16 = lax.broadcasted_iota(jnp.int32, (16, SHARE), 0)

    @pl.when(step == DRAIN - 1)
    def _():
        v_sum[0, 8:10, :] = n1_ref[0:2, :]
        v_sum[0, 10:12, :] = bs_ref[0:2, :]
        lane = lax.broadcasted_iota(jnp.int32, (4, SHARE), 1)
        top = jnp.full((4, SHARE), NEG, F32)
        for h in range(LH):
            top = jnp.where(lane == h, jnp.max(hm[h]), top)
        v_sum[0, 12:16, :] = top
        send_total(0).start()

    for n in range(levels):

        @pl.when(step == DRAIN + n)
        def _():
            send_total(n).wait_recv()
            mine, other = v_sum[n], v_got[n]
            total = jnp.where(row16 < 12, mine + other, jnp.maximum(mine, other))
            if n == levels - 1:
                vt_ref[...] = total
            else:
                v_sum[n + 1] = total
                send_total(n + 1).start()

    for j in range(half - 1, -1, -1):

        @pl.when(step == half - j)
        def _():
            send_gy(j, 0).wait_recv()
            send_gy(j, 1).wait_recv()
            send_gf(j).start()

    for p in range(12):
        for n in range(1, levels):
            pl.when(step == step_of(p, n, levels))(functools.partial(split, p, n))
        pl.when(step == step_of(p, levels, levels))(functools.partial(whole_tile, p))

    def load_next(p):
        load_keep(p).start()
        if p < 4:
            load_got(p).start()

    for n in range(2, 8):
        pl.when(step == FIRST[USE[n - 2]])(functools.partial(load_next, USE[n]))

    @pl.when(step == last)
    def _():
        for j in range(half):
            close(j)
            send_out(j).wait()
            for copy in (send_gn, send_mr, send_gf, send_last):
                copy(j).wait_send()
            for side in range(2):
                send_gy(j, side).wait_send()
            for level in range(1, levels):
                send_stage(8 + j, level).wait_send()
        for n in range(NB):
            for copy in (send_sum, send_tc, send_ty):
                copy(n).wait_send()
        for n in range(3):
            send_part(n).wait_send()
        for p in range(4, 8):
            send_first(p).wait_send()
        for p in range(8, 12):
            for part in range(2):
                send_weights(p, part).wait_send()
        send_away().wait_send()
        for n in range(levels):
            send_total(n).wait_send()


def attention_backward(
    xs, h1, gn, mk, ms, dy, gu, gd, ru, su, sd, up_sums, hm, p, q, linv, ctx, k, v, vec, wq, wk, wv, wd,
    orders, chunk,
):
    levels = len(orders[0])
    half = NB // 2
    block = lambda s: jnp.clip(NB - 1 + LEAD - s, 0, NB - 1)
    late = lambda s: jnp.clip(NB - 1 + LEAD + FINAL - s, 0, NB - 1)
    row = lambda width: pl.BlockSpec((B, width), lambda s: (block(s), 0))
    own = lambda width: pl.BlockSpec((B, width), lambda s: (jnp.maximum(half - 1 - s, 0), 0))
    once = pl.Buffered(1)
    whole = lambda *shape: pl.BlockSpec(shape, lambda s: (0,) * len(shape), pipeline_mode=once)
    anywhere = pl.BlockSpec(memory_space=pl.ANY)
    like = jax.ShapeDtypeStruct
    vmem = lambda *shape, dtype=BF: pltpu.VMEM(shape, dtype)
    dma = lambda n: pltpu.SemaphoreType.DMA((n,))
    final_late = pl.BlockSpec((B, SHARE), lambda s: (late(s), 0))
    return pl.pallas_call(
        functools.partial(bwd_kernel, orders=orders, chunk=chunk),
        grid=(last_step(levels) + 1,),
        in_specs=[row(SHARE)] * 4
        + [final_late, own(D), own(D), anywhere, own(D // 2), anywhere]
        + [own(D)]
        + [anywhere] * 2
        + [anywhere] * 3
        + [whole(8, 2 * UNITS), whole(LH, 8, B)]
        + [pl.BlockSpec((LH, B, STRIP), lambda s: (0, block(s), 0))]
        + [row(SHARE)] * 3
        + [whole(SEQ, SHARE)] * 2
        + [whole(8, D)]
        + [whole(D, SHARE)] * 3
        + [whole(SHARE, D)],
        out_specs=[anywhere, anywhere, final_late]
        + [whole(chunk, UNITS)] * 2
        + [whole(chunk, TILE)] * 2
        + [whole(16, SHARE)],
        scratch_shapes=[
            vmem(B, D, dtype=F32),
            vmem(B, D),
            vmem(LH, B, SHARE),
            vmem(LH, HD, B),
            vmem(LH, HD, B),
            vmem(LH, B, 128, dtype=F32),
            vmem(B, STRIP),
            vmem(LH, B, SHARE, dtype=F32),
            vmem(LH, HD, SEQ, dtype=F32),
            vmem(LH, HD, SEQ, dtype=F32),
            vmem(D, 4 * SHARE, dtype=F32),
            vmem(2, 2, B, SHARE),
            vmem(half, B, D),
            vmem(half, B, D // 2),
            vmem(half, B, D),
            vmem(half, B, D // 2),
            vmem(half, B, D // 2),
            vmem(2, B, D // 2),
            vmem(3, B, D // 2),
            vmem(NB, B, D // 2),
            vmem(3, B, SHARE, dtype=F32),
            vmem(NB, B, SHARE),
            vmem(NB, B, SHARE),
            vmem(4, B, SHARE),
            vmem(NB, 8, B, dtype=F32),
            vmem(NB, 8, B, dtype=F32),
            vmem(NB, 8, B, dtype=F32),
            vmem(NB, 8, B, dtype=F32),
            vmem(2, D // 2, TILE),
            vmem(2, D // 2, TILE),
            vmem(6, D // 2, TILE),
            vmem(half, chunk, TILE),
            vmem(half, chunk, TILE),
            vmem(8, D, dtype=F32),
            vmem(8, SHARE, dtype=F32),
            vmem(8, SHARE, dtype=F32),
            vmem(8, SHARE, dtype=F32),
            vmem(8, SHARE, dtype=F32),
            vmem(8, SHARE, dtype=F32),
            vmem(levels, 16, SHARE, dtype=F32),
            vmem(levels, 16, SHARE, dtype=F32),
        ]
        + [vmem(slots, D >> (n + 1), TILE) for n in range(1, levels) for slots in (4, 4, 10)]
        + [dma(half)] * 4
        + [dma(NB)] * 2
        + [dma(half)] * 2
        + [dma(NB)] * 8
        + [dma(4)] * 2
        + [dma(half)] * 2
        + [dma(2)] * 2
        + [dma(8)] * 2
        + [dma(1)] * 2
        + [dma(levels)] * 2
        + [dma(half)] * 3
        + [dma(12)] * (2 * (levels - 1)),
        out_shape=[like((SEQ, SHARE), BF), like((OWN, SHARE), BF)]
        + [like((SEQ, SHARE), F32)]
        + [like((chunk, UNITS), F32)] * 2
        + [like((chunk, TILE), F32)] * 2
        + [like((16, SHARE), F32)],
        compiler_params=remote_params(2),
        cost_estimate=pl.CostEstimate(
            flops=30 * 10**9, bytes_accessed=50 * 2**20, transcendentals=0
        ),
        name="backward",
    )(
        *xs, xs[0], h1, gn, gn, mk, ms, dy, gu, gd, ru, su, sd, up_sums, hm, p, q, linv, ctx, k, v, vec, wq, wk, wv, wd
    )


def swap(value, axis, bit):
    size = lax.axis_size(axis)
    return lax.ppermute(value, axis, [(i, i ^ bit) for i in range(size)])


def dp_bits():
    bits, bit = [], 1
    while bit < lax.axis_size("dp"):
        bits.append(bit)
        bit *= 2
    return bits


def pick(value, axis, index):
    return lax.dynamic_index_in_dim(value, index, axis, keepdims=False)


def shards(
    tokens,
    out_grad,
    segments,
    padding,
    norm1_gain,
    norm1_bias,
    w_query,
    b_query,
    w_key,
    w_value,
    b_value,
    w_dense,
    dense_bias,
    norm2_gain,
    norm2_bias,
    w_up,
    b_up,
    w_down,
    down_bias,
):
    t = lax.axis_index("tensor")
    rank = lax.axis_index("dp")
    size = lax.axis_size("dp")
    core, y = t % 2, t // 2
    core_swap = lambda value: swap(value, "tensor", 1)
    y_swap = lambda value: swap(value, "tensor", 2)
    rows8 = lambda value: jnp.pad(value, ((0, 8 - value.shape[0]), (0, 0)))

    own_vec = jnp.concatenate(
        [
            jnp.stack([norm1_gain, norm1_bias, dense_bias, norm2_gain, norm2_bias, down_bias, down_bias, down_bias]),
            b_up.reshape(4, SHARE),
            b_up.reshape(4, SHARE),
        ]
    ).astype(F32)

    part = D // size
    cut = lambda w: lax.dynamic_slice_in_dim(w, rank * part, part, 0)
    w_part = y_swap(jnp.concatenate([cut(w_up), cut(w_down)], axis=1))
    seg = segments.reshape(SEQ)
    index = jnp.arange(SEQ, dtype=jnp.int32)
    first = jnp.zeros((SEQ,), jnp.int32)
    for value in range(1, 4):
        first = jnp.where(seg == value, jnp.sum((seg < value).astype(jnp.int32)), first)
    lowest = jnp.maximum(first, index - (WIN - 1))
    pad_row = rows8(jnp.where(padding.reshape(1, SEQ) == 1, 0.0, NEG).astype(F32))
    heads = t * LH + jnp.arange(LH)
    slopes = jnp.exp2(-8.0 * (heads.astype(F32) + 1.0) / HEADS)
    alibi = rows8(slopes[:, None] * (jnp.arange(STRIP) - (STRIP - 1)).astype(F32)[None, :])

    b_qv = rows8(jnp.stack([b_query, b_value]).astype(F32))
    lows = lowest.reshape(SEQ, 1)
    w_part, own_vec, b_qv, lows, pad_row, alibi = lax.optimization_barrier(
        (w_part, own_vec, b_qv, lows, pad_row, alibi)
    )
    w_other = lax.all_gather(w_part, "dp", axis=0, tiled=True)

    p, q, k, v, linv, ctx, a_own, a_par, x1, x2, x3, xm, hm, vec, b_up_pair, dy = attention_forward(
        tokens, out_grad, own_vec, w_query, w_key, w_value,
        b_qv, w_dense, lows, pad_row, alibi,
    )
    xs = [tokens, x1, x2, x3]

    bits = dp_bits()
    order_a = bits if size == 8 else bits[::-1]
    order_b = [2, 4, 1] if size == 8 else [bits[-2], bits[-1], *bits[:-2][::-1]]
    mk, ms, gn, h1, gu, su, gd, sd, up_sums, ru = feed_forward(
        a_own, a_par, xm, dy, vec, b_up_pair, w_up, w_down, w_other, (order_a[0], order_b[0]), part
    )
    output, _, tokens_grad, w_up_grad, w_down_grad, g_qk, g_vd, sums = attention_backward(
        xs, h1, gn, mk, ms, dy, gu, gd, ru, su, sd, up_sums, hm, p, q, linv, ctx, k, v, vec,
        w_query, w_key, w_value, w_dense, (order_a, order_b), part,
    )
    w_down_grad = w_down_grad.T
    head_max = sums[12, :LH]
    column_scale = jnp.repeat(jnp.sqrt(TAU / jnp.maximum(head_max, TAU)), HD)
    return (
        output,
        tokens_grad,
        sums[8],
        sums[9],
        g_qk[:, :SHARE],
        sums[10],
        g_qk[:, SHARE:],
        g_vd[:, :SHARE],
        sums[11],
        g_vd[:, SHARE:].T,
        sums[2],
        sums[0],
        sums[1],
        w_up_grad,
        sums[4:8].reshape(UNITS),
        w_down_grad,
        sums[3],
        head_max,
        w_query.astype(F32) * column_scale,
        b_query.astype(F32) * column_scale,
        w_key.astype(F32) * column_scale,
    )


def solution(mesh):
    in_specs = (
        P("dp", "tensor"),
        P("dp", "tensor"),
        P("dp", None),
        P("dp", None),
        P("tensor"),
        P("tensor"),
        P(None, "tensor"),
        P("tensor"),
        P(None, "tensor"),
        P(None, "tensor"),
        P("tensor"),
        P("tensor", None),
        P("tensor"),
        P("tensor"),
        P("tensor"),
        P(None, "tensor"),
        P("tensor"),
        P("tensor", None),
        P("tensor"),
    )
    out_specs = (
        P("dp", "tensor"),
        P("dp", "tensor"),
        P("tensor"),
        P("tensor"),
        P("dp", "tensor"),
        P("tensor"),
        P("dp", "tensor"),
        P("dp", "tensor"),
        P("tensor"),
        P("tensor", "dp"),
        P("tensor"),
        P("tensor"),
        P("tensor"),
        P("dp", "tensor"),
        P("tensor"),
        P("tensor", "dp"),
        P("tensor"),
        P("tensor"),
        P(None, "tensor"),
        P("tensor"),
        P(None, "tensor"),
    )
    return jax.shard_map(shards, mesh=mesh, in_specs=in_specs, out_specs=out_specs, check_vma=False)
```

```python
import functools
import math

import jax
import jax.numpy as jnp
from jax import lax
from jax.experimental import pallas as pl
from jax.experimental.pallas import tpu as pltpu
from jax.sharding import PartitionSpec as P

HEADS = 16
HD = 64
WIN = 1024
D = 1024
FF = 4096
SEQ = 2048
B = 256
NB = SEQ // B
SLOTS = WIN // B + 1
STRIP = SLOTS * B
LH = 4
SHARE = LH * HD
UNITS = FF // 4
TILE = 512
OWN = SEQ // 2

EPS = 1e-05
TAU = 2.0
NEG = -1e30
F32 = jnp.float32
BF = jnp.bfloat16
VMEM_LIMIT = 62 * 2**20


def dot(a, b):
    return jnp.dot(a, b, preferred_element_type=F32)


def dot_nt(a, b):
    return lax.dot_general(a, b, (((1,), (1,)), ((), ())), preferred_element_type=F32)


def params():
    return pltpu.CompilerParams(
        dimension_semantics=("arbitrary",), vmem_limit_bytes=VMEM_LIMIT
    )


def feature_block(rank):
    return pl.ds(pl.multiple_of(rank * SHARE, SHARE), SHARE)


def head_of_lane(shape):
    return lax.broadcasted_iota(jnp.int32, shape, 1) // HD


def ordered(kernel, count):
    return lambda ids, *refs: kernel(ids, *refs[count:])


def waits(after):
    return [pl.BlockSpec(memory_space=pl.ANY)] * len(after)


def row_stats(rows):
    mean = jnp.sum(rows, axis=1, keepdims=True) / D
    square = jnp.sum(rows * rows, axis=1, keepdims=True) / D
    return mean, lax.rsqrt(square - mean * mean + EPS)


def piece(j, bit, chunk):
    inner = bit * chunk
    mine = dp_bit(bit)
    base = (j * 128) // inner * (2 * inner) + (j * 128) % inner
    return [
        pl.ds(pl.multiple_of(base + side * inner, 128), 128) for side in (mine, 1 - mine)
    ]


def dp_bit(bit):
    return lax.rem(lax.div(lax.axis_index("dp"), bit), 2)


def dp_partner(bit):
    return lax.axis_index("dp") + bit - 2 * bit * dp_bit(bit)


def place():
    t = lax.axis_index("tensor")
    core, y = lax.rem(t, 2), lax.div(t, 2)
    return core, y, (t, 2 * y + 1 - core, 2 * (1 - y) + core, 2 * (1 - y) + 1 - core)


def remote(src, dst, send, got, where):
    return pltpu.make_async_remote_copy(
        src_ref=src, dst_ref=dst, send_sem=send, recv_sem=got,
        device_id=where, device_id_type=pl.DeviceIdType.MESH,
    )


def greet(places):
    barrier = pltpu.get_barrier_semaphore()
    for where in places:
        pl.semaphore_signal(
            barrier, inc=1, device_id=where, device_id_type=pl.DeviceIdType.MESH
        )
    pl.semaphore_wait(barrier, len(places))


def block_rows(b):
    return pl.ds(pl.multiple_of(b * B, B), B)


def remote_params(collective_id):
    return pltpu.CompilerParams(
        dimension_semantics=("arbitrary",),
        vmem_limit_bytes=VMEM_LIMIT,
        collective_id=collective_id,
        has_side_effects=True,
    )


def split_store(keep_ref, send_ref, value_ref, core):
    for half in range(2):
        cols = slice(half * SHARE, (half + 1) * SHARE)
        keep_ref[:, cols] = value_ref[:, feature_block(2 * half + core)].astype(keep_ref.dtype)
        send_ref[:, cols] = value_ref[:, feature_block(2 * half + 1 - core)].astype(
            send_ref.dtype
        )


TAIL = 3


def fwd_kernel(
    x_any, g_any, x_own, own_vec, wq, wk, wv, bqv, wd, lo, pad, alibi,
    p_ref, q_ref, k_ref, v_ref, linv_ref, ctx_ref, a_ref, b_ref, x1_ref, x2_ref, x3_ref, xm_ref, hm_ref, vec, bup_ref, dy_any,
    xs, qm_s, k_s, va_s, u_s, res_s, lo_s,
    xc, xy, xf, part_keep, part_send, part_got, sum_keep, sum_send, sum_got, whole_own, whole_got,
    v_all,
    s_xc, r_xc, s_xy, r_xy, s_xf, r_xf, s_pc, r_pc, s_sy, r_sy, s_wc, r_wc,
    s_v, r_v, l_d, s_dc, r_dc, s_dy, r_dy, s_df, r_df,
):
    step = pl.program_id(0)
    core, y, ranks = place()

    rows = block_rows
    beside, across = {"tensor": ranks[1]}, {"tensor": ranks[2]}

    def to_core(b):
        return remote(x_any.at[rows(b)], xc.at[b], s_xc.at[b], r_xc.at[b], beside)

    def to_y(b):
        return remote(x_any.at[rows(b)], xy.at[b], s_xy.at[b], r_xy.at[b], across)

    def forward(b):
        return remote(xy.at[b], xf.at[b], s_xf.at[b], r_xf.at[b], beside)

    def part_to_core(b):
        return remote(part_send.at[b], part_got.at[b], s_pc.at[b], r_pc.at[b], beside)

    def sum_to_y(j):
        return remote(sum_send.at[j], sum_got.at[j], s_sy.at[j], r_sy.at[j], across)

    def whole_to_core(j):
        return remote(whole_own.at[j], whole_got.at[j], s_wc.at[j], r_wc.at[j], beside)

    def vectors(r):
        return remote(v_all.at[0], v_all.at[r], s_v.at[r - 1], r_v.at[r - 1], {"tensor": ranks[r]})

    mine = feature_block(ranks[0])

    def dy_own(j):
        return pltpu.make_async_copy(g_any.at[rows(2 * j + y)], dy_any.at[rows(j), mine], l_d.at[j])

    def dy_core(j):
        return remote(g_any.at[rows(2 * j + y)], dy_any.at[rows(j), mine], s_dc.at[j], r_dc.at[j], beside)

    def dy_y(j):
        return remote(g_any.at[rows(2 * j + 1 - y)], dy_any.at[rows(j), mine], s_dy.at[j], r_dy.at[j], across)

    def dy_forward(j):
        block = dy_any.at[rows(j), feature_block(ranks[2])]
        return remote(block, block, s_df.at[j], r_df.at[j], beside)

    @pl.when(step == 0)
    def _():
        v_all[0] = own_vec[...]
        greet((beside, across, {"tensor": ranks[3]}))
        for r in range(1, 4):
            vectors(r).start()
        for b in range(5):
            to_y(b).start()
            to_core(b).start()
        for r in range(1, 4):
            vectors(r).wait_recv()
        for r in range(4):
            vec[:, feature_block(ranks[r])] = v_all[r, 0:8, :]
        bup_ref[...] = jnp.zeros(bup_ref.shape, F32)
        for n, r in enumerate((0, 2)):
            for part in range(4):
                bup_ref[n : n + 1, part * SHARE : (part + 1) * SHARE] = v_all[r, 8 + part : 9 + part, :]
        to_y(0).wait_recv()
        forward(0).start()
        hm_ref[...] = jnp.full(hm_ref.shape, NEG, F32)

    for b in range(5, NB):

        @pl.when(step == b - 4)
        def _():
            to_y(b).start()
            to_core(b).start()

    row_i = lax.broadcasted_iota(jnp.int32, (B, B), 0)
    col_i = lax.broadcasted_iota(jnp.int32, (B, B), 1)
    lanes = head_of_lane((B, SHARE))

    for j in range(NB // 2):

        @pl.when(step == j + 4)
        def _():
            dy_own(j).start()
            dy_core(j).start()
            dy_y(j).start()

        @pl.when(step == j + 7)
        def _():
            dy_y(j).wait_recv()
            dy_forward(j).start()

    @pl.when(step < NB - 1)
    def _():
        to_y(step + 1).wait_recv()
        forward(step + 1).start()

    @pl.when(step < NB)
    def _():
        to_core(step).wait_recv()
        forward(step).wait_recv()
        blocks = (x_own[...], xc[step], xy[step], xf[step])
        for rank, block, ref in zip(ranks, blocks, (None, x1_ref, x2_ref, x3_ref)):
            xs[:, feature_block(rank)] = block.astype(F32)
            if ref is not None:
                ref[...] = block
        value = xs[...]

        @pl.when(lax.rem(step, 2) == y)
        def _():
            xm_ref[rows(step // 2), :] = value.astype(BF)

        mean, rstd = row_stats(value)
        n1 = ((value - mean) * rstd * vec[0:1, :] + vec[1:2, :]).astype(BF)
        q = (dot(n1, wq[...]) + bqv[0:1, :]).astype(BF)
        k = dot(n1, wk[...]).astype(BF)
        v = (dot(n1, wv[...]) + bqv[1:2, :]).astype(BF)
        qs = q * jnp.asarray(1.0 / math.sqrt(HD), BF)
        q_ref[...] = qs
        k_ref[...] = k
        v_ref[...] = v
        here = rows(step)
        k_s[here, :] = k
        for h in range(LH):
            qm_s[h] = jnp.where(lanes == h, qs, jnp.zeros_like(qs))
            va_s[h, here, :] = jnp.where(lanes == h, v, jnp.ones_like(v))
        lo_s[...] = jnp.broadcast_to(lo[...], (B, B))

    def attend(nb):
        start = pl.multiple_of((step + 1 - nb) * B, B)

        def head(h, carry):
            qm = qm_s[h]
            top = jnp.full((B, 128), NEG, F32)
            biggest = hm_ref[h]
            for r in range(nb):
                slot = SLOTS - nb + r
                base = pl.multiple_of(start + r * B, B)
                s = dot_nt(qm, k_s[pl.ds(base, B), :])
                inside = col_i + base >= lo_s[...]
                shut = pad[0:1, pl.ds(base, B)]
                if r == nb - 1:
                    s = jnp.where(row_i == col_i, s, s + shut)
                    s = jnp.where(inside & (col_i <= row_i), s, NEG)
                else:
                    s = jnp.where(inside, s + shut, NEG)
                biggest = jnp.maximum(biggest, jnp.max(s.reshape(B // 8, 8, B), axis=0))
                s = s + alibi[pl.ds(h, 1), slot * B : (slot + 1) * B]
                u_s[:, slot * B : (slot + 1) * B] = s
                top = jnp.maximum(top, jnp.maximum(s[:, :128], s[:, 128:]))
            hm_ref[h] = biggest
            top = jnp.max(top, axis=1, keepdims=True)
            for r in range(nb):
                slot = SLOTS - nb + r
                cols = slice(slot * B, (slot + 1) * B)
                p_ref[h, :, cols] = jnp.exp(u_s[:, cols] - top).astype(BF)
            res_s[h] = dot(p_ref[h, :, (SLOTS - nb) * B :], va_s[h, pl.ds(start, nb * B), :])
            return carry

        lax.fori_loop(0, LH, head, 0, unroll=True)

    for nb in range(1, SLOTS):
        pl.when(step == nb - 1)(functools.partial(attend, nb))
    pl.when((step >= SLOTS - 1) & (step < NB))(functools.partial(attend, SLOTS))

    @pl.when(step < NB)
    def _():
        ctx = res_s[0]
        total = res_s[LH - 1]
        for h in range(1, LH):
            ctx = jnp.where(lanes == h, res_s[h], ctx)
            total = jnp.where(lanes == h, res_s[h - 1], total)
        inv = 1.0 / pltpu.roll(total, SHARE - HD, 1)
        linv_ref[...] = inv
        ctx = (ctx * inv).astype(BF)
        ctx_ref[...] = ctx
        xs[...] = dot(ctx, wd[...])
        split_store(part_keep.at[step], part_send.at[step], xs, core)
        part_to_core(step).start()

    @pl.when((step >= 1) & (step <= NB))
    def _():
        b = step - 1
        j = b // 2
        part_to_core(b).wait_recv()
        total = part_keep[b].astype(F32) + part_got[b].astype(F32)

        @pl.when(lax.rem(b, 2) == y)
        def _():
            sum_keep[j] = total

        @pl.when(lax.rem(b, 2) != y)
        def _():
            sum_send[j] = total.astype(BF)
            sum_to_y(j).start()

    @pl.when((step >= TAIL) & (lax.rem(step + NB - TAIL, 2) == y))
    def _():
        j = (step - TAIL) // 2
        sum_to_y(j).wait_recv()
        total = (sum_keep[j] + sum_got[j].astype(F32)).astype(BF)
        whole_own[j] = total
        a_ref[rows(j), :] = total
        whole_to_core(j).start()

    @pl.when(step == NB + TAIL - 1)
    def _():
        for j in range(NB // 2):
            whole_to_core(j).wait_recv()
            b_ref[rows(j), :] = whole_got[j]
        for b in range(NB):
            to_core(b).wait_send()
            to_y(b).wait_send()
            forward(b).wait_send()
            part_to_core(b).wait_send()
        for j in range(NB // 2):
            sum_to_y(j).wait_send()
            whole_to_core(j).wait_send()
            dy_own(j).wait()
            dy_core(j).wait()
            dy_y(j).wait_send()
            dy_forward(j).wait()
        for r in range(1, 4):
            vectors(r).wait_send()


def attention_forward(x, g, own_vec, wq, wk, wv, bqv, wd, lo, pad, alibi):
    last = lambda s: jnp.minimum(s, NB - 1)
    row = lambda width: pl.BlockSpec((B, width), lambda s: (last(s), 0))
    whole = lambda shape: pl.BlockSpec(shape, lambda s: (0,) * len(shape))
    like = jax.ShapeDtypeStruct
    dma = lambda n: pltpu.SemaphoreType.DMA((n,))
    half = NB // 2
    return pl.pallas_call(
        fwd_kernel,
        grid=(NB + TAIL,),
        in_specs=[pl.BlockSpec(memory_space=pl.ANY)] * 2
        + [row(SHARE), whole((16, SHARE))]
        + [whole((D, SHARE))] * 3
        + [whole((8, SHARE)), whole((SHARE, D)), row(1), whole((8, SEQ)), whole((8, STRIP))],
        out_specs=[pl.BlockSpec((LH, B, STRIP), lambda s: (0, last(s), 0))]
        + [row(SHARE)] * 5
        + [whole((OWN, D // 2))] * 2
        + [row(SHARE)] * 3
        + [whole((OWN, D)), whole((LH, 8, B)), whole((8, D)), whole((8, UNITS))]
        + [pl.BlockSpec(memory_space=pl.ANY)],
        scratch_shapes=[
            pltpu.VMEM((B, D), F32),
            pltpu.VMEM((LH, B, SHARE), BF),
            pltpu.VMEM((SEQ, SHARE), BF),
            pltpu.VMEM((LH, SEQ, SHARE), BF),
            pltpu.VMEM((B, STRIP), F32),
            pltpu.VMEM((LH, B, SHARE), F32),
            pltpu.VMEM((B, B), jnp.int32),
        ]
        + [pltpu.VMEM((NB, B, SHARE), BF)] * 3
        + [pltpu.VMEM((NB, B, D // 2), BF)] * 3
        + [pltpu.VMEM((half, B, D // 2), F32)]
        + [pltpu.VMEM((half, B, D // 2), BF)] * 4
        + [pltpu.VMEM((4, 16, SHARE), F32)]
        + [dma(NB)] * 8
        + [dma(half)] * 4
        + [dma(3)] * 2
        + [dma(half)] * 7,
        out_shape=[like((LH, SEQ, STRIP), BF)]
        + [like((SEQ, SHARE), BF)] * 3
        + [like((SEQ, SHARE), F32), like((SEQ, SHARE), BF)]
        + [like((OWN, D // 2), BF)] * 2
        + [like((SEQ, SHARE), BF)] * 3
        + [like((OWN, D), BF), like((LH, 8, B), F32), like((8, D), F32), like((8, UNITS), F32)]
        + [like((OWN, D), BF)],
        compiler_params=remote_params(0),
        cost_estimate=pl.CostEstimate(
            flops=16 * 10**9, bytes_accessed=40 * 2**20, transcendentals=8 * 10**6
        ),
        name="attention_forward",
    )(x, g, x, own_vec, wq, wk, wv, bqv, wd, lo, pad, alibi)


def mlp_kernel(
    a_own, a_par, xm, dy_s, vec, bup, wu0, wu1, wd0, wd1,
    mk_ref, ms_ref, gn_ref, h1_ref, gu_ref, su_ref, gd_ref, sd_ref, bs_ref, ru_ref,
    n2_s, n2t_s, dyt_s, dyo_s, am_s, ag_s, act_s, gp_s, us_s, s_u, r_u,
    *, bits, chunk,
):
    i = pl.program_id(0)
    core, y, ranks = place()
    partners = [{"dp": dp_partner(bit)} for bit in bits]

    def send_tile(n, kind):
        return remote(us_s.at[n], ru_ref.at[n], s_u.at[n], r_u.at[n], partners[kind])

    @pl.when(i == 0)
    def _():
        greet(partners)

        def assemble(rb, carry):
            rows = block_rows(rb)
            h1_ref[rows, :] = xm[rows, :].astype(F32)
            for part, a in ((core, a_own), (1 - core, a_par)):
                for half in range(2):
                    cols = feature_block(2 * half + part)
                    h1_ref[rows, cols] += a[rows, half * SHARE : (half + 1) * SHARE].astype(F32)
            value = h1_ref[rows, :] + vec[2:3, :]
            h1_ref[rows, :] = value
            mean, rstd = row_stats(value)
            n2 = ((value - mean) * rstd * vec[3:4, :] + vec[4:5, :]).astype(BF)
            n2_s[rows, :] = n2
            for source, turned, bit in (
                (n2_s, n2t_s, bits[0]), (dy_s, dyt_s, bits[0]), (dy_s, dyo_s, bits[1])
            ):
                for j in range(D // 256):
                    for side, cols in enumerate(piece(j, bit, chunk)):
                        to = slice(side * (D // 2) + j * 128, side * (D // 2) + (j + 1) * 128)
                        turned[to, rows] = source[rows, cols].T
            am_s[rows, :] = jnp.zeros((B, D), F32)
            ag_s[rows, :] = jnp.zeros((B, D), F32)
            return carry

        lax.fori_loop(0, OWN // B, assemble, 0)

    def tile(wu, wd, which):
        bias = bup[which : which + 1, pl.ds(pl.multiple_of(lax.rem(i, 2) * TILE, TILE), TILE)]
        scale = math.sqrt(2.0 / math.pi)

        def rows_of(rb, sums):
            rows = pl.ds(pl.multiple_of(rb * B, B), B)
            pre = dot(n2_s[rows, :], wu[...]) + bias
            back = dot_nt(dy_s[rows, :], wd[...])
            square = pre * pre
            th = jnp.tanh(scale * pre * (1.0 + 0.044715 * square))
            half = 0.5 * (1.0 + th)
            act = (pre * half).astype(BF)
            slope = half + 0.5 * pre * (1.0 - th * th) * (scale + (3 * 0.044715 * scale) * square)
            gp = (slope * back).astype(BF)
            act_s[rows, :] = act
            gp_s[rows, :] = gp
            am_s[rows, :] += dot(act, wd[...])
            ag_s[rows, :] += dot_nt(gp, wu[...])
            return sums + jnp.sum(gp.astype(F32), axis=0, keepdims=True)

        sums = lax.fori_loop(0, OWN // B, rows_of, jnp.zeros((1, TILE), F32))
        bs_ref[...] = jnp.broadcast_to(sums, bs_ref.shape)

        def grads(left, right, keep, send):
            keep[...] = dot(left[0 : D // 2, :], right[...]).astype(BF)
            send[...] = dot(left[D // 2 :, :], right[...]).astype(BF)

        first = which == 0
        grads(n2t_s, gp_s, gu_ref, us_s.at[i] if first else su_ref)
        if first:
            send_tile(i, 0).start()
        grads(dyo_s if first else dyt_s, act_s, gd_ref, us_s.at[2 + i] if first else sd_ref)
        if first:
            send_tile(2 + i, 1).start()

    pl.when(i < 2)(lambda: tile(wu0, wd0, 0))
    pl.when(i >= 2)(lambda: tile(wu1, wd1, 1))

    @pl.when(i == 3)
    def _():
        split_store(mk_ref, ms_ref, am_s, core)
        gn_ref[...] = ag_s[...].astype(BF)
        for n in range(4):
            send_tile(n, n // 2).wait()


def feed_forward(a_own, a_par, xm, dy, vec, bup, wu0, wd0, w_other, bits, chunk):
    whole = lambda shape: pl.BlockSpec(shape, lambda i: (0,) * len(shape))
    low = lambda i: jnp.minimum(i, 1)
    high = lambda i: jnp.maximum(i - 2, 0)
    like = jax.ShapeDtypeStruct
    tile = pl.BlockSpec((D // 2, TILE), lambda i: (0, i))
    return pl.pallas_call(
        functools.partial(mlp_kernel, bits=bits, chunk=chunk),
        grid=(4,),
        in_specs=[whole((OWN, D // 2))] * 2
        + [whole((OWN, D))] * 2
        + [
            whole((8, D)),
            whole((8, UNITS)),
            pl.BlockSpec((D, TILE), lambda i: (0, low(i))),
            pl.BlockSpec((D, TILE), lambda i: (0, high(i))),
            pl.BlockSpec((TILE, D), lambda i: (low(i), 0)),
            pl.BlockSpec((TILE, D), lambda i: (high(i), 1)),
        ],
        out_specs=[whole((OWN, D // 2))] * 2
        + [whole((OWN, D))] * 2
        + [
            tile,
            pl.BlockSpec((D // 2, TILE), lambda i: (0, high(i))),
            tile,
            pl.BlockSpec((D // 2, TILE), lambda i: (0, high(i))),
            pl.BlockSpec((8, TILE), lambda i: (0, i)),
            pl.BlockSpec(memory_space=pl.ANY),
        ],
        scratch_shapes=[
            pltpu.VMEM((OWN, D), BF),
            pltpu.VMEM((D, OWN), BF),
            pltpu.VMEM((D, OWN), BF),
            pltpu.VMEM((D, OWN), BF),
            pltpu.VMEM((OWN, D), F32),
            pltpu.VMEM((OWN, D), F32),
            pltpu.VMEM((OWN, TILE), BF),
            pltpu.VMEM((OWN, TILE), BF),
            pltpu.VMEM((4, D // 2, TILE), BF),
            pltpu.SemaphoreType.DMA((4,)),
            pltpu.SemaphoreType.DMA((4,)),
        ],
        out_shape=[like((OWN, D // 2), BF)] * 2
        + [
            like((OWN, D), BF),
            like((OWN, D), F32),
            like((D // 2, 2 * UNITS), BF),
            like((D // 2, UNITS), BF),
            like((D // 2, 2 * UNITS), BF),
            like((D // 2, UNITS), BF),
            like((8, 2 * UNITS), F32),
            like((4, D // 2, TILE), BF),
        ],
        compiler_params=remote_params(1),
        cost_estimate=pl.CostEstimate(
            flops=26 * 10**9, bytes_accessed=40 * 2**20, transcendentals=2 * 10**6
        ),
        name="feed_forward",
    )(a_own, a_par, xm, dy, vec, bup, wu0, w_other, wd0, w_other)


LEAD = 2
FINAL = 3
TILES = (("u", 0), ("u", 1), ("d", 0), ("d", 1), ("u", 2), ("d", 2), ("d", 3), ("u", 3), *(("a", n) for n in range(4)))
OTHER_ORDER = (2, 3, 11)
FIRST = (0, 1, 0, 2, 3, 4, 6, 7)
USE = sorted(range(8), key=lambda p: (FIRST[p], p))
SLOT = [USE.index(p) % 2 for p in range(8)] + [0, 0, 1, 1]
PAIRS = ((0, 4), (1, 7), (2, 5), (3, 6))
DRAIN = LEAD + FINAL + NB


def step_of(p, n, levels):
    if p < 8:
        return FIRST[p] + 3 * (n - 1)
    if n <= 2:
        return ((11, 12, 13, 11), (13, 14, 14, 13))[n - 1][p - 8]
    free = step_of(p - 4, n + 1, levels) if n < levels else 0
    return max(step_of(p, n - 1, levels) + 1, free)


def last_step(levels):
    return max(DRAIN + levels - 1, max(step_of(p, levels, levels) for p in range(7, 12)))


def bwd_kernel(
    x0, x1, x2, x3, x_late, h1, gn, gn_any, mk, ms_any, dy_in, gu, gd, ru, su_any, sd_any, up_sums, hm,
    p_ref, q_ref, linv_ref, ctx_ref, k_ref, v_ref, vec, wq, wk, wv, wd,
    out_any, os_any, tg_ref, wu_ref, wdn_ref, wqk_ref, wvd_ref, vt_ref,
    w_s, gh_s, gm_s, gt_s, qt_s, dl_s, ds_s, res_s, dkt_s, dvt_s, acc_s,
    o_s, gn_got, mr_got, gh_own, gh_y, gh_f,
    part_keep, part_send, part_got, sum_keep, sum_send, sum_got, ghx_s, st_keep, st_got, st_sum, st_all,
    gk, ru_s, g1, y_send, y_got, y_keep, cs_ref, bs_ref, n1_ref, v_keep, v_send, v_away, v_sum, v_got,
    *rest, orders, chunk,
):
    levels = len(orders[0])
    stages = [rest[3 * n : 3 * n + 3] for n in range(levels - 1)]
    (
        s_gn, r_gn, s_mr, r_mr, s_gy, r_gy, s_gf, r_gf, s_pc, r_pc, s_sy, r_sy,
        s_tc, r_tc, s_ty, r_ty, s_g1, r_g1, s_yy, r_yy, l_g, l_r, s_gw, r_gw, s_va, r_va, s_vt, r_vt, l_o, s_o, r_o, *g_sems,
    ) = rest[3 * (levels - 1) :]
    step = pl.program_id(0)
    b = NB - 1 - (step - LEAD)
    core, y, ranks = place()
    beside, across = {"tensor": ranks[1]}, {"tensor": ranks[2]}
    order_of = lambda p: orders[1 if p in OTHER_ORDER else 0]
    partner = lambda bit: {"dp": dp_partner(bit)}
    half = NB // 2
    last = last_step(levels)
    lanes = head_of_lane((B, SHARE))

    send_gn = lambda j: remote(gn_any.at[block_rows(j)], gn_got.at[j], s_gn.at[j], r_gn.at[j], beside)
    send_mr = lambda j: remote(ms_any.at[block_rows(j)], mr_got.at[j], s_mr.at[j], r_mr.at[j], beside)
    send_gy = lambda j, side: remote(
        gh_own.at[j, :, feature_block(2 * side + core)],
        gh_y.at[j, :, side * SHARE : (side + 1) * SHARE],
        s_gy.at[2 * j + side], r_gy.at[2 * j + side], across,
    )
    send_gf = lambda j: remote(gh_y.at[j], gh_f.at[j], s_gf.at[j], r_gf.at[j], beside)
    store_out = lambda j, side: pltpu.make_async_copy(
        o_s.at[lax.rem(j, 2), side],
        (out_any.at[block_rows(2 * j + y)], os_any.at[block_rows(j)])[side],
        l_o.at[2 * lax.rem(j, 2) + side],
    )
    send_out = lambda j: remote(
        os_any.at[block_rows(j)], out_any.at[block_rows(2 * j + y)], s_o.at[j], r_o.at[j], across
    )
    send_part = lambda n: remote(part_send.at[lax.rem(n, 3)], part_got.at[n], s_pc.at[n], r_pc.at[n], beside)
    send_sum = lambda n: remote(sum_send.at[n], sum_got.at[n], s_sy.at[n], r_sy.at[n], across)
    send_tc = lambda n: remote(st_keep.at[n], st_got.at[n], s_tc.at[n], r_tc.at[n], beside)
    send_ty = lambda n: remote(st_sum.at[n], st_all.at[n], s_ty.at[n], r_ty.at[n], across)

    def tile_of(p):
        kind, n = TILES[p]
        return slice(n * TILE, (n + 1) * TILE), kind == "u"

    span = lambda p: slice(0, TILE) if p < 8 else slice((p - 8) % 2 * SHARE, ((p - 8) % 2 + 1) * SHARE)
    wide = lambda p: slice(0, TILE if p < 8 else SHARE)
    shared = lambda p: p if p < 8 else 8 + (p - 8) // 2

    def send_first(p):
        cols, up = tile_of(p)
        src = (su_any if up else sd_any).at[:, slice(cols.start - UNITS, cols.stop - UNITS)]
        return remote(src, g1.at[p - 4], s_g1.at[p - 4], r_g1.at[p - 4], partner(order_of(p)[0]))

    def send_weights(p, part):
        n = 2 * (p - 8) + part
        return remote(
            gn_got.at[p - 8, :, slice(part * SHARE, (part + 1) * SHARE)],
            g1.at[4 + (p - 8) // 2, block_rows(part), span(p)],
            s_gw.at[n], r_gw.at[n], partner(order_of(p)[0]),
        )

    slot = SLOT

    def load_keep(p):
        cols, up = tile_of(p)
        return pltpu.make_async_copy((gu if up else gd).at[:, cols], gk.at[slot[p]], l_g.at[slot[p]])

    def load_got(p):
        return pltpu.make_async_copy(ru.at[p], ru_s.at[slot[p]], l_r.at[slot[p]])

    def send_stage(p, n):
        _, send, got = stages[n - 1]
        return remote(
            send.at[p % 4, :, wide(p)], got.at[shared(p), :, span(p)], g_sems[2 * n - 2].at[p], g_sems[2 * n - 1].at[p], partner(order_of(p)[n])
        )

    send_last = lambda n: remote(y_send.at[n], y_got.at[n], s_yy.at[n], r_yy.at[n], across)

    def split(p, n):
        order = order_of(p)
        if n == 1:
            keep = lambda rows: gk[slot[p], rows, span(p)]
            if p < 4:
                load_got(p).wait()
                got = lambda rows: ru_s[slot[p], rows, :]
            else:
                got = lambda rows: g1[shared(p) - 4, rows, span(p)]
            if p < 8:
                load_keep(p).wait()
            if 4 <= p < 8:
                send_first(p).wait_recv()
            if p >= 8:
                send_weights(p, 0).wait_recv()
                send_weights(p, 1).wait_recv()
        else:
            send_stage(p, n - 1).wait_recv()
            keep = lambda rows: stages[n - 2][0][p % 4, rows, wide(p)]
            got = lambda rows: stages[n - 2][2][shared(p), rows, span(p)]
        size = D >> n
        following = order[n]
        inner = chunk
        for other in order[n + 1 :]:
            inner *= 2 if other < following else 1
        mine = dp_bit(following)
        if p >= 4:
            send_stage(p - 4, n).wait_send()
        for group in range(size // (2 * inner)):
            to = slice(group * inner, (group + 1) * inner)
            for side, ref in ((mine, stages[n - 1][0]), (1 - mine, stages[n - 1][1])):
                rows = pl.ds(pl.multiple_of(group * 2 * inner + side * inner, inner), inner)
                ref[p % 4, to, wide(p)] = (keep(rows).astype(F32) + got(rows).astype(F32)).astype(BF)
        send_stage(p, n).start()

    def whole_tile(p):
        send_stage(p, levels - 1).wait_recv()
        keep, _, got = stages[levels - 2]
        total = keep[p % 4, :, wide(p)].astype(F32) + got[shared(p), :, span(p)].astype(F32)
        if p >= 8:
            (wqk_ref, wvd_ref)[(p - 8) // 2][:, span(p)] = total
        for n, (own, other) in enumerate(PAIRS):
            cols, up = tile_of(own)
            if p == own:
                if up:
                    wu_ref[:, cols] = total
                else:
                    y_keep[n - 2] = total
            if p == other:
                y_send[n] = total.astype(BF)
                send_last(n).start()

    def close(n):
        cols, up = tile_of(PAIRS[n][0])
        send_last(n).wait_recv()
        if up:
            wu_ref[:, cols] += y_got[n].astype(F32)
        else:
            wdn_ref[cols, :] = (y_keep[n - 2] + y_got[n].astype(F32)).T

    @pl.when(step == 0)
    def _():
        greet([beside, across] + [partner(bit) for bit in orders[0]])
        for j in range(half - 1, -1, -1):
            send_gn(j).start()
            send_mr(j).start()
        for p in range(4, 8):
            send_first(p).start()
        for p in USE[:2]:
            load_keep(p).start()
            load_got(p).start()
        cs_ref[...] = jnp.zeros(cs_ref.shape, F32)
        bs_ref[...] = jnp.zeros(bs_ref.shape, F32)
        n1_ref[...] = jnp.zeros(n1_ref.shape, F32)

    @pl.when(step == 1)
    def _():
        dkt_s[...] = jnp.zeros(dkt_s.shape, F32)
        dvt_s[...] = jnp.zeros(dvt_s.shape, F32)
        acc_s[...] = jnp.zeros(acc_s.shape, F32)

    @pl.when(step < half)
    def _():
        j = half - 1 - step
        send_gn(j).wait_recv()
        send_mr(j).wait_recv()
        dy = dy_in[...].astype(F32)
        value = h1[...]

        def out(side):
            part = pl.ds(pl.multiple_of(side * SHARE, SHARE), SHARE)
            cols = feature_block(2 * side + core)
            total = mk[:, part].astype(F32) + mr_got[j, :, part].astype(F32)
            return (h1[:, cols] + total + vec[5:6, cols]).astype(BF)


        @pl.when(step >= 2)
        def _():
            for side in range(2):
                store_out(j + 2, side).wait()

        for side, which in enumerate((y, 1 - y)):
            o_s[lax.rem(j, 2), side] = out(which)
            store_out(j, side).start()
        mean, rstd = row_stats(value)
        xhat = (value - mean) * rstd
        grad = gn[...].astype(F32) + gn_got[j].astype(F32)
        scaled = grad * vec[3:4, :]
        first = jnp.sum(scaled, axis=1, keepdims=True) / D
        second = jnp.sum(scaled * xhat, axis=1, keepdims=True) / D
        gh = dy + rstd * (scaled - first - xhat * second)
        for n, columns in enumerate((grad * xhat, grad, gh, dy)):
            cs_ref[n : n + 1, :] += jnp.sum(columns, axis=0, keepdims=True)
        gh_own[j] = gh.astype(BF)
        send_gy(j, 0).start()
        send_gy(j, 1).start()

    @pl.when((step >= LEAD) & (step < LEAD + NB))
    def _():
        j = b // 2

        @pl.when(lax.rem(b, 2) == y)
        def _():
            gh_s[...] = gh_own[j]

        @pl.when(lax.rem(b, 2) != y)
        def _():
            send_gf(j).wait_recv()
            for part, ref in ((core, gh_y), (1 - core, gh_f)):
                for side in range(2):
                    gh_s[:, feature_block(2 * side + part)] = ref[j, :, side * SHARE : (side + 1) * SHARE]

        gc = dot_nt(gh_s[...], wd[...]).astype(BF).astype(F32)
        scaled = gc * linv_ref[...]
        gcs = scaled.astype(BF)
        product = scaled * ctx_ref[...].astype(F32)
        qt_s[...] = q_ref[...].T.reshape(LH, HD, B)
        gt_s[...] = gcs.T.reshape(LH, HD, B)
        for h in range(LH):
            gm_s[h] = jnp.where(lanes == h, gcs, jnp.zeros_like(gcs))
            delta = jnp.sum(jnp.where(lanes == h, product, 0.0), axis=1, keepdims=True)
            dl_s[h] = jnp.broadcast_to(delta, (B, 128))

    def attend(nb):
        start = pl.multiple_of((b + 1 - nb) * B, B)

        def head(h, carry):
            gm = gm_s[h]
            delta = jnp.concatenate([dl_s[h]] * 2, axis=1)
            for r in range(nb):
                slot = SLOTS - nb + r
                cols = slice(slot * B, (slot + 1) * B)
                dp = dot_nt(gm, v_ref[pl.ds(pl.multiple_of(start + r * B, B), B), :])
                ds_s[:, cols] = (p_ref[h, :, cols].astype(F32) * (dp - delta)).astype(BF)
            live = slice((SLOTS - nb) * B, STRIP)
            keys = pl.ds(start, nb * B)
            res_s[h] = dot(ds_s[:, live], k_ref[keys, :])
            dkt_s[h, :, keys] += dot(qt_s[h], ds_s[:, live])
            dvt_s[h, :, keys] += dot(gt_s[h], p_ref[h, :, live])
            return carry

        lax.fori_loop(0, LH, head, 0, unroll=2)

    pl.when((step >= LEAD) & (b >= SLOTS - 1))(functools.partial(attend, SLOTS))
    for nb in range(SLOTS - 1, 0, -1):
        pl.when(b == nb - 1)(functools.partial(attend, nb))

    @pl.when((step >= LEAD) & (step < LEAD + NB))
    def _():
        dq = res_s[0]
        for h in range(1, LH):
            dq = jnp.where(lanes == h, res_s[h], dq)
        dq = (dq * (1.0 / math.sqrt(HD))).astype(BF)
        here = block_rows(b)
        dk = dkt_s[:, :, here].reshape(SHARE, B).astype(BF).T
        dv = dvt_s[:, :, here].reshape(SHARE, B).astype(BF).T
        bs_ref[0:1, :] += jnp.sum(dq.astype(F32), axis=0, keepdims=True)
        bs_ref[1:2, :] += jnp.sum(dv.astype(F32), axis=0, keepdims=True)

        for rank, x in zip(ranks, (x0, x1, x2, x3)):
            w_s[:, feature_block(rank)] = x[...].astype(F32)
        value = w_s[...]
        mean, rstd = row_stats(value)
        xhat = (value - mean) * rstd
        n1t = (xhat * vec[0:1, :] + vec[1:2, :]).astype(BF).T
        acc_s[:, 0:SHARE] += dot(n1t, dq)
        acc_s[:, SHARE : 2 * SHARE] += dot(n1t, dk)
        acc_s[:, 2 * SHARE : 3 * SHARE] += dot(n1t, dv)
        acc_s[:, 3 * SHARE :] += dot(gh_s[...].T, ctx_ref[...])

        grad = dot_nt(dq, wq[...]) + dot_nt(dk, wk[...]) + dot_nt(dv, wv[...])
        scaled = grad * vec[0:1, :]
        first = jnp.sum(scaled, axis=1, keepdims=True)
        second = jnp.sum(scaled * xhat, axis=1, keepdims=True)
        column = lax.broadcasted_iota(jnp.int32, (B, 128), 1)
        packed = jnp.where(
            column == 0, first, jnp.where(column == 1, second, jnp.where(column == 2, mean, rstd))
        )
        st_keep[b] = packed.T[0:8, :]
        send_tc(b).start()
        w_s[...] = grad

        @pl.when(step >= LEAD + 3)
        def _():
            send_part(b + 3).wait_send()

        for n, side in enumerate((y, 1 - y)):
            cols = slice(n * SHARE, (n + 1) * SHARE)
            part_keep[lax.rem(b, 2), :, cols] = w_s[:, feature_block(2 * side + core)].astype(BF)
            part_send[lax.rem(b, 3), :, cols] = w_s[:, feature_block(2 * side + 1 - core)].astype(BF)
        send_part(b).start()
        ghx_s[lax.rem(b, 4)] = gh_s[:, feature_block(ranks[0])]

    @pl.when(step == LEAD + NB - 1)
    def _():
        for p in (11, 8, 9, 10):
            cols = slice((p - 8) * SHARE, (p - 7) * SHARE)
            for j in range(D // 256):
                mine, other = piece(j, order_of(p)[0], chunk)
                gk[slot[p], j * 128 : (j + 1) * 128, span(p)] = acc_s[mine, cols].astype(BF)
                into = slice(j // 2 * SHARE, (j // 2 + 1) * SHARE)
                gn_got[p - 8, j % 2 * 128 : (j % 2 + 1) * 128, into] = acc_s[other, cols].astype(BF)
            for part in range(2):
                send_weights(p, part).start()
        for j in range(half):
            send_out(j).start()

    send_away = lambda: remote(v_send, v_away, s_va.at[0], r_va.at[0], across)
    send_total = lambda n: remote(
        v_sum.at[n], v_got.at[n], s_vt.at[n], r_vt.at[n], partner(orders[0][n])
    )

    @pl.when(step == half)
    def _():
        for j in range(2):
            for side in range(2):
                store_out(j, side).wait()
        for ref, rank, side in ((v_keep, ranks[0], 0), (v_send, ranks[2], UNITS)):
            ref[0:4, :] = cs_ref[0:4, feature_block(rank)]
            for n in range(4):
                ref[4 + n : 5 + n, :] = up_sums[0:1, side + n * SHARE : side + (n + 1) * SHARE]
        send_away().start()

    @pl.when(step == half + 4)
    def _():
        send_away().wait_recv()
        v_sum[0, 0:8, :] = v_keep[...] + v_away[...]

    @pl.when((step >= LEAD + 1) & (step < LEAD + 1 + NB))
    def _():
        n = b + 1
        send_part(n).wait_recv()
        send_tc(n).wait_recv()
        keep = part_keep[lax.rem(n, 2)].astype(F32)
        sum_keep[lax.rem(n, 3)] = keep[:, :SHARE] + part_got[n, :, :SHARE].astype(F32)
        sum_send[n] = (keep[:, SHARE:] + part_got[n, :, SHARE:].astype(F32)).astype(BF)
        st_sum[n] = st_keep[n] + st_got[n]
        send_sum(n).start()
        send_ty(n).start()

    @pl.when((step >= LEAD + FINAL) & (step < LEAD + FINAL + NB))
    def _():
        n = b + FINAL
        send_sum(n).wait_recv()
        send_ty(n).wait_recv()
        grad = sum_keep[lax.rem(n, 3)] + sum_got[n].astype(F32)
        row = lax.broadcasted_iota(jnp.int32, (8, B), 0)
        stats = jnp.where(row < 2, st_sum[n] + st_all[n], st_keep[n])
        stats = jnp.concatenate([stats] * 16, axis=0).T
        xhat = (x_late[...].astype(F32) - stats[:, 2:3]) * stats[:, 3:4]
        scaled = grad * vec[0:1, feature_block(ranks[0])]
        inner = scaled - stats[:, 0:1] / D - xhat * (stats[:, 1:2] / D)
        tg_ref[...] = ghx_s[lax.rem(n, 4)].astype(F32) + stats[:, 3:4] * inner
        n1_ref[0:1, :] += jnp.sum(grad * xhat, axis=0, keepdims=True)
        n1_ref[1:2, :] += jnp.sum(grad, axis=0, keepdims=True)

    row16 = lax.broadcasted_iota(jnp.int32, (16, SHARE), 0)

    @pl.when(step == DRAIN - 1)
    def _():
        v_sum[0, 8:10, :] = n1_ref[0:2, :]
        v_sum[0, 10:12, :] = bs_ref[0:2, :]
        lane = lax.broadcasted_iota(jnp.int32, (4, SHARE), 1)
        top = jnp.full((4, SHARE), NEG, F32)
        for h in range(LH):
            top = jnp.where(lane == h, jnp.max(hm[h]), top)
        v_sum[0, 12:16, :] = top
        send_total(0).start()

    for n in range(levels):

        @pl.when(step == DRAIN + n)
        def _():
            send_total(n).wait_recv()
            mine, other = v_sum[n], v_got[n]
            total = jnp.where(row16 < 12, mine + other, jnp.maximum(mine, other))
            if n == levels - 1:
                vt_ref[...] = total
            else:
                v_sum[n + 1] = total
                send_total(n + 1).start()

    for j in range(half - 1, -1, -1):

        @pl.when(step == half - j)
        def _():
            send_gy(j, 0).wait_recv()
            send_gy(j, 1).wait_recv()
            send_gf(j).start()

    for p in range(12):
        for n in range(1, levels):
            pl.when(step == step_of(p, n, levels))(functools.partial(split, p, n))
        pl.when(step == step_of(p, levels, levels))(functools.partial(whole_tile, p))

    def load_next(p):
        load_keep(p).start()
        if p < 4:
            load_got(p).start()

    for n in range(2, 8):
        pl.when(step == FIRST[USE[n - 2]])(functools.partial(load_next, USE[n]))

    @pl.when(step == last)
    def _():
        for j in range(half):
            close(j)
            send_out(j).wait()
            for copy in (send_gn, send_mr, send_gf, send_last):
                copy(j).wait_send()
            for side in range(2):
                send_gy(j, side).wait_send()
            for level in range(1, levels):
                send_stage(8 + j, level).wait_send()
        for n in range(NB):
            for copy in (send_sum, send_tc, send_ty):
                copy(n).wait_send()
        for n in range(3):
            send_part(n).wait_send()
        for p in range(4, 8):
            send_first(p).wait_send()
        for p in range(8, 12):
            for part in range(2):
                send_weights(p, part).wait_send()
        send_away().wait_send()
        for n in range(levels):
            send_total(n).wait_send()


def attention_backward(
    xs, h1, gn, mk, ms, dy, gu, gd, ru, su, sd, up_sums, hm, p, q, linv, ctx, k, v, vec, wq, wk, wv, wd,
    orders, chunk,
):
    levels = len(orders[0])
    half = NB // 2
    block = lambda s: jnp.clip(NB - 1 + LEAD - s, 0, NB - 1)
    late = lambda s: jnp.clip(NB - 1 + LEAD + FINAL - s, 0, NB - 1)
    row = lambda width: pl.BlockSpec((B, width), lambda s: (block(s), 0))
    own = lambda width: pl.BlockSpec((B, width), lambda s: (jnp.maximum(half - 1 - s, 0), 0))
    once = pl.Buffered(1)
    whole = lambda *shape: pl.BlockSpec(shape, lambda s: (0,) * len(shape), pipeline_mode=once)
    anywhere = pl.BlockSpec(memory_space=pl.ANY)
    like = jax.ShapeDtypeStruct
    vmem = lambda *shape, dtype=BF: pltpu.VMEM(shape, dtype)
    dma = lambda n: pltpu.SemaphoreType.DMA((n,))
    final_late = pl.BlockSpec((B, SHARE), lambda s: (late(s), 0))
    return pl.pallas_call(
        functools.partial(bwd_kernel, orders=orders, chunk=chunk),
        grid=(last_step(levels) + 1,),
        in_specs=[row(SHARE)] * 4
        + [final_late, own(D), own(D), anywhere, own(D // 2), anywhere]
        + [own(D)]
        + [anywhere] * 2
        + [anywhere] * 3
        + [whole(8, 2 * UNITS), whole(LH, 8, B)]
        + [pl.BlockSpec((LH, B, STRIP), lambda s: (0, block(s), 0))]
        + [row(SHARE)] * 3
        + [whole(SEQ, SHARE)] * 2
        + [whole(8, D)]
        + [whole(D, SHARE)] * 3
        + [whole(SHARE, D)],
        out_specs=[anywhere, anywhere, final_late]
        + [whole(chunk, UNITS), whole(UNITS, chunk)]
        + [whole(chunk, TILE)] * 2
        + [whole(16, SHARE)],
        scratch_shapes=[
            vmem(B, D, dtype=F32),
            vmem(B, D),
            vmem(LH, B, SHARE),
            vmem(LH, HD, B),
            vmem(LH, HD, B),
            vmem(LH, B, 128, dtype=F32),
            vmem(B, STRIP),
            vmem(LH, B, SHARE, dtype=F32),
            vmem(LH, HD, SEQ, dtype=F32),
            vmem(LH, HD, SEQ, dtype=F32),
            vmem(D, 4 * SHARE, dtype=F32),
            vmem(2, 2, B, SHARE),
            vmem(half, B, D),
            vmem(half, B, D // 2),
            vmem(half, B, D),
            vmem(half, B, D // 2),
            vmem(half, B, D // 2),
            vmem(2, B, D // 2),
            vmem(3, B, D // 2),
            vmem(NB, B, D // 2),
            vmem(3, B, SHARE, dtype=F32),
            vmem(NB, B, SHARE),
            vmem(NB, B, SHARE),
            vmem(4, B, SHARE),
            vmem(NB, 8, B, dtype=F32),
            vmem(NB, 8, B, dtype=F32),
            vmem(NB, 8, B, dtype=F32),
            vmem(NB, 8, B, dtype=F32),
            vmem(2, D // 2, TILE),
            vmem(2, D // 2, TILE),
            vmem(6, D // 2, TILE),
            vmem(half, chunk, TILE),
            vmem(half, chunk, TILE),
            vmem(2, chunk, TILE, dtype=F32),
            vmem(8, D, dtype=F32),
            vmem(8, SHARE, dtype=F32),
            vmem(8, SHARE, dtype=F32),
            vmem(8, SHARE, dtype=F32),
            vmem(8, SHARE, dtype=F32),
            vmem(8, SHARE, dtype=F32),
            vmem(levels, 16, SHARE, dtype=F32),
            vmem(levels, 16, SHARE, dtype=F32),
        ]
        + [vmem(slots, D >> (n + 1), TILE) for n in range(1, levels) for slots in (4, 4, 10)]
        + [dma(half)] * 4
        + [dma(NB)] * 2
        + [dma(half)] * 2
        + [dma(NB)] * 8
        + [dma(4)] * 2
        + [dma(half)] * 2
        + [dma(2)] * 2
        + [dma(8)] * 2
        + [dma(1)] * 2
        + [dma(levels)] * 2
        + [dma(half)] * 3
        + [dma(12)] * (2 * (levels - 1)),
        out_shape=[like((SEQ, SHARE), BF), like((OWN, SHARE), BF)]
        + [like((SEQ, SHARE), F32)]
        + [like((chunk, UNITS), F32), like((UNITS, chunk), F32)]
        + [like((chunk, TILE), F32)] * 2
        + [like((16, SHARE), F32)],
        compiler_params=remote_params(2),
        cost_estimate=pl.CostEstimate(
            flops=30 * 10**9, bytes_accessed=50 * 2**20, transcendentals=0
        ),
        name="backward",
    )(
        *xs, xs[0], h1, gn, gn, mk, ms, dy, gu, gd, ru, su, sd, up_sums, hm, p, q, linv, ctx, k, v, vec, wq, wk, wv, wd
    )


def swap(value, axis, bit):
    size = lax.axis_size(axis)
    return lax.ppermute(value, axis, [(i, i ^ bit) for i in range(size)])


def dp_bits():
    bits, bit = [], 1
    while bit < lax.axis_size("dp"):
        bits.append(bit)
        bit *= 2
    return bits


def pick(value, axis, index):
    return lax.dynamic_index_in_dim(value, index, axis, keepdims=False)


def shards(
    tokens,
    out_grad,
    segments,
    padding,
    norm1_gain,
    norm1_bias,
    w_query,
    b_query,
    w_key,
    w_value,
    b_value,
    w_dense,
    dense_bias,
    norm2_gain,
    norm2_bias,
    w_up,
    b_up,
    w_down,
    down_bias,
):
    t = lax.axis_index("tensor")
    rank = lax.axis_index("dp")
    size = lax.axis_size("dp")
    core, y = t % 2, t // 2
    core_swap = lambda value: swap(value, "tensor", 1)
    y_swap = lambda value: swap(value, "tensor", 2)
    rows8 = lambda value: jnp.pad(value, ((0, 8 - value.shape[0]), (0, 0)))

    own_vec = jnp.concatenate(
        [
            jnp.stack([norm1_gain, norm1_bias, dense_bias, norm2_gain, norm2_bias, down_bias, down_bias, down_bias]),
            b_up.reshape(4, SHARE),
            b_up.reshape(4, SHARE),
        ]
    ).astype(F32)

    part = D // size
    cut = lambda w: lax.dynamic_slice_in_dim(w, rank * part, part, 0)
    w_part = y_swap(jnp.concatenate([cut(w_up), cut(w_down)], axis=1))
    seg = segments.reshape(SEQ)
    index = jnp.arange(SEQ, dtype=jnp.int32)
    first = jnp.zeros((SEQ,), jnp.int32)
    for value in range(1, 4):
        first = jnp.where(seg == value, jnp.sum((seg < value).astype(jnp.int32)), first)
    lowest = jnp.maximum(first, index - (WIN - 1))
    pad_row = rows8(jnp.where(padding.reshape(1, SEQ) == 1, 0.0, NEG).astype(F32))
    heads = t * LH + jnp.arange(LH)
    slopes = jnp.exp2(-8.0 * (heads.astype(F32) + 1.0) / HEADS)
    alibi = rows8(slopes[:, None] * (jnp.arange(STRIP) - (STRIP - 1)).astype(F32)[None, :])

    b_qv = rows8(jnp.stack([b_query, b_value]).astype(F32))
    lows = lowest.reshape(SEQ, 1)
    w_part, own_vec, b_qv, lows, pad_row, alibi = lax.optimization_barrier(
        (w_part, own_vec, b_qv, lows, pad_row, alibi)
    )
    w_other = lax.all_gather(w_part, "dp", axis=0, tiled=True)

    p, q, k, v, linv, ctx, a_own, a_par, x1, x2, x3, xm, hm, vec, b_up_pair, dy = attention_forward(
        tokens, out_grad, own_vec, w_query, w_key, w_value,
        b_qv, w_dense, lows, pad_row, alibi,
    )
    xs = [tokens, x1, x2, x3]

    bits = dp_bits()
    order_a = bits if size == 8 else bits[::-1]
    order_b = [2, 4, 1] if size == 8 else [bits[-2], bits[-1], *bits[:-2][::-1]]
    mk, ms, gn, h1, gu, su, gd, sd, up_sums, ru = feed_forward(
        a_own, a_par, xm, dy, vec, b_up_pair, w_up, w_down, w_other, (order_a[0], order_b[0]), part
    )
    output, _, tokens_grad, w_up_grad, w_down_grad, g_qk, g_vd, sums = attention_backward(
        xs, h1, gn, mk, ms, dy, gu, gd, ru, su, sd, up_sums, hm, p, q, linv, ctx, k, v, vec,
        w_query, w_key, w_value, w_dense, (order_a, order_b), part,
    )
    head_max = sums[12, :LH]
    column_scale = jnp.repeat(jnp.sqrt(TAU / jnp.maximum(head_max, TAU)), HD)
    return (
        output,
        tokens_grad,
        sums[8],
        sums[9],
        g_qk[:, :SHARE],
        sums[10],
        g_qk[:, SHARE:],
        g_vd[:, :SHARE],
        sums[11],
        g_vd[:, SHARE:].T,
        sums[2],
        sums[0],
        sums[1],
        w_up_grad,
        sums[4:8].reshape(UNITS),
        w_down_grad,
        sums[3],
        head_max,
        w_query.astype(F32) * column_scale,
        b_query.astype(F32) * column_scale,
        w_key.astype(F32) * column_scale,
    )


def solution(mesh):
    in_specs = (
        P("dp", "tensor"),
        P("dp", "tensor"),
        P("dp", None),
        P("dp", None),
        P("tensor"),
        P("tensor"),
        P(None, "tensor"),
        P("tensor"),
        P(None, "tensor"),
        P(None, "tensor"),
        P("tensor"),
        P("tensor", None),
        P("tensor"),
        P("tensor"),
        P("tensor"),
        P(None, "tensor"),
        P("tensor"),
        P("tensor", None),
        P("tensor"),
    )
    out_specs = (
        P("dp", "tensor"),
        P("dp", "tensor"),
        P("tensor"),
        P("tensor"),
        P("dp", "tensor"),
        P("tensor"),
        P("dp", "tensor"),
        P("dp", "tensor"),
        P("tensor"),
        P("tensor", "dp"),
        P("tensor"),
        P("tensor"),
        P("tensor"),
        P("dp", "tensor"),
        P("tensor"),
        P("tensor", "dp"),
        P("tensor"),
        P("tensor"),
        P(None, "tensor"),
        P("tensor"),
        P(None, "tensor"),
    )
    return jax.shard_map(shards, mesh=mesh, in_specs=in_specs, out_specs=out_specs, check_vma=False)
```
